256 devices in a mesh: lon: 32 (over y_hi, z, core), lat: 8 (over y_lo, x).
Axes of the slice: x: 4, y: 4 (y_hi: 2, y_lo: 2; y = y_hi * 2 + y_lo), z: 8, core: 2. Of those that a mesh axis runs over, the one named last changes fastest.
Arguments:
- layer_u: float32 [12, 512, 4096], P(None, 'lat', 'lon'), may hold values from -3 to 3
- layer_v: float32 [12, 512, 4096], P(None, 'lat', 'lon'), may hold values from -3 to 3
- thickness: float32 [12, 512, 4096], P(None, 'lat', 'lon'), may hold values from 0.02 to 0.16
- surface_height: float32 [512, 4096], P('lat', 'lon'), may hold values from -2 to 2
- barotropic_u: float32 [512, 4096], P('lat', 'lon'), may hold values from -2 to 2
- barotropic_v: float32 [512, 4096], P('lat', 'lon'), may hold values from -2 to 2
- land_mask: int32 [512, 4096], P('lat', 'lon'), may hold values 0 or 1
- bottom_level: int32 [512, 4096], P('lat', 'lon'), may hold values from 1 to 12
- fold_map: int32 [4096], P('lon'), may hold values from 0 to 4095, as said below
- reduced_gravity: float32 [12], replicated, may hold values from 0.05 to 0.5
Outputs:
- new_u: float32 [12, 512, 4096], P(None, 'lat', 'lon')
- new_v: float32 [12, 512, 4096], P(None, 'lat', 'lon')
- new_thickness: float32 [12, 512, 4096], P(None, 'lat', 'lon')
- new_surface: float32 [512, 4096], P('lat', 'lon')
- mean_u: float32 [512, 4096], P('lat', 'lon')
- mean_v: float32 [512, 4096], P('lat', 'lon')
The draws below stay inside these ranges and needn't reach their ends.
Inputs may be any that keep to these rules, and one draw needn't show every extreme that they name: fold_map[i] = (p - i) mod 4096 for one p, so the map is its own inverse.
All inputs are finite; a program needn't handle non-finite values. No bound on the sum of `land_mask` on one device may be relied on, other than what follows from the above.
Results may differ from the reference program's by a relative error of at most 0.00002.
Values sent between devices are 32-bit elements; how exact they have to be, the bound alone decides.
No kernel may reach another device: no remote copies, remote signals or barrier semaphores. Data moves between devices by JAX's collectives and lax.ppermute only.
A program may use at most 64 MiB of HBM per device.

```python
import math
import jax
import jax.numpy as jnp

LAYERS = 12
SUBSTEPS = 8
NLAT = 512
NLON = 4096


def draw_fold_map(key, part):
    key = jax.random.fold_in(key, 7)
    pivot = jax.random.randint(key, (), 0, NLON, dtype=jnp.int32)
    return jnp.mod(pivot - jnp.arange(NLON, dtype=jnp.int32), NLON).astype(jnp.int32)


def touch_ends(values, rng, low, high):
    shape = values.shape
    index_at = [jax.random.randint(jax.random.fold_in(rng, axis), (), 0, shape[axis]) for axis in range(len(shape))]
    values = values.at[tuple(index_at)].set(low)
    longest = shape.index(max(shape))
    index_at[longest] = (index_at[longest] + 1) % shape[longest]
    return values.at[tuple(index_at)].set(high)


def block_levels(own_key, dims, split, least, largest):
    factor_of, own = 1.0, jax.random.fold_in(own_key, 6)
    for position, blocks in split:
        heights = jnp.exp(jax.random.uniform(jax.random.fold_in(own, position), (blocks,), jnp.float32, least / len(split), largest / len(split)))
        factor_of = factor_of * jnp.repeat(heights, dims[position] // blocks).reshape([-1 if axis == position else 1 for axis in range(len(dims))])
    return factor_of


def normal_values(key, dims, scale, bound, split=(), held_as=jnp.bfloat16):
    level = block_levels(key, dims, split, -0.22, 0.18) if split else 1.0
    entries = jax.random.normal(key, dims, jnp.float32) * scale * level
    return jnp.minimum(jnp.maximum(entries, -bound), bound).astype(held_as)


def setup_inputs(seed: int = 0) -> dict:
    seeds = jax.random.split(jax.random.key(seed), 11)
    layer_u = normal_values(seeds[0], (LAYERS, NLAT, NLON), 0.5, 3.0, ((1, 8), (2, 32)), jnp.float32)
    layer_v = normal_values(seeds[1], (LAYERS, NLAT, NLON), 0.5, 3.0, ((1, 8), (2, 32)), jnp.float32)
    thickness = jnp.clip(jnp.exp(math.log(0.16) - 2.0794415 * jax.random.uniform(seeds[2], (LAYERS, NLAT, NLON), jnp.float32) ** block_levels(seeds[2], (LAYERS, NLAT, NLON), ((1, 8), (2, 32)), -0.2, 0.2)), 0.02, 0.16)
    surface_height = normal_values(seeds[3], (NLAT, NLON), 0.3, 2.0, ((0, 8), (1, 32)), jnp.float32)
    barotropic_u = normal_values(seeds[4], (NLAT, NLON), 0.3, 2.0, ((0, 8), (1, 32)), jnp.float32)
    barotropic_v = normal_values(seeds[5], (NLAT, NLON), 0.3, 2.0, ((0, 8), (1, 32)), jnp.float32)
    land_mask = touch_ends((jax.random.randint(seeds[6], (NLAT, NLON), 0, 4) < 3).astype(jnp.int32), jax.random.fold_in(seeds[6], 1), 0, 1)
    bottom_level = touch_ends(jax.random.randint(seeds[7], (NLAT, NLON), 1, LAYERS + 1), jax.random.fold_in(seeds[7], 1), 1, LAYERS).astype(jnp.int32)
    fold_map = draw_fold_map(jax.random.fold_in(seeds[10], 71), 0)
    reduced_gravity = jnp.clip(jnp.exp(jax.random.uniform(seeds[9], (LAYERS,), jnp.float32, math.log(0.05), math.log(0.5))), 0.05, 0.5)
    return dict(layer_u=layer_u, layer_v=layer_v, thickness=thickness, surface_height=surface_height, barotropic_u=barotropic_u, barotropic_v=barotropic_v, land_mask=land_mask, bottom_level=bottom_level, fold_map=fold_map, reduced_gravity=reduced_gravity)


barotropic_step = 0.45
baroclinic_step = 0.1
coriolis_scale = 0.3
bottom_drag = 0.05


def extend(values, margin, parity, fold_map):
    height = values.shape[-2]
    upper = parity * jnp.flip(values[..., height - margin:, :], axis=-2)
    upper = jnp.take(upper, fold_map, axis=-1)
    lower = jnp.zeros_like(values[..., :margin, :])
    stacked = jnp.concatenate([lower, values, upper], axis=-2)
    return jnp.concatenate([stacked[..., -margin:], stacked, stacked[..., :margin]], axis=-1)


def east_west(extended):
    return 0.5 * (extended[..., 1:-1, 2:] - extended[..., 1:-1, :-2])


def north_south(extended):
    return 0.5 * (extended[..., 2:, 1:-1] - extended[..., :-2, 1:-1])


def reference(layer_u, layer_v, thickness, surface_height, barotropic_u, barotropic_v, land_mask, bottom_level, fold_map, reduced_gravity):
    layers = thickness.shape[0]
    wet = land_mask.astype(jnp.float32)
    levels = jnp.arange(layers, dtype=jnp.int32)[:, None, None]
    weights = jnp.where(levels < bottom_level[None], wet[None], 0.0)
    weighted = weights * thickness
    depth = jnp.sum(weighted, axis=0)
    safe_depth = depth + (1.0 - wet)
    interfaces = jnp.cumsum(weighted, axis=0)
    potential = jnp.cumsum(reduced_gravity[:, None, None] * interfaces, axis=0)
    potential_ext = extend(potential, 1, 1.0, fold_map)
    latitude = jnp.pi * (jnp.arange(NLAT, dtype=jnp.float32) + 0.5) / NLAT
    coriolis = (-coriolis_scale * jnp.cos(latitude))[:, None]
    tend_u = weights * (-east_west(potential_ext) + coriolis * layer_v)
    tend_v = weights * (-north_south(potential_ext) - coriolis * layer_u)
    force_u = jnp.sum(weighted * tend_u, axis=0) / safe_depth
    force_v = jnp.sum(weighted * tend_v, axis=0) / safe_depth
    column_u = jnp.sum(weighted * layer_u, axis=0) / safe_depth
    column_v = jnp.sum(weighted * layer_v, axis=0) / safe_depth
    level = surface_height
    speed_u = barotropic_u
    speed_v = barotropic_v
    total_u = jnp.zeros_like(speed_u)
    total_v = jnp.zeros_like(speed_v)
    for sweep in range(SUBSTEPS):
        transport = jnp.stack([depth * speed_u, depth * speed_v])
        trans_ext = extend(transport, 1, -1.0, fold_map)
        level = level - barotropic_step * (east_west(trans_ext[0]) + north_south(trans_ext[1]))
        level_ext = extend(level, 1, 1.0, fold_map)
        next_u = wet * (speed_u + barotropic_step * (-east_west(level_ext) + coriolis * speed_v + force_u - bottom_drag * speed_u))
        next_v = wet * (speed_v + barotropic_step * (-north_south(level_ext) - coriolis * speed_u + force_v - bottom_drag * speed_v))
        speed_u, speed_v = next_u, next_v
        total_u = total_u + speed_u
        total_v = total_v + speed_v
    mean_u = total_u / SUBSTEPS
    mean_v = total_v / SUBSTEPS
    new_u = weights * (layer_u - column_u + baroclinic_step * (tend_u - force_u) + mean_u)
    new_v = weights * (layer_v - column_v + baroclinic_step * (tend_v - force_v) + mean_v)
    fluxes = jnp.concatenate([weighted * new_u, weighted * new_v], axis=0)
    flux_ext = extend(fluxes, 1, -1.0, fold_map)
    new_thickness = thickness - baroclinic_step * (east_west(flux_ext[:layers]) + north_south(flux_ext[layers:]))
    return new_u, new_v, new_thickness, level, mean_u, mean_v
```

```python
import functools

import jax
import jax.numpy as jnp
from jax import lax
from jax.experimental import pallas as pl
from jax.experimental.pallas import tpu as pltpu
from jax.sharding import PartitionSpec as P

SUBSTEPS = 8
LAYERS = 12
TOTAL_ROWS = 512
ROWS, COLS = 64, 128
HALO = 16

barotropic_step = 0.45
baroclinic_step = 0.1
coriolis_scale = 0.3
bottom_drag = 0.05

W_LANE = 96
C_LANE = 108
T_LANE = 120
TOP_ROW = 64
W_TOP, C_TOP, W_BOTTOM, C_BOTTOM = 160, 172, 184, 196
V_TOP, V_BOTTOM = 208, 209
LON_ROWS = 216
LAT_W, LAT_C, LAT_V, LAT_ROWS = 96, 108, 120, 128


def lane_index(shape):
    return lax.broadcasted_iota(jnp.int32, shape, 1)


def row_index(shape):
    return lax.broadcasted_iota(jnp.int32, shape, 0)


def roll(x, shift, axis):
    shift = shift % x.shape[axis]
    return x if shift == 0 else pltpu.roll(x, shift, axis)


def first_kernel(gravity, lu, lv, th, lev, u, v, land, bottom, msg_a, msg_b, flat, cor_out, pack_e, pack_w):
    lon, lat = lax.axis_index("lon"), lax.axis_index("lat")
    even = lax.rem(lon, 2) == 0
    rows = (row_index((ROWS + 2 * HALO, COLS)) + (lat * ROWS - HALO)).astype(jnp.float32)
    cor_all = -coriolis_scale * jnp.cos((rows + 0.5) * (jnp.pi / TOTAL_ROWS))
    cor_out[...] = cor_all
    cor = cor_all[HALO : HALO + ROWS]
    lane = lane_index((ROWS, COLS))
    row = row_index((ROWS, COLS))
    wet = land[...].astype(jnp.float32)
    bot = bottom[...]
    zero = jnp.zeros((ROWS, COLS), jnp.float32)

    depth, potential = zero, zero
    grad_u, grad_v, sum_u, sum_v = zero, zero, zero, zero
    tails_u = []
    for k in range(LAYERS):
        w = jnp.where(bot > k, wet, 0.0) * th[k]
        depth = depth + w
        potential = potential + gravity[k] * depth
        right = jnp.where(lane == COLS - 1, 0.0, roll(potential, -1, 1))
        left = jnp.where(lane == 0, 0.0, roll(potential, 1, 1))
        above = jnp.where(row == ROWS - 1, 0.0, roll(potential, -1, 0))
        below = jnp.where(row == 0, 0.0, roll(potential, 1, 0))
        du = 0.5 * (left - right)
        dv = 0.5 * (below - above)
        grad_u = grad_u + w * du
        grad_v = grad_v + w * dv
        sum_u = sum_u + w * lu[k]
        sum_v = sum_v + w * lv[k]
        tail_u = lu[k] + baroclinic_step * (du + cor * lv[k])
        tail_v = lv[k] + baroclinic_step * (dv - cor * lu[k])
        lane_w, lane_c = W_LANE + k, C_LANE + k
        is_w, is_c = lane == lane_w, lane == lane_c
        for pack, edge in ((pack_w, 0), (pack_e, COLS - 1)):
            held = zero if k == 0 else pack[...]
            held = jnp.where(is_w, roll(w, lane_w - edge, 1), held)
            pack[...] = jnp.where(is_c, roll(tail_u, lane_c - edge, 1), held)
        for msg in (msg_a, msg_b):
            msg[W_TOP + k : W_TOP + k + 1, :] = w[ROWS - 1 :]
            msg[W_BOTTOM + k : W_BOTTOM + k + 1, :] = w[:1]
            msg[C_TOP + k : C_TOP + k + 1, :] = tail_v[ROWS - 1 :]
            msg[C_BOTTOM + k : C_BOTTOM + k + 1, :] = tail_v[:1]
    inverse = 1.0 / (depth + (1.0 - wet))
    column_u = sum_u * inverse
    column_v = sum_v * inverse
    force_u = grad_u * inverse + cor * column_v
    force_v = grad_v * inverse - cor * column_u
    fields = (depth, u[...], v[...], lev[...], force_u, force_v)
    flat[0] = depth
    flat[1] = force_u
    flat[2] = force_v
    flat[3] = column_u
    flat[4] = column_v
    transport_u = depth * u[...]
    transport_v = depth * v[...]
    strips = []
    for pack, edge, first, line in ((pack_w, 0, 0, HALO), (pack_e, COLS - 1, COLS - HALO, COLS - 1 - HALO)):
        column = jnp.sum(jnp.where(lane == edge, column_u, 0.0), axis=1, keepdims=True)
        strip = pack[...]
        strip = jnp.where((lane >= C_LANE) & (lane < C_LANE + LAYERS), strip - column, strip)
        for f, field in enumerate(fields):
            strip = jnp.where(lane // HALO == f, roll(field, HALO * f - first, 1), strip)
        strip = jnp.where(lane == T_LANE, roll(transport_u, T_LANE - line, 1), strip)
        strips.append(strip)
    west, east = strips
    msg_a[:ROWS] = jnp.where(even, east, west)
    msg_b[:ROWS] = jnp.where(even, west, east)
    for msg in (msg_a, msg_b):
        for f, field in enumerate(fields):
            msg[TOP_ROW + HALO * f : TOP_ROW + HALO * (f + 1)] = field[ROWS - HALO :]
        msg[C_TOP : C_TOP + LAYERS] = msg[C_TOP : C_TOP + LAYERS] - column_v[ROWS - 1 :]
        msg[C_BOTTOM : C_BOTTOM + LAYERS] = msg[C_BOTTOM : C_BOTTOM + LAYERS] - column_v[:1]
        msg[V_TOP : V_TOP + 1] = transport_v[ROWS - 1 - HALO : ROWS - HALO]
        msg[V_BOTTOM : V_BOTTOM + 1] = transport_v[HALO : HALO + 1]
        msg[V_BOTTOM + 1 :] = jnp.zeros((LON_ROWS - V_BOTTOM - 1, COLS), jnp.float32)


def lane_prefix(x):
    for shift in (1, 2, 4, 8):
        x = x + pltpu.roll(x, shift, 1)
    return x


def second_kernel(gravity, fold, lev, u, v, flat, own_a, own_b, got_a, got_b, ext, msg_x, msg_y, msg_f):
    lon, lat = lax.axis_index("lon"), lax.axis_index("lat")
    even_lon = lax.rem(lon, 2) == 0
    even_lat = lax.rem(lat, 2) == 0
    lane = lane_index((ROWS, COLS))
    is_layer = (lane >= W_LANE) & (lane < W_LANE + LAYERS)
    line = lane_index((1, COLS))
    weights_g = jnp.zeros((1, COLS), jnp.float32)
    for k in range(LAYERS):
        weights_g = jnp.where(line == W_LANE + k, gravity[k], weights_g)

    own_e = jnp.where(even_lon, own_a[:ROWS], own_b[:ROWS])
    own_w = jnp.where(even_lon, own_b[:ROWS], own_a[:ROWS])
    east = jnp.where(even_lon, got_a[:ROWS], got_b[:ROWS])
    west = jnp.where(even_lon, got_b[:ROWS], got_a[:ROWS])

    def layer_lanes(x):
        w = jnp.where(is_layer, x, 0.0)
        return w, lane_prefix(weights_g * lane_prefix(w))

    def dot(a, b):
        return jnp.sum(a * b, axis=1, keepdims=True)

    w_e, p_e = layer_lanes(own_e)
    w_w, p_w = layer_lanes(own_w)
    w_east, p_east = layer_lanes(east)
    w_west, p_west = layer_lanes(west)

    depth = flat[0]
    safe = depth + jnp.where(depth > 0.0, 0.0, 1.0)
    fix = jnp.where(lane == COLS - 1, -0.5 * dot(w_e, p_east), jnp.where(lane == 0, 0.5 * dot(w_w, p_west), 0.0))
    force_u = flat[1] + fix / safe

    sides = []
    for f in range(6):
        side = jnp.where(lane < HALO, roll(east, -HALO * f, 1), 0.0)
        side = jnp.where(lane >= COLS - HALO, roll(west, COLS - HALO - HALO * f, 1), side)
        sides.append(side)
    sides[1] = jnp.where(lane == HALO, roll(east, HALO - T_LANE, 1), sides[1])
    sides[1] = jnp.where(lane == COLS - HALO - 1, roll(west, COLS - HALO - 1 - T_LANE, 1), sides[1])
    safe = sides[0] + jnp.where(sides[0] > 0.0, 0.0, 1.0)
    fix = jnp.where(lane == 0, 0.5 * dot(w_east, p_e), jnp.where(lane == COLS - 1, -0.5 * dot(w_west, p_w), 0.0))
    sides[4] = sides[4] + fix / safe
    sides[0] = jnp.where((lane == HALO) | (lane == COLS - HALO - 1), 1.0, sides[0])

    for f, field in enumerate((depth, u[...], v[...], lev[...], force_u, flat[2])):
        ext[f, :, :COLS] = field
        ext[f, :, COLS:] = sides[f]

    lane12 = lane_index((LAYERS, COLS))

    def lat_message(msg, north):
        start, w_at, c_at, v_at = (ROWS - HALO, W_TOP, C_TOP, V_TOP) if north else (0, W_BOTTOM, C_BOTTOM, V_BOTTOM)
        for f in range(6):
            msg[HALO * f : HALO * (f + 1), :] = ext[f, start : start + HALO, :]
        msg[LAT_W : LAT_W + LAYERS, :COLS] = own_a[w_at : w_at + LAYERS, :]
        beside_e = jnp.where(even_lon, got_a[w_at : w_at + LAYERS, :], got_b[w_at : w_at + LAYERS, :])
        beside_w = jnp.where(even_lon, got_b[w_at : w_at + LAYERS, :], got_a[w_at : w_at + LAYERS, :])
        beside = jnp.where(lane12 < HALO, beside_e, jnp.where(lane12 >= COLS - HALO, beside_w, 0.0))
        msg[LAT_W : LAT_W + LAYERS, COLS:] = beside
        msg[LAT_C : LAT_C + LAYERS, :COLS] = own_a[c_at : c_at + LAYERS, :]
        msg[LAT_C : LAT_C + LAYERS, COLS:] = jnp.zeros((LAYERS, COLS), jnp.float32)
        msg[LAT_V : LAT_V + 1, :COLS] = own_a[v_at : v_at + 1, :]
        msg[LAT_V : LAT_V + 1, COLS:] = jnp.zeros((1, COLS), jnp.float32)
        msg[LAT_V + 1 :, :] = jnp.zeros((LAT_ROWS - LAT_V - 1, 2 * COLS), jnp.float32)

    @pl.when(even_lat)
    def _():
        lat_message(msg_x, True)
        lat_message(msg_y, False)

    @pl.when(jnp.logical_not(even_lat))
    def _():
        lat_message(msg_x, False)
        lat_message(msg_y, True)

    @pl.when(lat == lax.axis_size("lat") - 1)
    def _():
        offset = 64 + ((fold[0] + 64) & (COLS - 1))
        lane8 = lane_index((8, COLS))
        row8 = row_index((8, COLS))
        source = (offset - lane8) & (COLS - 1)
        block = (COLS + offset - lane8) >> 7
        side_block = jnp.where(lane8 < HALO, offset - lane8, 2 * COLS + offset - lane8) >> 7

        def gather(x, index, axis):
            return jnp.take_along_axis(x, index, axis=axis, mode="promise_in_bounds")

        def window(w_tile, o_tile, e_tile):
            a, b, c = gather(w_tile, source, 1), gather(o_tile, source, 1), gather(e_tile, source, 1)
            main = jnp.where(block == 0, a, jnp.where(block == 1, b, c))
            side = jnp.where(side_block == 0, a, jnp.where(side_block == 1, b, c))
            return main, side

        for f in range(6):
            sign = 1.0 if f in (0, 3) else -1.0
            for t in range(2):
                at = ROWS - 8 * (t + 1)
                mine = ext[f, at : at + 8, :COLS]
                side = ext[f, at : at + 8, COLS:]
                here = TOP_ROW + HALO * f + HALO - 8 * (t + 1)
                on_e = jnp.where(even_lon, got_a[here : here + 8, :], got_b[here : here + 8, :])
                on_w = jnp.where(even_lon, got_b[here : here + 8, :], got_a[here : here + 8, :])
                on_e = jnp.where(lane8 < HALO, side, on_e)
                on_w = jnp.where(lane8 >= COLS - HALO, side, on_w)
                main, beside = window(on_w, mine, on_e)
                to = HALO * f + 8 * t
                msg_f[to : to + 8, :COLS] = sign * gather(main, 7 - row8, 0)
                msg_f[to : to + 8, COLS:] = sign * gather(beside, 7 - row8, 0)
        at = W_TOP
        for t in range(3):
            mine = own_a[at + 8 * t : at + 8 * (t + 1), :]
            on_e = jnp.where(even_lon, got_a[at + 8 * t : at + 8 * (t + 1), :], got_b[at + 8 * t : at + 8 * (t + 1), :])
            on_w = jnp.where(even_lon, got_b[at + 8 * t : at + 8 * (t + 1), :], got_a[at + 8 * t : at + 8 * (t + 1), :])
            main, beside = window(on_w, mine, on_e)
            sign = jnp.where(row8 + 8 * t < LAYERS, 1.0, -1.0)
            msg_f[LAT_W + 8 * t : LAT_W + 8 * (t + 1), :COLS] = sign * main
            msg_f[LAT_W + 8 * t : LAT_W + 8 * (t + 1), COLS:] = sign * beside
        mine = own_a[V_TOP : V_TOP + 8, :]
        on_e = jnp.where(even_lon, got_a[V_TOP : V_TOP + 8, :], got_b[V_TOP : V_TOP + 8, :])
        on_w = jnp.where(even_lon, got_b[V_TOP : V_TOP + 8, :], got_a[V_TOP : V_TOP + 8, :])
        main, _ = window(on_w, mine, on_e)
        msg_f[LAT_V:, :COLS] = -main
        msg_f[LAT_V:, COLS:] = jnp.zeros((8, COLS), jnp.float32)

    @pl.when(lat != lax.axis_size("lat") - 1)
    def _():
        msg_f[...] = jnp.zeros((LAT_ROWS, 2 * COLS), jnp.float32)


def third_kernel(
    gravity, lu, lv, th, land, bottom, flat, cor_ref, own_a, got_a, got_b, ext, own_x, own_y, got_x, got_y, got_f,
    new_u, new_v, new_th, new_lev, mean_u_out, mean_v_out,
    north, south, line_u, line_v, level_pad, v_pad,
):
    lon, lat = lax.axis_index("lon"), lax.axis_index("lat")
    even_lon = lax.rem(lon, 2) == 0
    even_lat = lax.rem(lat, 2) == 0
    at_top = lat == lax.axis_size("lat") - 1
    at_bottom = lat == 0
    full = ROWS + 2 * HALO
    wide = 2 * COLS
    north[...] = jnp.where(at_top, got_f[...], jnp.where(even_lat, got_x[...], got_y[...]))
    south[...] = jnp.where(at_bottom, 0.0, jnp.where(even_lat, got_y[...], got_x[...]))

    def whole(f):
        at = HALO * f
        return jnp.concatenate([south[at : at + HALO, :], ext[f], north[at : at + HALO, :]], axis=0)

    depth, u, v, level, force_u, force_v = (whole(f) for f in range(6))
    wet = jnp.where(depth > 0.0, 1.0, 0.0)
    cor = jnp.concatenate([cor_ref[...], cor_ref[...]], axis=1)

    def seam(below_w, above_w):
        sum_b, sum_a, pot_b, pot_a, to_b, to_a = (jnp.zeros((1, wide), jnp.float32) for _ in range(6))
        pots = []
        for k in range(LAYERS):
            wb, wa = below_w(k), above_w(k)
            sum_b, sum_a = sum_b + wb, sum_a + wa
            pot_b, pot_a = pot_b + gravity[k] * sum_b, pot_a + gravity[k] * sum_a
            to_b = to_b + wb * pot_a
            to_a = to_a + wa * pot_b
            pots.append((pot_b[:, :COLS], pot_a[:, :COLS]))
        safe_b = sum_b + jnp.where(sum_b > 0.0, 0.0, 1.0)
        safe_a = sum_a + jnp.where(sum_a > 0.0, 0.0, 1.0)
        return -0.5 * to_b / safe_b, 0.5 * to_a / safe_a, pots

    def own_edge(top):
        def get(k):
            at = LAT_W + k
            x, y = own_x[at : at + 1, :], own_y[at : at + 1, :]
            return jnp.where(even_lat, x, y) if top else jnp.where(even_lat, y, x)
        return get

    row = row_index((full, wide))
    fix_b, fix_a, pots_n = seam(own_edge(True), lambda k: north[LAT_W + k : LAT_W + k + 1, :])
    force_v = force_v + jnp.where(row == HALO + ROWS - 1, fix_b, jnp.where(row == HALO + ROWS, fix_a, 0.0))
    fix_b, fix_a, pots_s = seam(lambda k: south[LAT_W + k : LAT_W + k + 1, :], own_edge(False))
    force_v = force_v + jnp.where(row == HALO - 1, fix_b, jnp.where(row == HALO, fix_a, 0.0))

    keep = wet * (1.0 - barotropic_step * bottom_drag)
    turn = wet * (barotropic_step * cor)
    push_u = wet * (barotropic_step * force_u)
    push_v = wet * (barotropic_step * force_v)
    slope = wet * (0.5 * barotropic_step)
    rate = jnp.where(at_bottom & (row < HALO), 0.0, 0.5 * barotropic_step)

    v_pad[7:8, :] = south[LAT_V : LAT_V + 1, :]
    v_pad[8 + full : 9 + full, :] = north[LAT_V : LAT_V + 1, :]
    total_u = jnp.zeros((full, wide), jnp.float32)
    total_v = jnp.zeros((full, wide), jnp.float32)
    for _ in range(SUBSTEPS):
        trans_u = depth * u
        v_pad[8 : 8 + full, :] = depth * v
        dv = v_pad[9 : 9 + full, :] - v_pad[7 : 7 + full, :]
        du = pltpu.roll(trans_u, wide - 1, 1) - pltpu.roll(trans_u, 1, 1)
        level = level - rate * (du + dv)
        level_pad[8 : 8 + full, :] = level
        dy = level_pad[9 : 9 + full, :] - level_pad[7 : 7 + full, :]
        dx = pltpu.roll(level, wide - 1, 1) - pltpu.roll(level, 1, 1)
        u, v = (
            keep * u + turn * v + push_u - slope * dx,
            keep * v - turn * u + push_v - slope * dy,
        )
        total_u = total_u + u
        total_v = total_v + v
    mean_u = total_u * (1.0 / SUBSTEPS)
    mean_v = total_v * (1.0 / SUBSTEPS)
    inner = slice(HALO, HALO + ROWS)
    new_lev[...] = level[inner, :COLS]
    mean_u_out[...] = mean_u[inner, :COLS]
    mean_v_out[...] = mean_v[inner, :COLS]

    rest_u = mean_u - baroclinic_step * force_u
    rest_v = mean_v - baroclinic_step * force_v
    lane = lane_index((ROWS, COLS))
    row = row_index((ROWS, COLS))
    is_e, is_w = lane == COLS - 1, lane == 0
    is_n, is_s = row == ROWS - 1, row == 0
    side_u = rest_u[inner, COLS:]
    halo_rest = jnp.where(is_e, pltpu.roll(side_u, COLS - 1, 1), pltpu.roll(side_u, 1, 1))
    rest_n = rest_v[HALO + ROWS : HALO + ROWS + 1, :COLS]
    rest_s = rest_v[HALO - 1 : HALO, :COLS]
    base_u = rest_u[inner, :COLS] - flat[3]
    base_v = rest_v[inner, :COLS] - flat[4]
    east = jnp.where(even_lon, got_a[:ROWS], got_b[:ROWS])
    west = jnp.where(even_lon, got_b[:ROWS], got_a[:ROWS])
    half = 0.5 * baroclinic_step
    signed = jnp.where(is_e, half, -half)
    cor = cor_ref[HALO : HALO + ROWS, :]
    land_f = land[...].astype(jnp.float32)
    bot = bottom[...]
    zero = jnp.zeros((ROWS, COLS), jnp.float32)
    thick, potential, halo_thick, halo_potential = zero, zero, zero, zero

    def edged(x, halo, axis):
        if axis == 1:
            return jnp.where(is_e, halo, pltpu.roll(x, COLS - 1, 1)) - jnp.where(is_w, halo, pltpu.roll(x, 1, 1))
        above, below = halo
        return jnp.where(is_n, above, pltpu.roll(x, ROWS - 1, 0)) - jnp.where(is_s, below, pltpu.roll(x, 1, 0))

    for k in range(LAYERS):
        mask = jnp.where(bot > k, land_f, 0.0)
        th_k, lu_k, lv_k = th[k], lu[k], lv[k]
        w = mask * th_k
        thick = thick + w
        potential = potential + gravity[k] * thick
        halo_w = jnp.where(is_e, roll(east, COLS - 1 - W_LANE - k, 1), roll(west, -W_LANE - k, 1))
        halo_c = jnp.where(is_e, roll(east, COLS - 1 - C_LANE - k, 1), roll(west, -C_LANE - k, 1))
        halo_thick = halo_thick + halo_w
        halo_potential = halo_potential + gravity[k] * halo_thick
        pot_top, pot_north = pots_n[k]
        pot_south, pot_low = pots_s[k]
        du = edged(potential, halo_potential, 1)
        dv = edged(potential, (pot_north, pot_south), 0)
        out_u = mask * (lu_k + baroclinic_step * (cor * lv_k - 0.5 * du) + base_u)
        out_v = mask * (lv_k - baroclinic_step * (cor * lu_k + 0.5 * dv) + base_v)
        new_u[k] = out_u
        new_v[k] = out_v
        halo_flux = halo_w * (halo_c + signed * potential + halo_rest)
        flux_n = north[LAT_W + k : LAT_W + k + 1, :COLS] * (
            north[LAT_C + k : LAT_C + k + 1, :COLS] + half * pot_top + rest_n
        )
        flux_s = south[LAT_W + k : LAT_W + k + 1, :COLS] * (
            south[LAT_C + k : LAT_C + k + 1, :COLS] - half * pot_low + rest_s
        )
        divergence = edged(w * out_u, halo_flux, 1) + edged(w * out_v, (flux_n, flux_s), 0)
        new_th[k] = th_k - half * divergence


def vmem(count):
    return [pl.BlockSpec(memory_space=pltpu.VMEM)] * count


def smem(count):
    return [pl.BlockSpec(memory_space=pltpu.SMEM)] * count


def f32(*shape):
    return jax.ShapeDtypeStruct(shape, jnp.float32)


PARAMS = pltpu.CompilerParams(vmem_limit_bytes=40 * 2**20)


def local(lu, lv, th, lev, u, v, land, bottom, fold_map, gravity):
    lons, lats = lax.axis_size("lon"), lax.axis_size("lat")
    lon_msg = f32(LON_ROWS, COLS)
    full = ROWS + 2 * HALO
    msg_a, msg_b, flat, cor = pl.pallas_call(
        first_kernel,
        out_shape=(lon_msg, lon_msg, f32(5, ROWS, COLS), f32(full, COLS)),
        in_specs=smem(1) + vmem(8),
        out_specs=vmem(4),
        scratch_shapes=[pltpu.VMEM((ROWS, COLS), jnp.float32)] * 2,
        compiler_params=PARAMS,
        name="edges",
    )(gravity, lu, lv, th, lev, u, v, land, bottom)

    got_a = lax.ppermute(msg_a, "lon", [(i, i ^ 1) for i in range(lons)])
    got_b = lax.ppermute(msg_b, "lon", [(i, ((i + 1) ^ 1) - 1 & (lons - 1)) for i in range(lons)])

    lat_msg = f32(LAT_ROWS, 2 * COLS)
    ext, msg_x, msg_y, msg_f = pl.pallas_call(
        second_kernel,
        out_shape=(f32(6, ROWS, 2 * COLS), lat_msg, lat_msg, lat_msg),
        in_specs=smem(2) + vmem(8),
        out_specs=vmem(4),
        compiler_params=PARAMS,
        name="extend",
    )(gravity, fold_map, lev, u, v, flat, msg_a, msg_b, got_a, got_b)

    got_x = lax.ppermute(msg_x, "lat", [(i, i ^ 1) for i in range(lats)])
    got_y = lax.ppermute(msg_y, "lat", [(i, ((i + 1) ^ 1) - 1) for i in range(1, lats - 1)])
    total = lons * COLS
    pivot = fold_map[0] + lax.axis_index("lon") * COLS
    shift = jnp.mod(pivot - COLS // 2, total) // COLS
    top = lats - 1

    def mirrored(q):
        pairs = [(((q - b) % lons) * lats + top, b * lats + top) for b in range(lons)]
        return lambda x: lax.ppermute(x, ("lon", "lat"), pairs)

    got_f = lax.switch(shift, [mirrored(q) for q in range(lons)], msg_f)

    layers = f32(LAYERS, ROWS, COLS)
    plane = f32(ROWS, COLS)
    return pl.pallas_call(
        third_kernel,
        out_shape=(layers, layers, layers, plane, plane, plane),
        in_specs=smem(1) + vmem(16),
        out_specs=vmem(6),
        scratch_shapes=[
            pltpu.VMEM((LAT_ROWS, 2 * COLS), jnp.float32),
            pltpu.VMEM((LAT_ROWS, 2 * COLS), jnp.float32),
            pltpu.VMEM((8, COLS), jnp.float32),
            pltpu.VMEM((8, COLS), jnp.float32),
            pltpu.VMEM((full + 16, 2 * COLS), jnp.float32),
            pltpu.VMEM((full + 16, 2 * COLS), jnp.float32),
        ],
        compiler_params=PARAMS,
        name="advance",
    )(gravity, lu, lv, th, land, bottom, flat, cor, msg_a, got_a, got_b, ext, msg_x, msg_y, got_x, got_y, got_f)


def solution(mesh):
    layered, plane = P(None, "lat", "lon"), P("lat", "lon")
    return jax.shard_map(
        local,
        mesh=mesh,
        in_specs=(layered,) * 3 + (plane,) * 5 + (P("lon"), P()),
        out_specs=(layered,) * 3 + (plane,) * 3,
        check_vma=False,
    )
```

```python
import functools

import jax
import jax.numpy as jnp
from jax import lax
from jax.experimental import pallas as pl
from jax.experimental.pallas import tpu as pltpu
from jax.sharding import PartitionSpec as P

SUBSTEPS = 8
LAYERS = 12
TOTAL_ROWS = 512
ROWS, COLS = 64, 128
HALO = 16

barotropic_step = 0.45
baroclinic_step = 0.1
coriolis_scale = 0.3
bottom_drag = 0.05

W_LANE = 96
C_LANE = 108
T_LANE = 120
TOP_ROW = 64
W_TOP, C_TOP, W_BOTTOM, C_BOTTOM = 160, 172, 184, 196
V_TOP, V_BOTTOM = 208, 209
LON_ROWS = 216
LAT_W, LAT_C, LAT_V, LAT_ROWS = 96, 108, 120, 128


def lane_index(shape):
    return lax.broadcasted_iota(jnp.int32, shape, 1)


def row_index(shape):
    return lax.broadcasted_iota(jnp.int32, shape, 0)


def roll(x, shift, axis):
    shift = shift % x.shape[axis]
    return x if shift == 0 else pltpu.roll(x, shift, axis)


def first_kernel(
    gravity_hbm, lu_hbm, lv_hbm, th_hbm, lev_hbm, u_hbm, v_hbm, land_hbm, bottom_hbm, fold_hbm,
    msg_a, msg_b, flat, cor_out, g_rows, lu, lv, th, floor,
    pack_e, pack_w, gravity, fold, sems,
):
    pairs = (
        (th_hbm, th), (land_hbm, floor.at[0]), (bottom_hbm, floor.at[1]), (gravity_hbm, gravity), (lu_hbm, lu),
        (lv_hbm, lv), (lev_hbm, flat.at[5]), (u_hbm, flat.at[6]), (v_hbm, flat.at[7]),
        (fold_hbm, fold),
    )
    copies = [pltpu.make_async_copy(a, b, sems.at[n]) for n, (a, b) in enumerate(pairs)]
    for copy in copies:
        copy.start()
    lon, lat = lax.axis_index("lon"), lax.axis_index("lat")
    even = lax.rem(lon, 2) == 0
    rows = (row_index((ROWS + 2 * HALO, COLS)) + (lat * ROWS - HALO)).astype(jnp.float32)
    cor_all = -coriolis_scale * jnp.cos((rows + 0.5) * (jnp.pi / TOTAL_ROWS))
    cor_out[...] = cor_all
    cor = cor_all[HALO : HALO + ROWS]
    lane = lane_index((ROWS, COLS))
    row = row_index((ROWS, COLS))
    for copy in copies:
        copy.wait()
    wet = floor[0].astype(jnp.float32)
    bot = floor[1]
    lev, u, v = flat[5], flat[6], flat[7]
    zero = jnp.zeros((ROWS, COLS), jnp.float32)
    line = lane_index((1, COLS))
    lanes_g = jnp.zeros((1, COLS), jnp.float32)
    for k in range(LAYERS):
        g_rows[k : k + 1, :] = jnp.full((1, COLS), gravity[k], jnp.float32)
        lanes_g = jnp.where(line == W_LANE + k, gravity[k], lanes_g)
    g_rows[LAYERS : LAYERS + 1, :] = lanes_g
    offset = 64 + ((fold[0] + 64) & (COLS - 1))
    g_rows[LAYERS + 1 : LAYERS + 2, :] = jnp.full((1, COLS), offset, jnp.int32).astype(jnp.float32)

    depth, potential = zero, zero
    grad_u, grad_v, sum_u, sum_v = zero, zero, zero, zero
    tails_u = []
    for k in range(LAYERS):
        w = jnp.where(bot > k, wet, 0.0) * th[k]
        depth = depth + w
        potential = potential + gravity[k] * depth
        right = jnp.where(lane == COLS - 1, 0.0, roll(potential, -1, 1))
        left = jnp.where(lane == 0, 0.0, roll(potential, 1, 1))
        above = jnp.where(row == ROWS - 1, 0.0, roll(potential, -1, 0))
        below = jnp.where(row == 0, 0.0, roll(potential, 1, 0))
        du = 0.5 * (left - right)
        dv = 0.5 * (below - above)
        grad_u = grad_u + w * du
        grad_v = grad_v + w * dv
        sum_u = sum_u + w * lu[k]
        sum_v = sum_v + w * lv[k]
        tail_u = lu[k] + baroclinic_step * (du + cor * lv[k])
        tail_v = lv[k] + baroclinic_step * (dv - cor * lu[k])
        lane_w, lane_c = W_LANE + k, C_LANE + k
        is_w, is_c = lane == lane_w, lane == lane_c
        for pack, edge in ((pack_w, 0), (pack_e, COLS - 1)):
            held = zero if k == 0 else pack[...]
            held = jnp.where(is_w, roll(w, lane_w - edge, 1), held)
            pack[...] = jnp.where(is_c, roll(tail_u, lane_c - edge, 1), held)
        for msg in (msg_a, msg_b):
            msg[W_TOP + k : W_TOP + k + 1, :] = w[ROWS - 1 :]
            msg[W_BOTTOM + k : W_BOTTOM + k + 1, :] = w[:1]
            msg[C_TOP + k : C_TOP + k + 1, :] = tail_v[ROWS - 1 :]
            msg[C_BOTTOM + k : C_BOTTOM + k + 1, :] = tail_v[:1]
    inverse = 1.0 / (depth + (1.0 - wet))
    column_u = sum_u * inverse
    column_v = sum_v * inverse
    force_u = grad_u * inverse + cor * column_v
    force_v = grad_v * inverse - cor * column_u
    fields = (depth, u, v, lev, force_u, force_v)
    flat[0] = depth
    flat[1] = force_u
    flat[2] = force_v
    flat[3] = column_u
    flat[4] = column_v
    transport_u = depth * u
    transport_v = depth * v
    strips = []
    for pack, edge, first, line in ((pack_w, 0, 0, HALO), (pack_e, COLS - 1, COLS - HALO, COLS - 1 - HALO)):
        column = jnp.sum(jnp.where(lane == edge, column_u, 0.0), axis=1, keepdims=True)
        strip = pack[...]
        strip = jnp.where((lane >= C_LANE) & (lane < C_LANE + LAYERS), strip - column, strip)
        for f, field in enumerate(fields):
            strip = jnp.where(lane // HALO == f, roll(field, HALO * f - first, 1), strip)
        strip = jnp.where(lane == T_LANE, roll(transport_u, T_LANE - line, 1), strip)
        strips.append(strip)
    west, east = strips
    msg_a[:ROWS] = jnp.where(even, east, west)
    msg_b[:ROWS] = jnp.where(even, west, east)
    for msg in (msg_a, msg_b):
        for f, field in enumerate(fields):
            msg[TOP_ROW + HALO * f : TOP_ROW + HALO * (f + 1)] = field[ROWS - HALO :]
        msg[C_TOP : C_TOP + LAYERS] = msg[C_TOP : C_TOP + LAYERS] - column_v[ROWS - 1 :]
        msg[C_BOTTOM : C_BOTTOM + LAYERS] = msg[C_BOTTOM : C_BOTTOM + LAYERS] - column_v[:1]
        msg[V_TOP : V_TOP + 1] = transport_v[ROWS - 1 - HALO : ROWS - HALO]
        msg[V_BOTTOM : V_BOTTOM + 1] = transport_v[HALO : HALO + 1]
        msg[V_BOTTOM + 1 :] = jnp.zeros((LON_ROWS - V_BOTTOM - 1, COLS), jnp.float32)


def lane_prefix(x):
    for shift in (1, 2, 4, 8):
        x = x + pltpu.roll(x, shift, 1)
    return x


def second_kernel(g_rows, flat, own_a, own_b, got_a, got_b, ext, msg_x, msg_y, msg_f):
    lon, lat = lax.axis_index("lon"), lax.axis_index("lat")
    even_lon = lax.rem(lon, 2) == 0
    even_lat = lax.rem(lat, 2) == 0
    lane = lane_index((ROWS, COLS))
    is_layer = (lane >= W_LANE) & (lane < W_LANE + LAYERS)
    weights_g = g_rows[LAYERS : LAYERS + 1, :]

    own_e = jnp.where(even_lon, own_a[:ROWS], own_b[:ROWS])
    own_w = jnp.where(even_lon, own_b[:ROWS], own_a[:ROWS])
    east = jnp.where(even_lon, got_a[:ROWS], got_b[:ROWS])
    west = jnp.where(even_lon, got_b[:ROWS], got_a[:ROWS])

    def layer_lanes(x):
        w = jnp.where(is_layer, x, 0.0)
        return w, lane_prefix(weights_g * lane_prefix(w))

    def dot(a, b):
        return jnp.sum(a * b, axis=1, keepdims=True)

    w_e, p_e = layer_lanes(own_e)
    w_w, p_w = layer_lanes(own_w)
    w_east, p_east = layer_lanes(east)
    w_west, p_west = layer_lanes(west)

    depth = flat[0]
    safe = depth + jnp.where(depth > 0.0, 0.0, 1.0)
    fix = jnp.where(lane == COLS - 1, -0.5 * dot(w_e, p_east), jnp.where(lane == 0, 0.5 * dot(w_w, p_west), 0.0))
    force_u = flat[1] + fix / safe

    sides = []
    for f in range(6):
        side = jnp.where(lane < HALO, roll(east, -HALO * f, 1), 0.0)
        side = jnp.where(lane >= COLS - HALO, roll(west, COLS - HALO - HALO * f, 1), side)
        sides.append(side)
    sides[1] = jnp.where(lane == HALO, roll(east, HALO - T_LANE, 1), sides[1])
    sides[1] = jnp.where(lane == COLS - HALO - 1, roll(west, COLS - HALO - 1 - T_LANE, 1), sides[1])
    safe = sides[0] + jnp.where(sides[0] > 0.0, 0.0, 1.0)
    fix = jnp.where(lane == 0, 0.5 * dot(w_east, p_e), jnp.where(lane == COLS - 1, -0.5 * dot(w_west, p_w), 0.0))
    sides[4] = sides[4] + fix / safe
    sides[0] = jnp.where((lane == HALO) | (lane == COLS - HALO - 1), 1.0, sides[0])

    for f, field in enumerate((depth, flat[6], flat[7], flat[5], force_u, flat[2])):
        ext[f, :, :COLS] = field
        ext[f, :, COLS:] = sides[f]

    lane12 = lane_index((LAYERS, COLS))

    def lat_message(msg, north):
        start, w_at, c_at, v_at = (ROWS - HALO, W_TOP, C_TOP, V_TOP) if north else (0, W_BOTTOM, C_BOTTOM, V_BOTTOM)
        for f in range(6):
            msg[HALO * f : HALO * (f + 1), :] = ext[f, start : start + HALO, :]
        msg[LAT_W : LAT_W + LAYERS, :COLS] = own_a[w_at : w_at + LAYERS, :]
        beside_e = jnp.where(even_lon, got_a[w_at : w_at + LAYERS, :], got_b[w_at : w_at + LAYERS, :])
        beside_w = jnp.where(even_lon, got_b[w_at : w_at + LAYERS, :], got_a[w_at : w_at + LAYERS, :])
        beside = jnp.where(lane12 < HALO, beside_e, jnp.where(lane12 >= COLS - HALO, beside_w, 0.0))
        msg[LAT_W : LAT_W + LAYERS, COLS:] = beside
        msg[LAT_C : LAT_C + LAYERS, :COLS] = own_a[c_at : c_at + LAYERS, :]
        msg[LAT_C : LAT_C + LAYERS, COLS:] = jnp.zeros((LAYERS, COLS), jnp.float32)
        msg[LAT_V : LAT_V + 1, :COLS] = own_a[v_at : v_at + 1, :]
        msg[LAT_V : LAT_V + 1, COLS:] = jnp.zeros((1, COLS), jnp.float32)
        msg[LAT_V + 1 :, :] = jnp.zeros((LAT_ROWS - LAT_V - 1, 2 * COLS), jnp.float32)

    @pl.when(even_lat)
    def _():
        lat_message(msg_x, True)
        lat_message(msg_y, False)

    @pl.when(jnp.logical_not(even_lat))
    def _():
        lat_message(msg_x, False)
        lat_message(msg_y, True)

    @pl.when(lat == lax.axis_size("lat") - 1)
    def _():
        lane8 = lane_index((8, COLS))
        offset = jnp.broadcast_to(g_rows[LAYERS + 1 : LAYERS + 2, :].astype(jnp.int32), (8, COLS))
        row8 = row_index((8, COLS))
        source = (offset - lane8) & (COLS - 1)
        block = (COLS + offset - lane8) >> 7
        side_block = jnp.where(lane8 < HALO, offset - lane8, 2 * COLS + offset - lane8) >> 7

        def gather(x, index, axis):
            return jnp.take_along_axis(x, index, axis=axis, mode="promise_in_bounds")

        def window(w_tile, o_tile, e_tile):
            a, b, c = gather(w_tile, source, 1), gather(o_tile, source, 1), gather(e_tile, source, 1)
            main = jnp.where(block == 0, a, jnp.where(block == 1, b, c))
            side = jnp.where(side_block == 0, a, jnp.where(side_block == 1, b, c))
            return main, side

        for f in range(6):
            sign = 1.0 if f in (0, 3) else -1.0
            for t in range(2):
                at = ROWS - 8 * (t + 1)
                mine = ext[f, at : at + 8, :COLS]
                side = ext[f, at : at + 8, COLS:]
                here = TOP_ROW + HALO * f + HALO - 8 * (t + 1)
                on_e = jnp.where(even_lon, got_a[here : here + 8, :], got_b[here : here + 8, :])
                on_w = jnp.where(even_lon, got_b[here : here + 8, :], got_a[here : here + 8, :])
                on_e = jnp.where(lane8 < HALO, side, on_e)
                on_w = jnp.where(lane8 >= COLS - HALO, side, on_w)
                main, beside = window(on_w, mine, on_e)
                to = HALO * f + 8 * t
                msg_f[to : to + 8, :COLS] = sign * gather(main, 7 - row8, 0)
                msg_f[to : to + 8, COLS:] = sign * gather(beside, 7 - row8, 0)
        at = W_TOP
        for t in range(3):
            mine = own_a[at + 8 * t : at + 8 * (t + 1), :]
            on_e = jnp.where(even_lon, got_a[at + 8 * t : at + 8 * (t + 1), :], got_b[at + 8 * t : at + 8 * (t + 1), :])
            on_w = jnp.where(even_lon, got_b[at + 8 * t : at + 8 * (t + 1), :], got_a[at + 8 * t : at + 8 * (t + 1), :])
            main, beside = window(on_w, mine, on_e)
            sign = jnp.where(row8 + 8 * t < LAYERS, 1.0, -1.0)
            msg_f[LAT_W + 8 * t : LAT_W + 8 * (t + 1), :COLS] = sign * main
            msg_f[LAT_W + 8 * t : LAT_W + 8 * (t + 1), COLS:] = sign * beside
        mine = own_a[V_TOP : V_TOP + 8, :]
        on_e = jnp.where(even_lon, got_a[V_TOP : V_TOP + 8, :], got_b[V_TOP : V_TOP + 8, :])
        on_w = jnp.where(even_lon, got_b[V_TOP : V_TOP + 8, :], got_a[V_TOP : V_TOP + 8, :])
        main, _ = window(on_w, mine, on_e)
        msg_f[LAT_V:, :COLS] = -main
        msg_f[LAT_V:, COLS:] = jnp.zeros((8, COLS), jnp.float32)

    @pl.when(lat != lax.axis_size("lat") - 1)
    def _():
        msg_f[...] = jnp.zeros((LAT_ROWS, 2 * COLS), jnp.float32)


def third_kernel(
    g_rows, lu, lv, th, floor, flat, cor_ref, own_a, got_a, got_b, ext, own_x, own_y, got_x, got_y, got_f,
    new_u_hbm, new_v_hbm, new_th_hbm, new_lev_hbm, mean_u_hbm, mean_v_hbm,
    north, south, level_pad, v_pad, state, fixed, pots, new_u, new_v, new_th, planes, sems, plane_sems,
):
    lon, lat = lax.axis_index("lon"), lax.axis_index("lat")
    even_lon = lax.rem(lon, 2) == 0
    even_lat = lax.rem(lat, 2) == 0
    at_top = lat == lax.axis_size("lat") - 1
    at_bottom = lat == 0
    full = ROWS + 2 * HALO
    wide = 2 * COLS
    north[...] = jnp.where(at_top, got_f[...], jnp.where(even_lat, got_x[...], got_y[...]))
    south[...] = jnp.where(at_bottom, 0.0, jnp.where(even_lat, got_y[...], got_x[...]))

    def whole(f):
        at = HALO * f
        return jnp.concatenate([south[at : at + HALO, :], ext[f], north[at : at + HALO, :]], axis=0)

    depth, u, v, level, force_u, force_v = (whole(f) for f in range(6))
    wet = jnp.where(depth > 0.0, 1.0, 0.0)
    cor = jnp.concatenate([cor_ref[...], cor_ref[...]], axis=1)

    def seam(at, below_w, above_w):
        sum_b, sum_a, pot_b, pot_a, to_b, to_a = (jnp.zeros((1, wide), jnp.float32) for _ in range(6))
        for k in range(LAYERS):
            wb, wa = below_w(k), above_w(k)
            g = jnp.concatenate([g_rows[k : k + 1, :]] * 2, axis=1)
            sum_b, sum_a = sum_b + wb, sum_a + wa
            pot_b, pot_a = pot_b + g * sum_b, pot_a + g * sum_a
            to_b = to_b + wb * pot_a
            to_a = to_a + wa * pot_b
            pots[at, k : k + 1, :] = pot_b[:, :COLS]
            pots[at + 1, k : k + 1, :] = pot_a[:, :COLS]
        safe_b = sum_b + jnp.where(sum_b > 0.0, 0.0, 1.0)
        safe_a = sum_a + jnp.where(sum_a > 0.0, 0.0, 1.0)
        return -0.5 * to_b / safe_b, 0.5 * to_a / safe_a

    def own_edge(top):
        def get(k):
            at = LAT_W + k
            x, y = own_x[at : at + 1, :], own_y[at : at + 1, :]
            return jnp.where(even_lat, x, y) if top else jnp.where(even_lat, y, x)
        return get

    row = row_index((full, wide))
    fix_b, fix_a = seam(0, own_edge(True), lambda k: north[LAT_W + k : LAT_W + k + 1, :])
    force_v = force_v + jnp.where(row == HALO + ROWS - 1, fix_b, jnp.where(row == HALO + ROWS, fix_a, 0.0))
    fix_b, fix_a = seam(2, lambda k: south[LAT_W + k : LAT_W + k + 1, :], own_edge(False))
    force_v = force_v + jnp.where(row == HALO - 1, fix_b, jnp.where(row == HALO, fix_a, 0.0))

    fixed[0] = depth
    fixed[1] = wet * (1.0 - barotropic_step * bottom_drag)
    fixed[2] = wet * (barotropic_step * cor)
    fixed[3] = wet * (barotropic_step * force_u)
    fixed[4] = wet * (barotropic_step * force_v)
    fixed[5] = wet * (0.5 * barotropic_step)
    fixed[6] = jnp.where(at_bottom & (row < HALO), 0.0, 0.5 * barotropic_step)
    state[0] = u
    state[1] = v
    state[2] = jnp.zeros((full, wide), jnp.float32)
    state[3] = jnp.zeros((full, wide), jnp.float32)
    level_pad[8 : 8 + full, :] = level
    v_pad[7:8, :] = south[LAT_V : LAT_V + 1, :]
    v_pad[8 + full : 9 + full, :] = north[LAT_V : LAT_V + 1, :]

    def substep(_, carry):
        depth, u, v = fixed[0], state[0], state[1]
        trans_u = depth * u
        v_pad[8 : 8 + full, :] = depth * v
        dv = v_pad[9 : 9 + full, :] - v_pad[7 : 7 + full, :]
        du = pltpu.roll(trans_u, wide - 1, 1) - pltpu.roll(trans_u, 1, 1)
        level = level_pad[8 : 8 + full, :] - fixed[6] * (du + dv)
        level_pad[8 : 8 + full, :] = level
        dy = level_pad[9 : 9 + full, :] - level_pad[7 : 7 + full, :]
        dx = pltpu.roll(level, wide - 1, 1) - pltpu.roll(level, 1, 1)
        keep, turn, slope = fixed[1], fixed[2], fixed[5]
        next_u = keep * u + turn * v + fixed[3] - slope * dx
        next_v = keep * v - turn * u + fixed[4] - slope * dy
        state[0] = next_u
        state[1] = next_v
        state[2] = state[2] + next_u
        state[3] = state[3] + next_v
        return carry

    for _ in range(SUBSTEPS):
        substep(0, 0)
    mean_u = state[2] * (1.0 / SUBSTEPS)
    mean_v = state[3] * (1.0 / SUBSTEPS)
    inner = slice(HALO, HALO + ROWS)
    planes[0] = level_pad[8 + HALO : 8 + HALO + ROWS, :COLS]
    planes[1] = mean_u[inner, :COLS]
    planes[2] = mean_v[inner, :COLS]
    plane_copies = [
        pltpu.make_async_copy(planes.at[n], out, plane_sems.at[n])
        for n, out in enumerate((new_lev_hbm, mean_u_hbm, mean_v_hbm))
    ]
    for copy in plane_copies:
        copy.start()

    rest_u = mean_u - baroclinic_step * force_u
    rest_v = mean_v - baroclinic_step * force_v
    lane = lane_index((ROWS, COLS))
    row = row_index((ROWS, COLS))
    is_e, is_w = lane == COLS - 1, lane == 0
    is_n, is_s = row == ROWS - 1, row == 0
    side_u = rest_u[inner, COLS:]
    halo_rest = jnp.where(is_e, pltpu.roll(side_u, COLS - 1, 1), pltpu.roll(side_u, 1, 1))
    rest_n = rest_v[HALO + ROWS : HALO + ROWS + 1, :COLS]
    rest_s = rest_v[HALO - 1 : HALO, :COLS]
    base_u = rest_u[inner, :COLS] - flat[3]
    base_v = rest_v[inner, :COLS] - flat[4]
    east = jnp.where(even_lon, got_a[:ROWS], got_b[:ROWS])
    west = jnp.where(even_lon, got_b[:ROWS], got_a[:ROWS])
    half = 0.5 * baroclinic_step
    signed = jnp.where(is_e, half, -half)
    cor = cor_ref[HALO : HALO + ROWS, :]
    land_f = floor[0].astype(jnp.float32)
    bot = floor[1]
    zero = jnp.zeros((ROWS, COLS), jnp.float32)

    def edged(x, halo, axis):
        if axis == 1:
            return jnp.where(is_e, halo, pltpu.roll(x, COLS - 1, 1)) - jnp.where(is_w, halo, pltpu.roll(x, 1, 1))
        above, below = halo
        return jnp.where(is_n, above, pltpu.roll(x, ROWS - 1, 0)) - jnp.where(is_s, below, pltpu.roll(x, 1, 0))

    def layer_copies(k):
        return [
            pltpu.make_async_copy(held.at[k], out.at[k], sems.at[n, k])
            for n, (held, out) in enumerate(((new_u, new_u_hbm), (new_v, new_v_hbm), (new_th, new_th_hbm)))
        ]

    def layer(k, carry):
        thick, potential, halo_thick, halo_potential = carry
        g = g_rows[pl.ds(k, 1), :]
        mask = jnp.where(bot > k, land_f, 0.0)
        th_k, lu_k, lv_k = th[k], lu[k], lv[k]
        w = mask * th_k
        thick = thick + w
        potential = potential + g * thick
        halo_w = jnp.where(is_e, pltpu.roll(east, COLS + COLS - 1 - W_LANE - k, 1), pltpu.roll(west, COLS - W_LANE - k, 1))
        halo_c = jnp.where(is_e, pltpu.roll(east, COLS + COLS - 1 - C_LANE - k, 1), pltpu.roll(west, COLS - C_LANE - k, 1))
        halo_thick = halo_thick + halo_w
        halo_potential = halo_potential + g * halo_thick

        def at_row(ref, at):
            return ref[pl.ds(at + k, 1), :][:, :COLS]

        def pot(n):
            return pots[n, pl.ds(k, 1), :]

        du = edged(potential, halo_potential, 1)
        dv = edged(potential, (pot(1), pot(2)), 0)
        out_u = mask * (lu_k + baroclinic_step * (cor * lv_k - 0.5 * du) + base_u)
        out_v = mask * (lv_k - baroclinic_step * (cor * lu_k + 0.5 * dv) + base_v)
        new_u[k] = out_u
        new_v[k] = out_v
        halo_flux = halo_w * (halo_c + signed * potential + halo_rest)
        flux_n = at_row(north, LAT_W) * (at_row(north, LAT_C) + half * pot(0) + rest_n)
        flux_s = at_row(south, LAT_W) * (at_row(south, LAT_C) - half * pot(3) + rest_s)
        divergence = edged(w * out_u, halo_flux, 1) + edged(w * out_v, (flux_n, flux_s), 0)
        new_th[k] = th_k - half * divergence
        for copy in layer_copies(k):
            copy.start()
        return thick, potential, halo_thick, halo_potential

    carry = (zero, zero, zero, zero)
    for k in range(LAYERS):
        carry = layer(k, carry)

    def finish(k, carry):
        for copy in layer_copies(k):
            copy.wait()
        return carry

    for k in range(LAYERS):
        finish(k, 0)
    for copy in plane_copies:
        copy.wait()


def vmem(count):
    return [pl.BlockSpec(memory_space=pltpu.VMEM)] * count


def hbm(count):
    return [pl.BlockSpec(memory_space=pltpu.HBM)] * count


def f32(*shape):
    return jax.ShapeDtypeStruct(shape, jnp.float32)


PARAMS = pltpu.CompilerParams(vmem_limit_bytes=40 * 2**20)


def local(lu, lv, th, lev, u, v, land, bottom, fold_map, gravity):
    lons, lats = lax.axis_size("lon"), lax.axis_size("lat")
    lon_msg = f32(LON_ROWS, COLS)
    full = ROWS + 2 * HALO
    layers = f32(LAYERS, ROWS, COLS)
    plane = f32(ROWS, COLS)
    msg_a, msg_b, flat, cor, g_rows, lu, lv, th, floor = pl.pallas_call(
        first_kernel,
        out_shape=(
            lon_msg, lon_msg, f32(8, ROWS, COLS), f32(full, COLS), f32(16, COLS), layers, layers, layers,
            jax.ShapeDtypeStruct((2, ROWS, COLS), jnp.int32),
        ),
        in_specs=hbm(10),
        out_specs=vmem(9),
        scratch_shapes=[
            pltpu.VMEM((ROWS, COLS), jnp.float32),
            pltpu.VMEM((ROWS, COLS), jnp.float32),
            pltpu.SMEM((LAYERS,), jnp.float32),
            pltpu.SMEM((COLS,), jnp.int32),
            pltpu.SemaphoreType.DMA((10,)),
        ],
        compiler_params=PARAMS,
        name="edges",
    )(*(pltpu.with_memory_space_constraint(x, pltpu.HBM) for x in (gravity, lu, lv, th, lev, u, v, land, bottom, fold_map)))

    got_a = lax.ppermute(msg_a, "lon", [(i, i ^ 1) for i in range(lons)])
    got_b = lax.ppermute(msg_b, "lon", [(i, ((i + 1) ^ 1) - 1 & (lons - 1)) for i in range(lons)])

    lat_msg = f32(LAT_ROWS, 2 * COLS)
    ext, msg_x, msg_y, msg_f = pl.pallas_call(
        second_kernel,
        out_shape=(f32(6, ROWS, 2 * COLS), lat_msg, lat_msg, lat_msg),
        in_specs=vmem(6),
        out_specs=vmem(4),
        compiler_params=PARAMS,
        name="extend",
    )(g_rows, flat, msg_a, msg_b, got_a, got_b)

    got_x = lax.ppermute(msg_x, "lat", [(i, i ^ 1) for i in range(lats)])
    got_y = lax.ppermute(msg_y, "lat", [(i, ((i + 1) ^ 1) - 1) for i in range(1, lats - 1)])
    total = lons * COLS
    pivot = fold_map[0] + lax.axis_index("lon") * COLS
    shift = jnp.mod(pivot - COLS // 2, total) // COLS
    top = lats - 1

    def mirrored(q):
        pairs = [(((q - b) % lons) * lats + top, b * lats + top) for b in range(lons)]
        return lambda x: lax.ppermute(x, ("lon", "lat"), pairs)

    got_f = lax.switch(shift, [mirrored(q) for q in range(lons)], msg_f)

    padded = pltpu.VMEM((full + 16, 2 * COLS), jnp.float32)
    held = pltpu.VMEM((LAYERS, ROWS, COLS), jnp.float32)
    return pl.pallas_call(
        third_kernel,
        out_shape=(layers, layers, layers, plane, plane, plane),
        in_specs=vmem(16),
        out_specs=hbm(6),
        scratch_shapes=[
            pltpu.VMEM((LAT_ROWS, 2 * COLS), jnp.float32),
            pltpu.VMEM((LAT_ROWS, 2 * COLS), jnp.float32),
            padded,
            padded,
            pltpu.VMEM((4, full, 2 * COLS), jnp.float32),
            pltpu.VMEM((7, full, 2 * COLS), jnp.float32),
            pltpu.VMEM((4, 16, COLS), jnp.float32),
            held,
            held,
            held,
            pltpu.VMEM((3, ROWS, COLS), jnp.float32),
            pltpu.SemaphoreType.DMA((3, LAYERS)),
            pltpu.SemaphoreType.DMA((3,)),
        ],
        compiler_params=PARAMS,
        name="advance",
    )(g_rows, lu, lv, th, floor, flat, cor, msg_a, got_a, got_b, ext, msg_x, msg_y, got_x, got_y, got_f)


def solution(mesh):
    layered, plane = P(None, "lat", "lon"), P("lat", "lon")
    return jax.shard_map(
        local,
        mesh=mesh,
        in_specs=(layered,) * 3 + (plane,) * 5 + (P("lon"), P()),
        out_specs=(layered,) * 3 + (plane,) * 3,
        check_vma=False,
    )
```

```python
import jax
import jax.numpy as jnp
from jax import lax
from jax.experimental import pallas as pl
from jax.experimental.pallas import tpu as pltpu
from jax.sharding import PartitionSpec as P

SUBSTEPS = 8
LAYERS = 12
TOTAL_ROWS = 512
ROWS, COLS = 64, 128
HALO = 16

barotropic_step = 0.45
baroclinic_step = 0.1
coriolis_scale = 0.3
bottom_drag = 0.05

PAIR_LANE = 96
PAIR_END = PAIR_LANE + 2 * LAYERS
T_LANE = PAIR_END
TOP_ROW = 64
W_TOP, C_TOP, W_BOTTOM, C_BOTTOM = 160, 172, 184, 196
V_TOP, V_BOTTOM = 208, 209
LON_ROWS = 216
LAT_W, LAT_C, LAT_V, LAT_SIDE, LAT_ROWS = 96, 108, 120, 128, 160
FULL = ROWS + 2 * HALO
WIDE = 2 * COLS
half = 0.5 * baroclinic_step


def lane_index(shape):
    return lax.broadcasted_iota(jnp.int32, shape, 1)


def row_index(shape):
    return lax.broadcasted_iota(jnp.int32, shape, 0)


def roll(x, shift, axis):
    shift = shift % x.shape[axis]
    return x if shift == 0 else pltpu.roll(x, shift, axis)


def first_kernel(
    gravity_hbm, lu_hbm, lv_hbm, th_hbm, lev_hbm, u_hbm, v_hbm, land_hbm, bottom_hbm, fold_hbm,
    msg_a, msg_b, flat, cor_out, g_rows, tail_u, tail_v, weight, th, floor,
    lu, lv, gravity, fold, sems,
):
    pairs = (
        (th_hbm, th), (land_hbm, floor.at[0]), (bottom_hbm, floor.at[1]), (gravity_hbm, gravity), (lu_hbm, lu),
        (lv_hbm, lv), (lev_hbm, flat.at[5]), (u_hbm, flat.at[6]), (v_hbm, flat.at[7]),
        (fold_hbm, fold),
    )
    copies = [pltpu.make_async_copy(a, b, sems.at[n]) for n, (a, b) in enumerate(pairs)]
    for copy in copies:
        copy.start()
    lon, lat = lax.axis_index("lon"), lax.axis_index("lat")
    even = lax.rem(lon, 2) == 0
    rows = (row_index((FULL, COLS)) + (lat * ROWS - HALO)).astype(jnp.float32)
    cor_all = -coriolis_scale * jnp.cos((rows + 0.5) * (jnp.pi / TOTAL_ROWS))
    cor_out[...] = cor_all
    cor = cor_all[HALO : HALO + ROWS]
    lane = lane_index((ROWS, COLS))
    row = row_index((ROWS, COLS))
    for copy in copies:
        copy.wait()
    wet = floor[0].astype(jnp.float32)
    bot = floor[1]
    lev, u, v = flat[5], flat[6], flat[7]
    zero = jnp.zeros((ROWS, COLS), jnp.float32)
    line = lane_index((1, COLS))
    lanes_g = jnp.zeros((1, COLS), jnp.float32)
    for k in range(LAYERS):
        g_rows[k : k + 1, :] = jnp.full((1, COLS), gravity[k], jnp.float32)
        lanes_g = jnp.where(line == PAIR_LANE + 2 * k, gravity[k], lanes_g)
    g_rows[LAYERS : LAYERS + 1, :] = lanes_g
    offset = 64 + ((fold[0] + 64) & (COLS - 1))
    g_rows[LAYERS + 1 : LAYERS + 2, :] = jnp.full((1, COLS), offset, jnp.int32).astype(jnp.float32)

    depth, potential = zero, zero
    grad_u, grad_v, sum_u, sum_v = zero, zero, zero, zero
    edge_w, edge_c = zero, zero
    for k in range(LAYERS):
        w = jnp.where(bot > k, wet, 0.0) * th[k]
        depth = depth + w
        potential = potential + gravity[k] * depth
        right = jnp.where(lane == COLS - 1, 0.0, roll(potential, -1, 1))
        left = jnp.where(lane == 0, 0.0, roll(potential, 1, 1))
        above = jnp.where(row == ROWS - 1, 0.0, roll(potential, -1, 0))
        below = jnp.where(row == 0, 0.0, roll(potential, 1, 0))
        du = 0.5 * (left - right)
        dv = 0.5 * (below - above)
        grad_u = grad_u + w * du
        grad_v = grad_v + w * dv
        sum_u = sum_u + w * lu[k]
        sum_v = sum_v + w * lv[k]
        rest_u = lu[k] + baroclinic_step * (du + cor * lv[k])
        rest_v = lv[k] + baroclinic_step * (dv - cor * lu[k])
        tail_u[k] = rest_u
        tail_v[k] = rest_v
        weight[k] = w
        here = (lane == 2 * k) | (lane == 2 * k + 1)
        edge_w = jnp.where(here, roll(w, 2 * k + 1, 1), edge_w)
        edge_c = jnp.where(here, roll(rest_u, 2 * k + 1, 1), edge_c)
        for msg in (msg_a, msg_b):
            msg[W_TOP + k : W_TOP + k + 1, :] = w[ROWS - 1 :]
            msg[W_BOTTOM + k : W_BOTTOM + k + 1, :] = w[:1]
            msg[C_TOP + k : C_TOP + k + 1, :] = rest_v[ROWS - 1 :]
            msg[C_BOTTOM + k : C_BOTTOM + k + 1, :] = rest_v[:1]
    inverse = 1.0 / (depth + (1.0 - wet))
    column_u = sum_u * inverse
    column_v = sum_v * inverse
    force_u = grad_u * inverse + cor * column_v
    force_v = grad_v * inverse - cor * column_u
    fields = (depth, u, v, lev, force_u, force_v)
    flat[0] = depth
    flat[1] = force_u
    flat[2] = force_v
    flat[3] = column_u
    flat[4] = column_v
    transport_u = depth * u
    transport_v = depth * v
    is_pair = (lane >= PAIR_LANE) & (lane < PAIR_END)
    is_first = is_pair & (lane % 2 == 0)
    is_second = is_pair & (lane % 2 == 1)
    strips = []
    for side, edge, first, line in ((1, 0, 0, HALO), (0, COLS - 1, COLS - HALO, COLS - 1 - HALO)):
        column = jnp.sum(jnp.where(lane == edge, column_u, 0.0), axis=1, keepdims=True)
        strip = jnp.where(is_first, roll(edge_w, PAIR_LANE - side, 1), zero)
        strip = jnp.where(is_second, roll(edge_c, PAIR_LANE + 1 - side, 1) - column, strip)
        for f, field in enumerate(fields):
            strip = jnp.where(lane // HALO == f, roll(field, HALO * f - first, 1), strip)
        strip = jnp.where(lane == T_LANE, roll(transport_u, T_LANE - line, 1), strip)
        strips.append(strip)
    west, east = strips
    msg_a[:ROWS] = jnp.where(even, east, west)
    msg_b[:ROWS] = jnp.where(even, west, east)
    for msg in (msg_a, msg_b):
        for f, field in enumerate(fields):
            msg[TOP_ROW + HALO * f : TOP_ROW + HALO * (f + 1)] = field[ROWS - HALO :]
        msg[C_TOP : C_TOP + LAYERS] = msg[C_TOP : C_TOP + LAYERS] - column_v[ROWS - 1 :]
        msg[C_BOTTOM : C_BOTTOM + LAYERS] = msg[C_BOTTOM : C_BOTTOM + LAYERS] - column_v[:1]
        msg[V_TOP : V_TOP + 1] = transport_v[ROWS - 1 - HALO : ROWS - HALO]
        msg[V_BOTTOM : V_BOTTOM + 1] = transport_v[HALO : HALO + 1]
        msg[V_BOTTOM + 1 :] = jnp.zeros((LON_ROWS - V_BOTTOM - 1, COLS), jnp.float32)


def lane_prefix(x):
    for shift in (2, 4, 8, 16):
        x = x + pltpu.roll(x, shift, 1)
    return x


def second_kernel(g_rows, flat, own_a, own_b, got_a, got_b, ext, edges, msg_x, msg_y, msg_f):
    lon, lat = lax.axis_index("lon"), lax.axis_index("lat")
    even_lon = lax.rem(lon, 2) == 0
    even_lat = lax.rem(lat, 2) == 0
    lane = lane_index((ROWS, COLS))
    is_first = (lane >= PAIR_LANE) & (lane < PAIR_END) & (lane % 2 == 0)
    weights_g = g_rows[LAYERS : LAYERS + 1, :]

    own_e = jnp.where(even_lon, own_a[:ROWS], own_b[:ROWS])
    own_w = jnp.where(even_lon, own_b[:ROWS], own_a[:ROWS])
    east = jnp.where(even_lon, got_a[:ROWS], got_b[:ROWS])
    west = jnp.where(even_lon, got_b[:ROWS], got_a[:ROWS])

    def layer_lanes(x):
        w = jnp.where(is_first, x, 0.0)
        return w, lane_prefix(weights_g * lane_prefix(w))

    def dot(a, b):
        return jnp.sum(a * b, axis=1, keepdims=True)

    w_e, p_e = layer_lanes(own_e)
    w_w, p_w = layer_lanes(own_w)
    w_east, p_east = layer_lanes(east)
    w_west, p_west = layer_lanes(west)

    def paired(a, b):
        return jnp.where(is_first, a, pltpu.roll(b, 1, 1))

    edges[0] = paired(-half * p_east, half * p_west)
    edges[1] = paired(w_east * (roll(east, -1, 1) + half * p_e), w_west * (roll(west, -1, 1) - half * p_w))
    edges[2] = paired(w_east, w_west)

    depth = flat[0]
    safe = depth + jnp.where(depth > 0.0, 0.0, 1.0)
    fix = jnp.where(lane == COLS - 1, -0.5 * dot(w_e, p_east), jnp.where(lane == 0, 0.5 * dot(w_w, p_west), 0.0))
    force_u = flat[1] + fix / safe

    sides = []
    for f in range(6):
        side = jnp.where(lane < HALO, roll(east, -HALO * f, 1), 0.0)
        side = jnp.where(lane >= COLS - HALO, roll(west, COLS - HALO - HALO * f, 1), side)
        sides.append(side)
    sides[1] = jnp.where(lane == HALO, roll(east, HALO - T_LANE, 1), sides[1])
    sides[1] = jnp.where(lane == COLS - HALO - 1, roll(west, COLS - HALO - 1 - T_LANE, 1), sides[1])
    safe = sides[0] + jnp.where(sides[0] > 0.0, 0.0, 1.0)
    fix = jnp.where(lane == 0, 0.5 * dot(w_east, p_e), jnp.where(lane == COLS - 1, -0.5 * dot(w_west, p_w), 0.0))
    sides[4] = sides[4] + fix / safe
    sides[0] = jnp.where((lane == HALO) | (lane == COLS - HALO - 1), 1.0, sides[0])

    for f, field in enumerate((depth, flat[6], flat[7], flat[5], force_u, flat[2])):
        ext[f, :, :COLS] = field
        ext[f, :, COLS:] = sides[f]

    lane12 = lane_index((LAYERS, COLS))
    lane16 = lane_index((HALO, COLS))

    def lat_message(msg, north):
        start, w_at, c_at, v_at = (ROWS - HALO, W_TOP, C_TOP, V_TOP) if north else (0, W_BOTTOM, C_BOTTOM, V_BOTTOM)
        packed = [jnp.zeros((HALO, COLS), jnp.float32)] * 2
        for f in range(6):
            msg[HALO * f : HALO * (f + 1), :] = ext[f, start : start + HALO, :COLS]
            side = roll(ext[f, start : start + HALO, COLS:], HALO + 32 * (f % 4), 1)
            packed[f // 4] = jnp.where(lane16 // 32 == f % 4, side, packed[f // 4])
        msg[LAT_SIDE : LAT_SIDE + HALO, :] = packed[0]
        msg[LAT_SIDE + HALO :, :] = packed[1]
        msg[LAT_W : LAT_W + LAYERS, :] = own_a[w_at : w_at + LAYERS, :]
        beside_e = jnp.where(even_lon, got_a[w_at : w_at + LAYERS, :], got_b[w_at : w_at + LAYERS, :])
        beside_w = jnp.where(even_lon, got_b[w_at : w_at + LAYERS, :], got_a[w_at : w_at + LAYERS, :])
        beside = roll(jnp.where(lane12 < HALO, beside_e, beside_w), HALO + 64, 1)
        held = msg[LAT_SIDE + HALO : LAT_SIDE + HALO + LAYERS, :]
        msg[LAT_SIDE + HALO : LAT_SIDE + HALO + LAYERS, :] = jnp.where(lane12 // 32 == 2, beside, held)
        msg[LAT_C : LAT_C + LAYERS, :] = own_a[c_at : c_at + LAYERS, :]
        msg[LAT_V : LAT_V + 1, :] = own_a[v_at : v_at + 1, :]
        msg[LAT_V + 1 : LAT_SIDE, :] = jnp.zeros((LAT_SIDE - LAT_V - 1, COLS), jnp.float32)

    @pl.when(even_lat)
    def _():
        lat_message(msg_x, True)
        lat_message(msg_y, False)

    @pl.when(jnp.logical_not(even_lat))
    def _():
        lat_message(msg_x, False)
        lat_message(msg_y, True)

    @pl.when(lat == lax.axis_size("lat") - 1)
    def _():
        lane8 = lane_index((8, COLS))
        row8 = row_index((8, COLS))
        offset = jnp.broadcast_to(g_rows[LAYERS + 1 : LAYERS + 2, :].astype(jnp.int32), (8, COLS))
        source = (offset - lane8) & (COLS - 1)
        block = (COLS + offset - lane8) >> 7
        side_block = jnp.where(lane8 < HALO, offset - lane8, 2 * COLS + offset - lane8) >> 7

        def gather(x, index, axis):
            return jnp.take_along_axis(x, index, axis=axis, mode="promise_in_bounds")

        def window(w_tile, o_tile, e_tile):
            a, b, c = gather(w_tile, source, 1), gather(o_tile, source, 1), gather(e_tile, source, 1)
            main = jnp.where(block == 0, a, jnp.where(block == 1, b, c))
            side = jnp.where(side_block == 0, a, jnp.where(side_block == 1, b, c))
            return main, side

        def tiles(at):
            on_e = jnp.where(even_lon, got_a[at : at + 8, :], got_b[at : at + 8, :])
            on_w = jnp.where(even_lon, got_b[at : at + 8, :], got_a[at : at + 8, :])
            return on_w, own_a[at : at + 8, :], on_e

        packed = {}

        def pack(at, group, x):
            x = roll(x, HALO + 32 * group, 1)
            packed[at] = jnp.where(lane8 // 32 == group, x, packed[at]) if at in packed else x

        for f in range(6):
            sign = 1.0 if f in (0, 3) else -1.0
            for t in range(2):
                at = ROWS - 8 * (t + 1)
                mine = ext[f, at : at + 8, :COLS]
                side = ext[f, at : at + 8, COLS:]
                on_w, _, on_e = tiles(TOP_ROW + HALO * f + HALO - 8 * (t + 1))
                on_e = jnp.where(lane8 < HALO, side, on_e)
                on_w = jnp.where(lane8 >= COLS - HALO, side, on_w)
                main, beside = window(on_w, mine, on_e)
                msg_f[HALO * f + 8 * t : HALO * f + 8 * (t + 1), :] = sign * gather(main, 7 - row8, 0)
                pack(LAT_SIDE + HALO * (f // 4) + 8 * t, f % 4, sign * gather(beside, 7 - row8, 0))
        for t in range(3):
            main, beside = window(*tiles(W_TOP + 8 * t))
            sign = jnp.where(row8 + 8 * t < LAYERS, 1.0, -1.0)
            msg_f[LAT_W + 8 * t : LAT_W + 8 * (t + 1), :] = sign * main
            if t < 2:
                pack(LAT_SIDE + HALO + 8 * t, 2, beside)
        main, _ = window(*tiles(V_TOP))
        msg_f[LAT_V : LAT_V + 8, :] = -main
        for at, x in packed.items():
            msg_f[at : at + 8, :] = x

    @pl.when(lat != lax.axis_size("lat") - 1)
    def _():
        msg_f[...] = jnp.zeros((LAT_ROWS, COLS), jnp.float32)


def third_kernel(
    g_rows, tail_u, tail_v, weight, th, floor, flat, cor_ref, edges, ext, own_x, own_y, got_x, got_y, got_f_hbm,
    new_u_hbm, new_v_hbm, new_th_hbm, new_lev_hbm, mean_u_hbm, mean_v_hbm,
    far, level_pad, v_pad, state, fixed, pots, seam_w, seam_rows, new_u, new_v, new_th, planes,
    sems, plane_sems, far_sem,
):
    lat = lax.axis_index("lat")
    even = lax.rem(lat, 2) == 0
    at_top = lat == lax.axis_size("lat") - 1
    at_bottom = lat == 0

    fold_copy = pltpu.make_async_copy(got_f_hbm, far, far_sem.at[0])
    fold_copy.start()
    inner = slice(HALO, HALO + ROWS)

    def place(at, count, depth, u, v, level, force_u, force_v, rate):
        rows = pl.ds(at, count)
        cor = cor_ref[rows, :]
        cor = jnp.concatenate([cor, cor], axis=1)
        wet = jnp.where(depth > 0.0, 1.0, 0.0)
        fixed[0, rows, :] = depth
        fixed[1, rows, :] = wet * (1.0 - barotropic_step * bottom_drag)
        fixed[2, rows, :] = wet * (barotropic_step * cor)
        fixed[3, rows, :] = wet * (barotropic_step * force_u)
        fixed[4, rows, :] = wet * (barotropic_step * force_v)
        fixed[5, rows, :] = wet * (0.5 * barotropic_step)
        fixed[6, rows, :] = jnp.full((count, WIDE), rate, jnp.float32)
        state[0, rows, :] = u
        state[1, rows, :] = v
        level_pad[pl.ds(at + 8, count), :] = level

    place(HALO, ROWS, *(ext[f] for f in range(6)), 0.5 * barotropic_step)

    def strip(got, mine, slot, is_north, keep):
        at = pl.multiple_of(jnp.where(is_north, HALO + ROWS, 0), HALO)
        sign = jnp.where(is_north, 1.0, -1.0)
        fields = []
        for f in range(6):
            main = got[HALO * f : HALO * (f + 1), :]
            side = got[LAT_SIDE + HALO * (f // 4) : LAT_SIDE + HALO * (f // 4 + 1), :]
            side = roll(side, -HALO - 32 * (f % 4), 1)
            fields.append(jnp.concatenate([main, side], axis=1))
        if keep is not None:
            fields = [jnp.where(keep, field, 0.0) for field in fields]
        rate = 0.5 * barotropic_step
        place(at, HALO, *fields, rate if keep is None else jnp.where(keep, rate, 0.0))
        v_row = got[LAT_V : LAT_V + 1, :]
        if keep is not None:
            v_row = jnp.where(keep, v_row, 0.0)
        v_rows = pl.ds(pl.multiple_of(jnp.where(is_north, 8 + FULL, 0), 8), 8)
        v_pad[v_rows, :COLS] = jnp.broadcast_to(v_row, (8, COLS))
        v_pad[v_rows, COLS:] = jnp.zeros((8, COLS), jnp.float32)
        for n, ref in enumerate((mine, got)):
            w = ref[LAT_W : LAT_W + LAYERS, :]
            side = roll(ref[LAT_SIDE + HALO : LAT_SIDE + HALO + LAYERS, :], -HALO - 64, 1)
            if n == 1 and keep is not None:
                w, side = jnp.where(keep, w, 0.0), jnp.where(keep, side, 0.0)
            seam_w[n, :LAYERS, :COLS] = w
            seam_w[n, :LAYERS, COLS:] = side
        sum_o, sum_s, pot_o, pot_s, to_o, to_s = (jnp.zeros((1, WIDE), jnp.float32) for _ in range(6))
        for k in range(LAYERS):
            wo, ws = seam_w[0, k : k + 1, :], seam_w[1, k : k + 1, :]
            g = jnp.concatenate([g_rows[k : k + 1, :]] * 2, axis=1)
            sum_o, sum_s = sum_o + wo, sum_s + ws
            pot_o, pot_s = pot_o + g * sum_o, pot_s + g * sum_s
            to_o = to_o + wo * pot_s
            to_s = to_s + ws * pot_o
            pots[0, k : k + 1, :] = pot_o[:, :COLS]
            pots[1, k : k + 1, :] = pot_s[:, :COLS]
        safe_o = sum_o + jnp.where(sum_o > 0.0, 0.0, 1.0)
        safe_s = sum_s + jnp.where(sum_s > 0.0, 0.0, 1.0)
        scale = 0.5 * barotropic_step * sign
        row8 = row_index((8, WIDE))
        own_rows = pl.ds(pl.multiple_of(jnp.where(is_north, HALO + ROWS - 8, HALO), 8), 8)
        strip_rows = pl.ds(pl.multiple_of(jnp.where(is_north, HALO + ROWS, HALO - 8), 8), 8)
        last, first = row8 == jnp.where(is_north, 7, 0), row8 == jnp.where(is_north, 0, 7)
        fixed[4, own_rows, :] = fixed[4, own_rows, :] - jnp.where(last, scale * to_o / safe_o, 0.0)
        fixed[4, strip_rows, :] = fixed[4, strip_rows, :] + jnp.where(first, scale * to_s / safe_s, 0.0)
        side = jnp.where(is_north, 0, 3)
        w = seam_w[1, :LAYERS, :COLS]
        seam_rows[side, :LAYERS, :] = (-half * sign) * pots[1, :LAYERS, :]
        seam_rows[side + 1, :LAYERS, :] = w * (got[LAT_C : LAT_C + LAYERS, :] + (half * sign) * pots[0, :LAYERS, :])
        seam_rows[side + 2, :LAYERS, :] = w

    strip(got_x, own_x, 0, even, None)
    fold_copy.wait()

    @pl.when(jnp.logical_not(at_top))
    def _():
        far[...] = got_y[...]

    strip(far, own_y, 1, jnp.logical_not(even), jnp.logical_not(at_bottom))

    for step in range(SUBSTEPS):
        depth, u, v = fixed[0], state[0], state[1]
        trans_u = depth * u
        v_pad[8 : 8 + FULL, :] = depth * v
        dv = v_pad[9 : 9 + FULL, :] - v_pad[7 : 7 + FULL, :]
        du = pltpu.roll(trans_u, WIDE - 1, 1) - pltpu.roll(trans_u, 1, 1)
        level = level_pad[8 : 8 + FULL, :] - fixed[6] * (du + dv)
        level_pad[8 : 8 + FULL, :] = level
        dy = level_pad[9 : 9 + FULL, :] - level_pad[7 : 7 + FULL, :]
        dx = pltpu.roll(level, WIDE - 1, 1) - pltpu.roll(level, 1, 1)
        keep, turn, slope = fixed[1], fixed[2], fixed[5]
        next_u = keep * u + turn * v + fixed[3] - slope * dx
        next_v = keep * v - turn * u + fixed[4] - slope * dy
        state[0] = next_u
        state[1] = next_v
        state[2] = next_u if step == 0 else state[2] + next_u
        state[3] = next_v if step == 0 else state[3] + next_v
    planes[0] = level_pad[8 + HALO : 8 + HALO + ROWS, :COLS]
    planes[1] = state[2, inner, :COLS] * (1.0 / SUBSTEPS)
    planes[2] = state[3, inner, :COLS] * (1.0 / SUBSTEPS)
    plane_copies = [
        pltpu.make_async_copy(planes.at[n], out, plane_sems.at[n])
        for n, out in enumerate((new_lev_hbm, mean_u_hbm, mean_v_hbm))
    ]
    for copy in plane_copies:
        copy.start()

    to_force = baroclinic_step / barotropic_step

    def rest(n, rows, lanes):
        return state[2 + n, rows, lanes] * (1.0 / SUBSTEPS) - to_force * fixed[3 + n, rows, lanes]

    main, beside = slice(0, COLS), slice(COLS, WIDE)
    lane = lane_index((ROWS, COLS))
    row = row_index((ROWS, COLS))
    is_e, is_w = lane == COLS - 1, lane == 0
    is_n, is_s = row == ROWS - 1, row == 0
    is_edge = is_e | is_w
    base_u = rest(0, inner, main) - flat[3]
    base_v = rest(1, inner, main) - flat[4]
    side_u = rest(0, inner, beside)
    rest_e = jnp.sum(jnp.where(is_w, side_u, 0.0), axis=1, keepdims=True)
    rest_w = jnp.sum(jnp.where(is_e, side_u, 0.0), axis=1, keepdims=True)
    pair_flux = edges[1] + edges[2] * jnp.where(lane % 2 == 0, rest_e, rest_w)
    pair_fix = edges[0]
    rest_n = rest(1, slice(HALO + ROWS, HALO + ROWS + 1), main)
    rest_s = rest(1, slice(HALO - 1, HALO), main)
    for side, line in ((0, rest_n), (3, rest_s)):
        seam_rows[side + 1, :LAYERS, :] = seam_rows[side + 1, :LAYERS, :] + seam_rows[side + 2, :LAYERS, :] * line
    levels = jnp.where(floor[0] > 0, floor[1], 0)
    copies = []
    for k in range(LAYERS):
        w = weight[k]
        mask = levels > k
        shift = COLS - 1 - PAIR_LANE - 2 * k
        fix_u = jnp.where(is_edge, roll(pair_fix, shift, 1), 0.0)
        fix_v = jnp.where(is_n, seam_rows[0, k : k + 1, :], jnp.where(is_s, seam_rows[3, k : k + 1, :], 0.0))
        out_u = jnp.where(mask, tail_u[k] + base_u + fix_u, 0.0)
        out_v = jnp.where(mask, tail_v[k] + base_v + fix_v, 0.0)
        new_u[k] = out_u
        new_v[k] = out_v
        flux_u, flux_v = w * out_u, w * out_v
        halo = roll(pair_flux, shift, 1)
        east = jnp.where(is_e, halo, pltpu.roll(flux_u, COLS - 1, 1))
        west = jnp.where(is_w, halo, pltpu.roll(flux_u, 1, 1))
        north = jnp.where(is_n, seam_rows[1, k : k + 1, :], pltpu.roll(flux_v, ROWS - 1, 0))
        south = jnp.where(is_s, seam_rows[4, k : k + 1, :], pltpu.roll(flux_v, 1, 0))
        new_th[k] = th[k] - half * ((east - west) + (north - south))
        for n, (held, out) in enumerate(((new_u, new_u_hbm), (new_v, new_v_hbm), (new_th, new_th_hbm))):
            copy = pltpu.make_async_copy(held.at[k], out.at[k], sems.at[n, k])
            copy.start()
            copies.append(copy)
    for copy in copies + plane_copies:
        copy.wait()


def vmem(count):
    return [pl.BlockSpec(memory_space=pltpu.VMEM)] * count


def hbm(count):
    return [pl.BlockSpec(memory_space=pltpu.HBM)] * count


def in_hbm(*arrays):
    return tuple(pltpu.with_memory_space_constraint(x, pltpu.HBM) for x in arrays)


def f32(*shape):
    return jax.ShapeDtypeStruct(shape, jnp.float32)


PARAMS = pltpu.CompilerParams(vmem_limit_bytes=40 * 2**20)


def local(lu, lv, th, lev, u, v, land, bottom, fold_map, gravity):
    lons, lats = lax.axis_size("lon"), lax.axis_size("lat")
    lon_msg, lat_msg = f32(LON_ROWS, COLS), f32(LAT_ROWS, COLS)
    layers, plane = f32(LAYERS, ROWS, COLS), f32(ROWS, COLS)
    held = pltpu.VMEM((LAYERS, ROWS, COLS), jnp.float32)
    total = lons * COLS
    pivot = fold_map[0] + lax.axis_index("lon") * COLS
    shift = jnp.mod(pivot - COLS // 2, total) // COLS

    msg_a, msg_b, flat, cor, g_rows, tail_u, tail_v, weight, th, floor = pl.pallas_call(
        first_kernel,
        out_shape=(
            lon_msg, lon_msg, f32(8, ROWS, COLS), f32(FULL, COLS), f32(16, COLS), layers, layers, layers, layers,
            jax.ShapeDtypeStruct((2, ROWS, COLS), jnp.int32),
        ),
        in_specs=hbm(10),
        out_specs=vmem(10),
        scratch_shapes=[
            held,
            held,
            pltpu.SMEM((LAYERS,), jnp.float32),
            pltpu.SMEM((COLS,), jnp.int32),
            pltpu.SemaphoreType.DMA((10,)),
        ],
        compiler_params=PARAMS,
        name="edges",
    )(*in_hbm(gravity, lu, lv, th, lev, u, v, land, bottom, fold_map))

    got_a = lax.ppermute(msg_a, "lon", [(i, i ^ 1) for i in range(lons)])
    got_b = lax.ppermute(msg_b, "lon", [(i, (((i + 1) ^ 1) - 1) % lons) for i in range(lons)])
    got_a, got_b, shift = lax.optimization_barrier((got_a, got_b, shift))

    ext, edges, msg_x, msg_y, msg_f = pl.pallas_call(
        second_kernel,
        out_shape=(f32(6, ROWS, WIDE), f32(3, ROWS, COLS), lat_msg, lat_msg, lat_msg),
        in_specs=vmem(6),
        out_specs=vmem(5),
        compiler_params=PARAMS,
        name="extend",
    )(g_rows, flat, msg_a, msg_b, got_a, got_b)

    got_x = lax.ppermute(msg_x, "lat", [(i, i ^ 1) for i in range(lats)])
    got_y = lax.ppermute(msg_y, "lat", [(i, ((i + 1) ^ 1) - 1) for i in range(1, lats - 1)])
    top = lats - 1

    def mirrored(q):
        pairs = [(((q - b) % lons) * lats + top, b * lats + top) for b in range(lons)]
        return lambda x: lax.ppermute(x, ("lon", "lat"), pairs)

    got_f = lax.switch(shift, [mirrored(q) for q in range(lons)], msg_f)

    padded = pltpu.VMEM((FULL + 16, WIDE), jnp.float32)
    rows16 = pltpu.VMEM((6, 16, COLS), jnp.float32)
    return pl.pallas_call(
        third_kernel,
        out_shape=(layers, layers, layers, plane, plane, plane),
        in_specs=vmem(14) + hbm(1),
        out_specs=hbm(6),
        scratch_shapes=[
            pltpu.VMEM((LAT_ROWS, COLS), jnp.float32),
            padded,
            padded,
            pltpu.VMEM((4, FULL, WIDE), jnp.float32),
            pltpu.VMEM((7, FULL, WIDE), jnp.float32),
            rows16,
            pltpu.VMEM((2, 16, WIDE), jnp.float32),
            rows16,
            held,
            held,
            held,
            pltpu.VMEM((3, ROWS, COLS), jnp.float32),
            pltpu.SemaphoreType.DMA((3, LAYERS)),
            pltpu.SemaphoreType.DMA((3,)),
            pltpu.SemaphoreType.DMA((1,)),
        ],
        compiler_params=PARAMS,
        name="advance",
    )(g_rows, tail_u, tail_v, weight, th, floor, flat, cor, edges, ext, msg_x, msg_y, got_x, got_y, *in_hbm(got_f))


def solution(mesh):
    layered, plane = P(None, "lat", "lon"), P("lat", "lon")
    return jax.shard_map(
        local,
        mesh=mesh,
        in_specs=(layered,) * 3 + (plane,) * 5 + (P("lon"), P()),
        out_specs=(layered,) * 3 + (plane,) * 3,
        check_vma=False,
    )
```

```python
import jax
import jax.numpy as jnp
from jax import lax
from jax.experimental import pallas as pl
from jax.experimental.pallas import tpu as pltpu
from jax.sharding import PartitionSpec as P

SUBSTEPS = 8
LAYERS = 12
TOTAL_ROWS = 512
ROWS, COLS = 64, 128
HALO = 16

barotropic_step = 0.45
baroclinic_step = 0.1
coriolis_scale = 0.3
bottom_drag = 0.05

PAIR_LANE, EAST_PAIR_LANE = 96, 80
PAIR_END = PAIR_LANE + 2 * LAYERS
TOP_ROW, W_TOP, C_TOP, V_TOP, W_BOTTOM, LON_ROWS = 64, 112, 124, 136, 137, 152
V_BOTTOM = LAYERS
LAT_W, LAT_C, LAT_V, LAT_SIDE, LAT_ROWS = 96, 108, 120, 128, 160
FULL = ROWS + 2 * HALO
WIDE = 2 * COLS
half = 0.5 * baroclinic_step


def lane_index(shape):
    return lax.broadcasted_iota(jnp.int32, shape, 1)


def row_index(shape):
    return lax.broadcasted_iota(jnp.int32, shape, 0)


def roll(x, shift, axis):
    shift = shift % x.shape[axis]
    return x if shift == 0 else pltpu.roll(x, shift, axis)


def first_kernel(
    gravity_hbm, lu_hbm, lv_hbm, th_hbm, lev_hbm, u_hbm, v_hbm, land_hbm, bottom_hbm, fold_hbm,
    msg_a, msg_b, own_pairs, own_rows, flat, cor_out, g_rows, tail_u, tail_v, weight, th, floor,
    lu, lv, gravity, fold, sems,
):
    pairs = (
        (th_hbm, th), (land_hbm, floor.at[0]), (bottom_hbm, floor.at[1]), (gravity_hbm, gravity), (lu_hbm, lu),
        (lv_hbm, lv), (lev_hbm, flat.at[5]), (u_hbm, flat.at[6]), (v_hbm, flat.at[7]),
        (fold_hbm, fold),
    )
    copies = [pltpu.make_async_copy(a, b, sems.at[n]) for n, (a, b) in enumerate(pairs)]
    for copy in copies:
        copy.start()
    lon, lat = lax.axis_index("lon"), lax.axis_index("lat")
    even = lax.rem(lon, 2) == 0
    rows = (row_index((FULL, COLS)) + (lat * ROWS - HALO)).astype(jnp.float32)
    cor_all = -coriolis_scale * jnp.cos((rows + 0.5) * (jnp.pi / TOTAL_ROWS))
    cor_out[...] = cor_all
    cor = cor_all[HALO : HALO + ROWS]
    lane = lane_index((ROWS, COLS))
    row = row_index((ROWS, COLS))
    for copy in copies:
        copy.wait()
    wet = floor[0].astype(jnp.float32)
    bot = floor[1]
    lev, u, v = flat[5], flat[6], flat[7]
    zero = jnp.zeros((ROWS, COLS), jnp.float32)
    line = lane_index((1, COLS))
    lanes_g = jnp.zeros((1, COLS), jnp.float32)
    for k in range(LAYERS):
        g_rows[k : k + 1, :] = jnp.full((1, COLS), gravity[k], jnp.float32)
        lanes_g = jnp.where((line - PAIR_LANE) >> 1 == k, gravity[k], lanes_g)
    g_rows[LAYERS : LAYERS + 1, :] = lanes_g
    offset = 64 + ((fold[0] + 64) & (COLS - 1))
    g_rows[LAYERS + 1 : LAYERS + 2, :] = jnp.full((1, COLS), offset, jnp.int32).astype(jnp.float32)

    depth, potential = zero, zero
    grad_u, grad_v, sum_u, sum_v = zero, zero, zero, zero
    for k in range(LAYERS):
        w = jnp.where(bot > k, wet, 0.0) * th[k]
        depth = depth + w
        potential = potential + gravity[k] * depth
        right = jnp.where(lane == COLS - 1, 0.0, roll(potential, -1, 1))
        left = jnp.where(lane == 0, 0.0, roll(potential, 1, 1))
        above = jnp.where(row == ROWS - 1, 0.0, roll(potential, -1, 0))
        below = jnp.where(row == 0, 0.0, roll(potential, 1, 0))
        du = 0.5 * (left - right)
        dv = 0.5 * (below - above)
        grad_u = grad_u + w * du
        grad_v = grad_v + w * dv
        sum_u = sum_u + w * lu[k]
        sum_v = sum_v + w * lv[k]
        rest_u = lu[k] + baroclinic_step * (du + cor * lv[k])
        rest_v = lv[k] + baroclinic_step * (dv - cor * lu[k])
        tail_u[k] = rest_u
        tail_v[k] = rest_v
        weight[k] = w
        for msg in (msg_a, msg_b):
            msg[W_TOP + k : W_TOP + k + 1, :] = w[ROWS - 1 :]
            msg[W_BOTTOM + k : W_BOTTOM + k + 1, :] = w[:1]
            msg[C_TOP + k : C_TOP + k + 1, :] = rest_v[ROWS - 1 :]
        own_rows[k : k + 1, :] = rest_v[:1]
    edge_w, edge_c = zero, zero
    for k in range(LAYERS):
        here = lane >> 1 == k
        edge_w = jnp.where(here, roll(weight[k], 2 * k + 1, 1), edge_w)
        edge_c = jnp.where(here, roll(tail_u[k], 2 * k + 1, 1), edge_c)
    own_pairs[...] = edge_w
    inverse = 1.0 / (depth + (1.0 - wet))
    column_u = sum_u * inverse
    column_v = sum_v * inverse
    force_u = grad_u * inverse + cor * column_v
    force_v = grad_v * inverse - cor * column_u
    fields = (depth, u, v, lev, force_u, force_v)
    flat[0] = depth
    flat[1] = force_u
    flat[2] = force_v
    flat[3] = column_u
    flat[4] = column_v
    transport_u = depth * u
    transport_v = depth * v
    is_odd = lane % 2 == 1
    west, east = zero, zero
    for f, field in enumerate(fields):
        moved = roll(field, HALO * f, 1)
        west = jnp.where(lane // HALO == f, moved, west)
        east = jnp.where(lane // HALO == (f - 1) % 8, moved, east)
    in_west = (lane >= PAIR_LANE) & (lane < PAIR_END)
    in_east = (lane >= EAST_PAIR_LANE) & (lane < EAST_PAIR_LANE + 2 * LAYERS)

    def pairs_of(w, rest, edge):
        column = jnp.sum(jnp.where(lane == edge, column_u, 0.0), axis=1, keepdims=True)
        return jnp.where(is_odd, rest - column, w)

    west = jnp.where(in_west, pairs_of(roll(edge_w, PAIR_LANE - 1, 1), roll(edge_c, PAIR_LANE, 1), 0), west)
    west = jnp.where(lane == PAIR_END, roll(transport_u, PAIR_END - HALO, 1), west)
    at = EAST_PAIR_LANE
    east = jnp.where(in_east, pairs_of(roll(edge_w, at, 1), roll(edge_c, at + 1, 1), COLS - 1), east)
    at = PAIR_END - HALO
    east = jnp.where(lane == at, roll(transport_u, at - (COLS - 1 - HALO), 1), east)
    msg_a[:ROWS] = jnp.where(even, east, west)
    msg_b[:ROWS] = jnp.where(even, west, east)
    low = lane_index((8, COLS)) < 64
    for f, field in enumerate(fields):
        lower, upper = field[ROWS - HALO : ROWS - 8], field[ROWS - 8 :]
        west = jnp.where(low, roll(lower, -16, 1), roll(upper, 48, 1))
        east = jnp.where(low, roll(lower, -48, 1), roll(upper, 16, 1))
        msg_a[TOP_ROW + 8 * f : TOP_ROW + 8 * (f + 1)] = jnp.where(even, east, west)
        msg_b[TOP_ROW + 8 * f : TOP_ROW + 8 * (f + 1)] = jnp.where(even, west, east)
    for msg in (msg_a, msg_b):
        msg[C_TOP : C_TOP + LAYERS] = msg[C_TOP : C_TOP + LAYERS] - column_v[ROWS - 1 :]
        msg[V_TOP : V_TOP + 1] = transport_v[ROWS - 1 - HALO : ROWS - HALO]
        msg[W_BOTTOM + LAYERS :] = jnp.zeros((LON_ROWS - W_BOTTOM - LAYERS, COLS), jnp.float32)
    own_rows[:LAYERS] = own_rows[:LAYERS] - column_v[:1]
    own_rows[V_BOTTOM : V_BOTTOM + 1] = transport_v[HALO : HALO + 1]
    own_rows[V_BOTTOM + 1 :] = jnp.zeros((16 - V_BOTTOM - 1, COLS), jnp.float32)


def lane_prefix(x):
    for shift in (2, 4, 8, 16):
        x = x + pltpu.roll(x, shift, 1)
    return x


def second_kernel(g_rows, flat, own_pairs, own_rows, own_a, got_a, got_b, ext, edges, msg_x, msg_y, msg_f):
    lon, lat = lax.axis_index("lon"), lax.axis_index("lat")
    even_lon = lax.rem(lon, 2) == 0
    even_lat = lax.rem(lat, 2) == 0
    lane = lane_index((ROWS, COLS))
    is_pair = (lane >= PAIR_LANE) & (lane < PAIR_END)
    is_odd = lane % 2 == 1
    sign = jnp.where(is_odd, -1.0, 1.0)
    weights_g = g_rows[LAYERS : LAYERS + 1, :]
    east = jnp.where(even_lon, got_a[:ROWS], got_b[:ROWS])
    west = jnp.where(even_lon, got_b[:ROWS], got_a[:ROWS])

    def potentials(w):
        return lane_prefix(weights_g * lane_prefix(w))

    def dots(x):
        even_sum = jnp.sum(jnp.where(is_odd, 0.0, x), axis=1, keepdims=True)
        odd_sum = jnp.sum(jnp.where(is_odd, x, 0.0), axis=1, keepdims=True)
        return 0.5 * even_sum, 0.5 * odd_sum

    apart = PAIR_LANE - EAST_PAIR_LANE
    w_halo = jnp.where(is_pair, jnp.where(is_odd, roll(west, apart + 1, 1), east), 0.0)
    c_halo = jnp.where(is_odd, roll(west, apart, 1), roll(east, -1, 1))
    w_own = roll(own_pairs[...], PAIR_LANE, 1)
    p_halo, p_own = potentials(w_halo), potentials(w_own)
    edges[0] = (-half * sign) * p_halo
    edges[1] = w_halo * (c_halo + (half * sign) * p_own)
    edges[2] = w_halo

    depth = flat[0]
    safe = depth + jnp.where(depth > 0.0, 0.0, 1.0)
    to_e, to_w = dots(w_own * p_halo)
    force_u = flat[1] + jnp.where(lane == COLS - 1, -to_e, jnp.where(lane == 0, to_w, 0.0)) / safe

    sides = [roll(jnp.where(lane // HALO == f, east, west), -HALO * f, 1) for f in range(6)]
    sides[1] = jnp.where(lane == HALO, roll(east, HALO - PAIR_END, 1), sides[1])
    at = COLS - HALO - 1
    sides[1] = jnp.where(lane == at, roll(west, at - (PAIR_END - HALO), 1), sides[1])
    safe = sides[0] + jnp.where(sides[0] > 0.0, 0.0, 1.0)
    to_e, to_w = dots(w_halo * p_own)
    sides[4] = sides[4] + jnp.where(lane == 0, to_e, jnp.where(lane == COLS - 1, -to_w, 0.0)) / safe
    sides[0] = jnp.where((lane == HALO) | (lane == at), 1.0, sides[0])

    for f, field in enumerate((depth, flat[6], flat[7], flat[5], force_u, flat[2])):
        ext[f, :, :COLS] = field
        ext[f, :, COLS:] = sides[f]

    lane12 = lane_index((LAYERS, COLS))
    lane16 = lane_index((HALO, COLS))

    def lat_message(msg, north):
        start, w_at = (ROWS - HALO, W_TOP) if north else (0, W_BOTTOM)
        edge, c_at, v_at = (own_a, C_TOP, V_TOP) if north else (own_rows, 0, V_BOTTOM)
        packed = [jnp.zeros((HALO, COLS), jnp.float32)] * 2
        for f in range(6):
            msg[HALO * f : HALO * (f + 1), :] = ext[f, start : start + HALO, :COLS]
            side = roll(ext[f, start : start + HALO, COLS:], HALO + 32 * (f % 4), 1)
            packed[f // 4] = jnp.where(lane16 // 32 == f % 4, side, packed[f // 4])
        msg[LAT_SIDE : LAT_SIDE + HALO, :] = packed[0]
        msg[LAT_SIDE + HALO :, :] = packed[1]
        msg[LAT_W : LAT_W + LAYERS, :] = own_a[w_at : w_at + LAYERS, :]
        beside_e = jnp.where(even_lon, got_a[w_at : w_at + LAYERS, :], got_b[w_at : w_at + LAYERS, :])
        beside_w = jnp.where(even_lon, got_b[w_at : w_at + LAYERS, :], got_a[w_at : w_at + LAYERS, :])
        beside = roll(jnp.where(lane12 < HALO, beside_e, beside_w), HALO + 64, 1)
        held = msg[LAT_SIDE + HALO : LAT_SIDE + HALO + LAYERS, :]
        msg[LAT_SIDE + HALO : LAT_SIDE + HALO + LAYERS, :] = jnp.where(lane12 // 32 == 2, beside, held)
        msg[LAT_C : LAT_C + LAYERS, :] = edge[c_at : c_at + LAYERS, :]
        msg[LAT_V : LAT_V + 1, :] = edge[v_at : v_at + 1, :]
        msg[LAT_V + 1 : LAT_SIDE, :] = jnp.zeros((LAT_SIDE - LAT_V - 1, COLS), jnp.float32)

    @pl.when(even_lat)
    def _():
        lat_message(msg_x, True)
        lat_message(msg_y, False)

    @pl.when(jnp.logical_not(even_lat))
    def _():
        lat_message(msg_x, False)
        lat_message(msg_y, True)

    @pl.when(lat == lax.axis_size("lat") - 1)
    def _():
        lane8 = lane_index((8, COLS))
        row8 = row_index((8, COLS))
        offset = jnp.broadcast_to(g_rows[LAYERS + 1 : LAYERS + 2, :].astype(jnp.int32), (8, COLS))
        source = (offset - lane8) & (COLS - 1)
        block = (COLS + offset - lane8) >> 7
        side_block = jnp.where(lane8 < HALO, offset - lane8, 2 * COLS + offset - lane8) >> 7

        def gather(x, index, axis):
            return jnp.take_along_axis(x, index, axis=axis, mode="promise_in_bounds")

        def window(w_tile, o_tile, e_tile):
            a, b, c = gather(w_tile, source, 1), gather(o_tile, source, 1), gather(e_tile, source, 1)
            main = jnp.where(block == 0, a, jnp.where(block == 1, b, c))
            side = jnp.where(side_block == 0, a, jnp.where(side_block == 1, b, c))
            return main, side

        def tiles(at):
            on_e = jnp.where(even_lon, got_a[at : at + 8, :], got_b[at : at + 8, :])
            on_w = jnp.where(even_lon, got_b[at : at + 8, :], got_a[at : at + 8, :])
            return on_w, own_a[at : at + 8, :], on_e

        packed = {}

        def pack(at, group, x):
            x = roll(x, HALO + 32 * group, 1)
            packed[at] = jnp.where(lane8 // 32 == group, x, packed[at]) if at in packed else x

        for f in range(6):
            sign = 1.0 if f in (0, 3) else -1.0
            for t in range(2):
                at = ROWS - 8 * (t + 1)
                mine = ext[f, at : at + 8, :COLS]
                side = ext[f, at : at + 8, COLS:]
                on_w, _, on_e = tiles(TOP_ROW + 8 * f)
                on_e = jnp.where(lane8 < HALO, side, roll(on_e, -48 if t == 0 else 16, 1))
                on_w = jnp.where(lane8 >= COLS - HALO, side, roll(on_w, -16 if t == 0 else 48, 1))
                main, beside = window(on_w, mine, on_e)
                msg_f[HALO * f + 8 * t : HALO * f + 8 * (t + 1), :] = sign * gather(main, 7 - row8, 0)
                pack(LAT_SIDE + HALO * (f // 4) + 8 * t, f % 4, sign * gather(beside, 7 - row8, 0))
        for t in range(3):
            main, beside = window(*tiles(W_TOP + 8 * t))
            sign = jnp.where(row8 + 8 * t < LAYERS, 1.0, -1.0)
            msg_f[LAT_W + 8 * t : LAT_W + 8 * (t + 1), :] = sign * main
            if t < 2:
                pack(LAT_SIDE + HALO + 8 * t, 2, beside)
        main, _ = window(*tiles(V_TOP))
        msg_f[LAT_V : LAT_V + 8, :] = -main
        for at, x in packed.items():
            msg_f[at : at + 8, :] = x

    @pl.when(lat != lax.axis_size("lat") - 1)
    def _():
        msg_f[...] = jnp.zeros((LAT_ROWS, COLS), jnp.float32)


def third_kernel(
    g_rows, tail_u, tail_v, weight, th, floor, flat, cor_ref, edges, ext, own_x, own_y, got_x, got_y, got_f_hbm,
    new_u_hbm, new_v_hbm, new_th_hbm, new_lev_hbm, mean_u_hbm, mean_v_hbm,
    far, level_pad, v_pad, state, fixed, pots, seam_w, seam_rows, new_u, new_v, new_th, planes,
    sems, plane_sems, far_sem,
):
    lat = lax.axis_index("lat")
    even = lax.rem(lat, 2) == 0
    at_top = lat == lax.axis_size("lat") - 1
    at_bottom = lat == 0

    fold_copy = pltpu.make_async_copy(got_f_hbm, far, far_sem.at[0])
    fold_copy.start()
    inner = slice(HALO, HALO + ROWS)

    def place(at, count, depth, u, v, level, force_u, force_v, rate):
        rows = pl.ds(at, count)
        cor = cor_ref[rows, :]
        cor = jnp.concatenate([cor, cor], axis=1)
        wet = jnp.where(depth > 0.0, 1.0, 0.0)
        fixed[0, rows, :] = depth
        fixed[1, rows, :] = wet * (1.0 - barotropic_step * bottom_drag)
        fixed[2, rows, :] = wet * (barotropic_step * cor)
        fixed[3, rows, :] = wet * (barotropic_step * force_u)
        fixed[4, rows, :] = wet * (barotropic_step * force_v)
        fixed[5, rows, :] = wet * (0.5 * barotropic_step)
        fixed[6, rows, :] = jnp.full((count, WIDE), rate, jnp.float32)
        state[0, rows, :] = u
        state[1, rows, :] = v
        level_pad[pl.ds(at + 8, count), :] = level

    place(HALO, ROWS, *(ext[f] for f in range(6)), 0.5 * barotropic_step)

    def strip(got, mine, slot, is_north, keep):
        at = pl.multiple_of(jnp.where(is_north, HALO + ROWS, 0), HALO)
        sign = jnp.where(is_north, 1.0, -1.0)
        fields = []
        for f in range(6):
            main = got[HALO * f : HALO * (f + 1), :]
            side = got[LAT_SIDE + HALO * (f // 4) : LAT_SIDE + HALO * (f // 4 + 1), :]
            side = roll(side, -HALO - 32 * (f % 4), 1)
            fields.append(jnp.concatenate([main, side], axis=1))
        if keep is not None:
            fields = [jnp.where(keep, field, 0.0) for field in fields]
        rate = 0.5 * barotropic_step
        place(at, HALO, *fields, rate if keep is None else jnp.where(keep, rate, 0.0))
        v_row = got[LAT_V : LAT_V + 1, :]
        if keep is not None:
            v_row = jnp.where(keep, v_row, 0.0)
        v_rows = pl.ds(pl.multiple_of(jnp.where(is_north, 8 + FULL, 0), 8), 8)
        v_pad[v_rows, :COLS] = jnp.broadcast_to(v_row, (8, COLS))
        v_pad[v_rows, COLS:] = jnp.zeros((8, COLS), jnp.float32)
        for n, ref in enumerate((mine, got)):
            w = ref[LAT_W : LAT_W + LAYERS, :]
            side = roll(ref[LAT_SIDE + HALO : LAT_SIDE + HALO + LAYERS, :], -HALO - 64, 1)
            if n == 1 and keep is not None:
                w, side = jnp.where(keep, w, 0.0), jnp.where(keep, side, 0.0)
            seam_w[n, :LAYERS, :COLS] = w
            seam_w[n, :LAYERS, COLS:] = side
        sum_o, sum_s, pot_o, pot_s, to_o, to_s = (jnp.zeros((1, WIDE), jnp.float32) for _ in range(6))
        for k in range(LAYERS):
            wo, ws = seam_w[0, k : k + 1, :], seam_w[1, k : k + 1, :]
            g = jnp.concatenate([g_rows[k : k + 1, :]] * 2, axis=1)
            sum_o, sum_s = sum_o + wo, sum_s + ws
            pot_o, pot_s = pot_o + g * sum_o, pot_s + g * sum_s
            to_o = to_o + wo * pot_s
            to_s = to_s + ws * pot_o
            pots[0, k : k + 1, :] = pot_o[:, :COLS]
            pots[1, k : k + 1, :] = pot_s[:, :COLS]
        safe_o = sum_o + jnp.where(sum_o > 0.0, 0.0, 1.0)
        safe_s = sum_s + jnp.where(sum_s > 0.0, 0.0, 1.0)
        scale = 0.5 * barotropic_step * sign
        row8 = row_index((8, WIDE))
        own_rows = pl.ds(pl.multiple_of(jnp.where(is_north, HALO + ROWS - 8, HALO), 8), 8)
        strip_rows = pl.ds(pl.multiple_of(jnp.where(is_north, HALO + ROWS, HALO - 8), 8), 8)
        last, first = row8 == jnp.where(is_north, 7, 0), row8 == jnp.where(is_north, 0, 7)
        fixed[4, own_rows, :] = fixed[4, own_rows, :] - jnp.where(last, scale * to_o / safe_o, 0.0)
        fixed[4, strip_rows, :] = fixed[4, strip_rows, :] + jnp.where(first, scale * to_s / safe_s, 0.0)
        side = jnp.where(is_north, 0, 3)
        w = seam_w[1, :LAYERS, :COLS]
        seam_rows[side, :LAYERS, :] = (-half * sign) * pots[1, :LAYERS, :]
        seam_rows[side + 1, :LAYERS, :] = w * (got[LAT_C : LAT_C + LAYERS, :] + (half * sign) * pots[0, :LAYERS, :])
        seam_rows[side + 2, :LAYERS, :] = w

    strip(got_x, own_x, 0, even, None)
    fold_copy.wait()

    @pl.when(jnp.logical_not(at_top))
    def _():
        far[...] = got_y[...]

    strip(far, own_y, 1, jnp.logical_not(even), jnp.logical_not(at_bottom))

    for step in range(SUBSTEPS):
        depth, u, v = fixed[0], state[0], state[1]
        trans_u = depth * u
        v_pad[8 : 8 + FULL, :] = depth * v
        dv = v_pad[9 : 9 + FULL, :] - v_pad[7 : 7 + FULL, :]
        du = pltpu.roll(trans_u, WIDE - 1, 1) - pltpu.roll(trans_u, 1, 1)
        level = level_pad[8 : 8 + FULL, :] - fixed[6] * (du + dv)
        level_pad[8 : 8 + FULL, :] = level
        dy = level_pad[9 : 9 + FULL, :] - level_pad[7 : 7 + FULL, :]
        dx = pltpu.roll(level, WIDE - 1, 1) - pltpu.roll(level, 1, 1)
        keep, turn, slope = fixed[1], fixed[2], fixed[5]
        next_u = keep * u + turn * v + fixed[3] - slope * dx
        next_v = keep * v - turn * u + fixed[4] - slope * dy
        state[0] = next_u
        state[1] = next_v
        state[2] = next_u if step == 0 else state[2] + next_u
        state[3] = next_v if step == 0 else state[3] + next_v
    planes[0] = level_pad[8 + HALO : 8 + HALO + ROWS, :COLS]
    planes[1] = state[2, inner, :COLS] * (1.0 / SUBSTEPS)
    planes[2] = state[3, inner, :COLS] * (1.0 / SUBSTEPS)
    plane_copies = [
        pltpu.make_async_copy(planes.at[n], out, plane_sems.at[n])
        for n, out in enumerate((new_lev_hbm, mean_u_hbm, mean_v_hbm))
    ]
    for copy in plane_copies:
        copy.start()

    to_force = baroclinic_step / barotropic_step

    def rest(n, rows, lanes):
        return state[2 + n, rows, lanes] * (1.0 / SUBSTEPS) - to_force * fixed[3 + n, rows, lanes]

    main, beside = slice(0, COLS), slice(COLS, WIDE)
    lane = lane_index((ROWS, COLS))
    row = row_index((ROWS, COLS))
    is_e, is_w = lane == COLS - 1, lane == 0
    is_n, is_s = row == ROWS - 1, row == 0
    is_edge = is_e | is_w
    base_u = rest(0, inner, main) - flat[3]
    base_v = rest(1, inner, main) - flat[4]
    side_u = rest(0, inner, beside)
    rest_e = jnp.sum(jnp.where(is_w, side_u, 0.0), axis=1, keepdims=True)
    rest_w = jnp.sum(jnp.where(is_e, side_u, 0.0), axis=1, keepdims=True)
    pair_flux = edges[1] + edges[2] * jnp.where(lane % 2 == 0, rest_e, rest_w)
    pair_fix = edges[0]
    rest_n = rest(1, slice(HALO + ROWS, HALO + ROWS + 1), main)
    rest_s = rest(1, slice(HALO - 1, HALO), main)
    for side, line in ((0, rest_n), (3, rest_s)):
        seam_rows[side + 1, :LAYERS, :] = seam_rows[side + 1, :LAYERS, :] + seam_rows[side + 2, :LAYERS, :] * line
    levels = jnp.where(floor[0] > 0, floor[1], 0)
    copies = []
    parts = ((0, 4), (4, 8), (8, 11), (11, 12))
    for k in range(LAYERS):
        w = weight[k]
        mask = levels > k
        shift = COLS - 1 - PAIR_LANE - 2 * k
        fix_u = jnp.where(is_edge, roll(pair_fix, shift, 1), 0.0)
        fix_v = jnp.where(is_n, seam_rows[0, k : k + 1, :], jnp.where(is_s, seam_rows[3, k : k + 1, :], 0.0))
        out_u = jnp.where(mask, tail_u[k] + base_u + fix_u, 0.0)
        out_v = jnp.where(mask, tail_v[k] + base_v + fix_v, 0.0)
        new_u[k] = out_u
        new_v[k] = out_v
        flux_u, flux_v = w * out_u, w * out_v
        halo = roll(pair_flux, shift, 1)
        east = jnp.where(is_e, halo, pltpu.roll(flux_u, COLS - 1, 1))
        west = jnp.where(is_w, halo, pltpu.roll(flux_u, 1, 1))
        north = jnp.where(is_n, seam_rows[1, k : k + 1, :], pltpu.roll(flux_v, ROWS - 1, 0))
        south = jnp.where(is_s, seam_rows[4, k : k + 1, :], pltpu.roll(flux_v, 1, 0))
        new_th[k] = th[k] - half * ((east - west) + (north - south))
        for part, (begin, end) in enumerate(parts):
            if k == end - 1:
                rows = pl.ds(begin, end - begin)
                for n, (held, out) in enumerate(((new_u, new_u_hbm), (new_v, new_v_hbm), (new_th, new_th_hbm))):
                    copy = pltpu.make_async_copy(held.at[rows], out.at[rows], sems.at[n, part])
                    copy.start()
                    copies.append(copy)
    for copy in copies + plane_copies:
        copy.wait()


def vmem(count):
    return [pl.BlockSpec(memory_space=pltpu.VMEM)] * count


def hbm(count):
    return [pl.BlockSpec(memory_space=pltpu.HBM)] * count


def in_hbm(*arrays):
    return tuple(pltpu.with_memory_space_constraint(x, pltpu.HBM) for x in arrays)


def f32(*shape):
    return jax.ShapeDtypeStruct(shape, jnp.float32)


PARAMS = pltpu.CompilerParams(vmem_limit_bytes=40 * 2**20)


def local(lu, lv, th, lev, u, v, land, bottom, fold_map, gravity):
    lons, lats = lax.axis_size("lon"), lax.axis_size("lat")
    lon_msg, lat_msg = f32(LON_ROWS, COLS), f32(LAT_ROWS, COLS)
    layers, plane = f32(LAYERS, ROWS, COLS), f32(ROWS, COLS)
    held = pltpu.VMEM((LAYERS, ROWS, COLS), jnp.float32)
    total = lons * COLS
    pivot = fold_map[0] + lax.axis_index("lon") * COLS
    shift = jnp.mod(pivot - COLS // 2, total) // COLS

    msg_a, msg_b, own_pairs, own_rows, flat, cor, g_rows, tail_u, tail_v, weight, th, floor = pl.pallas_call(
        first_kernel,
        out_shape=(
            lon_msg, lon_msg, plane, f32(16, COLS), f32(8, ROWS, COLS), f32(FULL, COLS), f32(16, COLS),
            layers, layers, layers, layers,
            jax.ShapeDtypeStruct((2, ROWS, COLS), jnp.int32),
        ),
        in_specs=hbm(10),
        out_specs=vmem(12),
        scratch_shapes=[
            held,
            held,
            pltpu.SMEM((LAYERS,), jnp.float32),
            pltpu.SMEM((COLS,), jnp.int32),
            pltpu.SemaphoreType.DMA((10,)),
        ],
        compiler_params=PARAMS,
        name="edges",
    )(*in_hbm(gravity, lu, lv, th, lev, u, v, land, bottom, fold_map))

    got_a = lax.ppermute(msg_a, "lon", [(i, i ^ 1) for i in range(lons)])
    got_b = lax.ppermute(msg_b, "lon", [(i, (((i + 1) ^ 1) - 1) % lons) for i in range(lons)])
    got_a, got_b, shift = lax.optimization_barrier((got_a, got_b, shift))

    ext, edges, msg_x, msg_y, msg_f = pl.pallas_call(
        second_kernel,
        out_shape=(f32(6, ROWS, WIDE), f32(3, ROWS, COLS), lat_msg, lat_msg, lat_msg),
        in_specs=vmem(7),
        out_specs=vmem(5),
        compiler_params=PARAMS,
        name="extend",
    )(g_rows, flat, own_pairs, own_rows, msg_a, got_a, got_b)

    got_x = lax.ppermute(msg_x, "lat", [(i, i ^ 1) for i in range(lats)])
    got_y = lax.ppermute(msg_y, "lat", [(i, ((i + 1) ^ 1) - 1) for i in range(1, lats - 1)])
    top = lats - 1

    def mirrored(q):
        pairs = [(((q - b) % lons) * lats + top, b * lats + top) for b in range(lons)]
        return lambda x: lax.ppermute(x, ("lon", "lat"), pairs)

    got_f = lax.switch(shift, [mirrored(q) for q in range(lons)], msg_f)

    padded = pltpu.VMEM((FULL + 16, WIDE), jnp.float32)
    rows16 = pltpu.VMEM((6, 16, COLS), jnp.float32)
    return pl.pallas_call(
        third_kernel,
        out_shape=(layers, layers, layers, plane, plane, plane),
        in_specs=vmem(14) + hbm(1),
        out_specs=hbm(6),
        scratch_shapes=[
            pltpu.VMEM((LAT_ROWS, COLS), jnp.float32),
            padded,
            padded,
            pltpu.VMEM((4, FULL, WIDE), jnp.float32),
            pltpu.VMEM((7, FULL, WIDE), jnp.float32),
            rows16,
            pltpu.VMEM((2, 16, WIDE), jnp.float32),
            rows16,
            held,
            held,
            held,
            pltpu.VMEM((3, ROWS, COLS), jnp.float32),
            pltpu.SemaphoreType.DMA((3, 4)),
            pltpu.SemaphoreType.DMA((3,)),
            pltpu.SemaphoreType.DMA((1,)),
        ],
        compiler_params=PARAMS,
        name="advance",
    )(g_rows, tail_u, tail_v, weight, th, floor, flat, cor, edges, ext, msg_x, msg_y, got_x, got_y, *in_hbm(got_f))


def solution(mesh):
    layered, plane = P(None, "lat", "lon"), P("lat", "lon")
    return jax.shard_map(
        local,
        mesh=mesh,
        in_specs=(layered,) * 3 + (plane,) * 5 + (P("lon"), P()),
        out_specs=(layered,) * 3 + (plane,) * 3,
        check_vma=False,
    )
```

```python
import jax
import jax.numpy as jnp
from jax import lax
from jax.experimental import pallas as pl
from jax.experimental.pallas import tpu as pltpu
from jax.sharding import PartitionSpec as P

SUBSTEPS = 8
LAYERS = 12
TOTAL_ROWS = 512
ROWS, COLS = 64, 128
HALO = 16

barotropic_step = 0.45
baroclinic_step = 0.1
coriolis_scale = 0.3
bottom_drag = 0.05

PAIR_LANE, EAST_PAIR_LANE = 96, 80
PAIR_END = PAIR_LANE + 2 * LAYERS
TOP_ROW, W_TOP, C_TOP, V_TOP, W_BOTTOM, LON_ROWS = 64, 112, 124, 136, 137, 152
V_BOTTOM = LAYERS
LAT_W, LAT_C, LAT_V, LAT_SIDE, LAT_ROWS = 96, 108, 120, 128, 160
FULL = ROWS + 2 * HALO
WIDE = 2 * COLS
half = 0.5 * baroclinic_step


def lane_index(shape):
    return lax.broadcasted_iota(jnp.int32, shape, 1)


def row_index(shape):
    return lax.broadcasted_iota(jnp.int32, shape, 0)


def roll(x, shift, axis):
    shift = shift % x.shape[axis]
    return x if shift == 0 else pltpu.roll(x, shift, axis)


def first_kernel(
    gravity_hbm, lu_hbm, lv_hbm, th_hbm, lev_hbm, u_hbm, v_hbm, land_hbm, bottom_hbm, fold_hbm,
    msg_a, msg_b, own_pairs, own_rows, flat, cor_out, g_rows, tail_u, tail_v, weight, th, floor,
    lu, lv, gravity, fold, sems,
):
    pairs = (
        (th_hbm, th), (land_hbm, floor.at[0]), (bottom_hbm, floor.at[1]), (gravity_hbm, gravity), (lu_hbm, lu),
        (lv_hbm, lv), (lev_hbm, flat.at[5]), (u_hbm, flat.at[6]), (v_hbm, flat.at[7]),
        (fold_hbm, fold),
    )
    copies = [pltpu.make_async_copy(a, b, sems.at[n]) for n, (a, b) in enumerate(pairs)]
    for copy in copies:
        copy.start()
    lon, lat = lax.axis_index("lon"), lax.axis_index("lat")
    even = lax.rem(lon, 2) == 0
    rows = (row_index((FULL, COLS)) + (lat * ROWS - HALO)).astype(jnp.float32)
    cor_all = -coriolis_scale * jnp.cos((rows + 0.5) * (jnp.pi / TOTAL_ROWS))
    cor_out[...] = cor_all
    cor = cor_all[HALO : HALO + ROWS]
    lane = lane_index((ROWS, COLS))
    row = row_index((ROWS, COLS))
    for copy in copies:
        copy.wait()
    wet = floor[0].astype(jnp.float32)
    bot = floor[1]
    lev, u, v = flat[5], flat[6], flat[7]
    zero = jnp.zeros((ROWS, COLS), jnp.float32)
    line = lane_index((1, COLS))
    lanes_g = jnp.zeros((1, COLS), jnp.float32)
    for k in range(LAYERS):
        g_rows[k : k + 1, :] = jnp.full((1, COLS), gravity[k], jnp.float32)
        lanes_g = jnp.where((line - PAIR_LANE) >> 1 == k, gravity[k], lanes_g)
    g_rows[LAYERS : LAYERS + 1, :] = lanes_g
    offset = 64 + ((fold[0] + 64) & (COLS - 1))
    g_rows[LAYERS + 1 : LAYERS + 2, :] = jnp.full((1, COLS), offset, jnp.int32).astype(jnp.float32)
    lons = lax.axis_size("lon")
    apart = lax.rem((fold[0] + lons * COLS - 64) // COLS - lon + lons, lons)
    g_rows[LAYERS + 2 : LAYERS + 3, :] = jnp.full((1, COLS), jnp.where(apart == 0, 1.0, 0.0), jnp.float32)
    g_rows[LAYERS + 3 :, :] = jnp.zeros((1, COLS), jnp.float32)

    depth, potential = zero, zero
    grad_u, grad_v, sum_u, sum_v = zero, zero, zero, zero
    for k in range(LAYERS):
        w = jnp.where(bot > k, wet, 0.0) * th[k]
        depth = depth + w
        potential = potential + gravity[k] * depth
        right = jnp.where(lane == COLS - 1, 0.0, roll(potential, -1, 1))
        left = jnp.where(lane == 0, 0.0, roll(potential, 1, 1))
        above = jnp.where(row == ROWS - 1, 0.0, roll(potential, -1, 0))
        below = jnp.where(row == 0, 0.0, roll(potential, 1, 0))
        du = 0.5 * (left - right)
        dv = 0.5 * (below - above)
        grad_u = grad_u + w * du
        grad_v = grad_v + w * dv
        sum_u = sum_u + w * lu[k]
        sum_v = sum_v + w * lv[k]
        rest_u = lu[k] + baroclinic_step * (du + cor * lv[k])
        rest_v = lv[k] + baroclinic_step * (dv - cor * lu[k])
        tail_u[k] = rest_u
        tail_v[k] = rest_v
        weight[k] = w
        for msg in (msg_a, msg_b):
            msg[W_TOP + k : W_TOP + k + 1, :] = w[ROWS - 1 :]
            msg[W_BOTTOM + k : W_BOTTOM + k + 1, :] = w[:1]
            msg[C_TOP + k : C_TOP + k + 1, :] = rest_v[ROWS - 1 :]
        own_rows[k : k + 1, :] = rest_v[:1]
    edge_w, edge_c = zero, zero
    for k in range(LAYERS):
        here = lane >> 1 == k
        edge_w = jnp.where(here, roll(weight[k], 2 * k + 1, 1), edge_w)
        edge_c = jnp.where(here, roll(tail_u[k], 2 * k + 1, 1), edge_c)
    own_pairs[...] = edge_w
    inverse = 1.0 / (depth + (1.0 - wet))
    column_u = sum_u * inverse
    column_v = sum_v * inverse
    force_u = grad_u * inverse + cor * column_v
    force_v = grad_v * inverse - cor * column_u
    fields = (depth, u, v, lev, force_u, force_v)
    flat[0] = depth
    flat[1] = force_u
    flat[2] = force_v
    flat[3] = column_u
    flat[4] = column_v
    transport_u = depth * u
    transport_v = depth * v
    is_odd = lane % 2 == 1
    west, east = zero, zero
    for f, field in enumerate(fields):
        moved = roll(field, HALO * f, 1)
        west = jnp.where(lane // HALO == f, moved, west)
        east = jnp.where(lane // HALO == (f - 1) % 8, moved, east)
    in_west = (lane >= PAIR_LANE) & (lane < PAIR_END)
    in_east = (lane >= EAST_PAIR_LANE) & (lane < EAST_PAIR_LANE + 2 * LAYERS)

    def pairs_of(w, rest, edge):
        column = jnp.sum(jnp.where(lane == edge, column_u, 0.0), axis=1, keepdims=True)
        return jnp.where(is_odd, rest - column, w)

    west = jnp.where(in_west, pairs_of(roll(edge_w, PAIR_LANE - 1, 1), roll(edge_c, PAIR_LANE, 1), 0), west)
    west = jnp.where(lane == PAIR_END, roll(transport_u, PAIR_END - HALO, 1), west)
    at = EAST_PAIR_LANE
    east = jnp.where(in_east, pairs_of(roll(edge_w, at, 1), roll(edge_c, at + 1, 1), COLS - 1), east)
    at = PAIR_END - HALO
    east = jnp.where(lane == at, roll(transport_u, at - (COLS - 1 - HALO), 1), east)
    msg_a[:ROWS] = jnp.where(even, east, west)
    msg_b[:ROWS] = jnp.where(even, west, east)
    low = lane_index((8, COLS)) < 64
    for f, field in enumerate(fields):
        lower, upper = field[ROWS - HALO : ROWS - 8], field[ROWS - 8 :]
        west = jnp.where(low, roll(lower, -16, 1), roll(upper, 48, 1))
        east = jnp.where(low, roll(lower, -48, 1), roll(upper, 16, 1))
        msg_a[TOP_ROW + 8 * f : TOP_ROW + 8 * (f + 1)] = jnp.where(even, east, west)
        msg_b[TOP_ROW + 8 * f : TOP_ROW + 8 * (f + 1)] = jnp.where(even, west, east)
    for msg in (msg_a, msg_b):
        msg[C_TOP : C_TOP + LAYERS] = msg[C_TOP : C_TOP + LAYERS] - column_v[ROWS - 1 :]
        msg[V_TOP : V_TOP + 1] = transport_v[ROWS - 1 - HALO : ROWS - HALO]
        msg[W_BOTTOM + LAYERS :] = jnp.zeros((LON_ROWS - W_BOTTOM - LAYERS, COLS), jnp.float32)
    own_rows[:LAYERS] = own_rows[:LAYERS] - column_v[:1]
    own_rows[V_BOTTOM : V_BOTTOM + 1] = transport_v[HALO : HALO + 1]
    own_rows[V_BOTTOM + 1 :] = jnp.zeros((16 - V_BOTTOM - 1, COLS), jnp.float32)


def lane_prefix(x):
    for shift in (2, 4, 8, 16):
        x = x + pltpu.roll(x, shift, 1)
    return x


def second_kernel(g_rows, flat, own_pairs, own_rows, own_a, got_a, got_b, ext, edges, msg_x, msg_y, msg_f):
    lon, lat = lax.axis_index("lon"), lax.axis_index("lat")
    even_lon = lax.rem(lon, 2) == 0
    even_lat = lax.rem(lat, 2) == 0
    lane = lane_index((ROWS, COLS))
    is_pair = (lane >= PAIR_LANE) & (lane < PAIR_END)
    is_odd = lane % 2 == 1
    sign = jnp.where(is_odd, -1.0, 1.0)
    weights_g = g_rows[LAYERS : LAYERS + 1, :]
    east = jnp.where(even_lon, got_a[:ROWS], got_b[:ROWS])
    west = jnp.where(even_lon, got_b[:ROWS], got_a[:ROWS])

    def potentials(w):
        return lane_prefix(weights_g * lane_prefix(w))

    def dots(x):
        even_sum = jnp.sum(jnp.where(is_odd, 0.0, x), axis=1, keepdims=True)
        odd_sum = jnp.sum(jnp.where(is_odd, x, 0.0), axis=1, keepdims=True)
        return 0.5 * even_sum, 0.5 * odd_sum

    apart = PAIR_LANE - EAST_PAIR_LANE
    w_halo = jnp.where(is_pair, jnp.where(is_odd, roll(west, apart + 1, 1), east), 0.0)
    c_halo = jnp.where(is_odd, roll(west, apart, 1), roll(east, -1, 1))
    w_own = roll(own_pairs[...], PAIR_LANE, 1)
    p_halo, p_own = potentials(w_halo), potentials(w_own)
    edges[0] = (-half * sign) * p_halo
    edges[1] = w_halo * (c_halo + (half * sign) * p_own)
    edges[2] = w_halo

    depth = flat[0]
    safe = depth + jnp.where(depth > 0.0, 0.0, 1.0)
    to_e, to_w = dots(w_own * p_halo)
    force_u = flat[1] + jnp.where(lane == COLS - 1, -to_e, jnp.where(lane == 0, to_w, 0.0)) / safe

    sides = [roll(jnp.where(lane // HALO == f, east, west), -HALO * f, 1) for f in range(6)]
    sides[1] = jnp.where(lane == HALO, roll(east, HALO - PAIR_END, 1), sides[1])
    at = COLS - HALO - 1
    sides[1] = jnp.where(lane == at, roll(west, at - (PAIR_END - HALO), 1), sides[1])
    safe = sides[0] + jnp.where(sides[0] > 0.0, 0.0, 1.0)
    to_e, to_w = dots(w_halo * p_own)
    sides[4] = sides[4] + jnp.where(lane == 0, to_e, jnp.where(lane == COLS - 1, -to_w, 0.0)) / safe
    sides[0] = jnp.where((lane == HALO) | (lane == at), 1.0, sides[0])

    for f, field in enumerate((depth, flat[6], flat[7], flat[5], force_u, flat[2])):
        ext[f, :, :COLS] = field
        ext[f, :, COLS:] = sides[f]

    lane12 = lane_index((LAYERS, COLS))
    lane16 = lane_index((HALO, COLS))

    def lat_message(msg, north):
        start, w_at = (ROWS - HALO, W_TOP) if north else (0, W_BOTTOM)
        edge, c_at, v_at = (own_a, C_TOP, V_TOP) if north else (own_rows, 0, V_BOTTOM)
        packed = [jnp.zeros((HALO, COLS), jnp.float32)] * 2
        for f in range(6):
            msg[HALO * f : HALO * (f + 1), :] = ext[f, start : start + HALO, :COLS]
            side = roll(ext[f, start : start + HALO, COLS:], HALO + 32 * (f % 4), 1)
            packed[f // 4] = jnp.where(lane16 // 32 == f % 4, side, packed[f // 4])
        msg[LAT_SIDE : LAT_SIDE + HALO, :] = packed[0]
        msg[LAT_SIDE + HALO :, :] = packed[1]
        msg[LAT_W : LAT_W + LAYERS, :] = own_a[w_at : w_at + LAYERS, :]
        beside_e = jnp.where(even_lon, got_a[w_at : w_at + LAYERS, :], got_b[w_at : w_at + LAYERS, :])
        beside_w = jnp.where(even_lon, got_b[w_at : w_at + LAYERS, :], got_a[w_at : w_at + LAYERS, :])
        beside = roll(jnp.where(lane12 < HALO, beside_e, beside_w), HALO + 64, 1)
        held = msg[LAT_SIDE + HALO : LAT_SIDE + HALO + LAYERS, :]
        msg[LAT_SIDE + HALO : LAT_SIDE + HALO + LAYERS, :] = jnp.where(lane12 // 32 == 2, beside, held)
        msg[LAT_C : LAT_C + LAYERS, :] = edge[c_at : c_at + LAYERS, :]
        msg[LAT_V : LAT_V + 1, :] = edge[v_at : v_at + 1, :]
        msg[LAT_V + 1 : LAT_SIDE, :] = jnp.zeros((LAT_SIDE - LAT_V - 1, COLS), jnp.float32)

    @pl.when(even_lat)
    def _():
        lat_message(msg_x, True)
        lat_message(msg_y, False)

    @pl.when(jnp.logical_not(even_lat))
    def _():
        lat_message(msg_x, False)
        lat_message(msg_y, True)

    @pl.when(lat == lax.axis_size("lat") - 1)
    def _():
        lane8 = lane_index((8, COLS))
        row8 = row_index((8, COLS))
        offset = jnp.broadcast_to(g_rows[LAYERS + 1 : LAYERS + 2, :].astype(jnp.int32), (8, COLS))
        source = (offset - lane8) & (COLS - 1)
        block = (COLS + offset - lane8) >> 7
        side_block = jnp.where(lane8 < HALO, offset - lane8, 2 * COLS + offset - lane8) >> 7

        def gather(x, index, axis):
            return jnp.take_along_axis(x, index, axis=axis, mode="promise_in_bounds")

        def window(w_tile, o_tile, e_tile):
            a, b, c = gather(w_tile, source, 1), gather(o_tile, source, 1), gather(e_tile, source, 1)
            main = jnp.where(block == 0, a, jnp.where(block == 1, b, c))
            side = jnp.where(side_block == 0, a, jnp.where(side_block == 1, b, c))
            return main, side

        def tiles(at):
            on_e = jnp.where(even_lon, got_a[at : at + 8, :], got_b[at : at + 8, :])
            on_w = jnp.where(even_lon, got_b[at : at + 8, :], got_a[at : at + 8, :])
            return on_w, own_a[at : at + 8, :], on_e

        packed = {}

        def pack(at, group, x):
            x = roll(x, HALO + 32 * group, 1)
            packed[at] = jnp.where(lane8 // 32 == group, x, packed[at]) if at in packed else x

        for f in range(6):
            sign = 1.0 if f in (0, 3) else -1.0
            for t in range(2):
                at = ROWS - 8 * (t + 1)
                mine = ext[f, at : at + 8, :COLS]
                side = ext[f, at : at + 8, COLS:]
                on_w, _, on_e = tiles(TOP_ROW + 8 * f)
                on_e = jnp.where(lane8 < HALO, side, roll(on_e, -48 if t == 0 else 16, 1))
                on_w = jnp.where(lane8 >= COLS - HALO, side, roll(on_w, -16 if t == 0 else 48, 1))
                main, beside = window(on_w, mine, on_e)
                msg_f[HALO * f + 8 * t : HALO * f + 8 * (t + 1), :] = sign * gather(main, 7 - row8, 0)
                pack(LAT_SIDE + HALO * (f // 4) + 8 * t, f % 4, sign * gather(beside, 7 - row8, 0))
        for t in range(3):
            main, beside = window(*tiles(W_TOP + 8 * t))
            sign = jnp.where(row8 + 8 * t < LAYERS, 1.0, -1.0)
            msg_f[LAT_W + 8 * t : LAT_W + 8 * (t + 1), :] = sign * main
            if t < 2:
                pack(LAT_SIDE + HALO + 8 * t, 2, beside)
        main, _ = window(*tiles(V_TOP))
        msg_f[LAT_V : LAT_V + 8, :] = -main
        for at, x in packed.items():
            msg_f[at : at + 8, :] = x

    @pl.when(lat != lax.axis_size("lat") - 1)
    def _():
        msg_f[...] = msg_y[...]


def third_kernel(
    g_rows, tail_u, tail_v, weight, th, floor, flat, cor_ref, edges, ext, own_x, own_y, own_f, got_x, got_f_hbm,
    new_u_hbm, new_v_hbm, new_th_hbm, new_lev_hbm, mean_u_hbm, mean_v_hbm,
    far, level_pad, v_pad, state, fixed, pots, seam_w, seam_rows, new_u, new_v, new_th, planes,
    sems, plane_sems, far_sem,
):
    lat = lax.axis_index("lat")
    even = lax.rem(lat, 2) == 0
    at_top = lat == lax.axis_size("lat") - 1
    at_bottom = lat == 0

    fold_copy = pltpu.make_async_copy(got_f_hbm, far, far_sem.at[0])
    fold_copy.start()
    inner = slice(HALO, HALO + ROWS)

    def place(at, count, depth, u, v, level, force_u, force_v, rate):
        rows = pl.ds(at, count)
        cor = cor_ref[rows, :]
        cor = jnp.concatenate([cor, cor], axis=1)
        wet = jnp.where(depth > 0.0, 1.0, 0.0)
        fixed[0, rows, :] = depth
        fixed[1, rows, :] = wet * (1.0 - barotropic_step * bottom_drag)
        fixed[2, rows, :] = wet * (barotropic_step * cor)
        fixed[3, rows, :] = wet * (barotropic_step * force_u)
        fixed[4, rows, :] = wet * (barotropic_step * force_v)
        fixed[5, rows, :] = wet * (0.5 * barotropic_step)
        fixed[6, rows, :] = jnp.full((count, WIDE), rate, jnp.float32)
        state[0, rows, :] = u
        state[1, rows, :] = v
        level_pad[pl.ds(at + 8, count), :] = level

    place(HALO, ROWS, *(ext[f] for f in range(6)), 0.5 * barotropic_step)

    def strip(got, mine, slot, is_north, keep):
        at = pl.multiple_of(jnp.where(is_north, HALO + ROWS, 0), HALO)
        sign = jnp.where(is_north, 1.0, -1.0)
        fields = []
        for f in range(6):
            main = got[HALO * f : HALO * (f + 1), :]
            side = got[LAT_SIDE + HALO * (f // 4) : LAT_SIDE + HALO * (f // 4 + 1), :]
            side = roll(side, -HALO - 32 * (f % 4), 1)
            fields.append(jnp.concatenate([main, side], axis=1))
        if keep is not None:
            fields = [jnp.where(keep, field, 0.0) for field in fields]
        rate = 0.5 * barotropic_step
        place(at, HALO, *fields, rate if keep is None else jnp.where(keep, rate, 0.0))
        v_row = got[LAT_V : LAT_V + 1, :]
        if keep is not None:
            v_row = jnp.where(keep, v_row, 0.0)
        v_rows = pl.ds(pl.multiple_of(jnp.where(is_north, 8 + FULL, 0), 8), 8)
        v_pad[v_rows, :COLS] = jnp.broadcast_to(v_row, (8, COLS))
        v_pad[v_rows, COLS:] = jnp.zeros((8, COLS), jnp.float32)
        for n, ref in enumerate((mine, got)):
            w = ref[LAT_W : LAT_W + LAYERS, :]
            side = roll(ref[LAT_SIDE + HALO : LAT_SIDE + HALO + LAYERS, :], -HALO - 64, 1)
            if n == 1 and keep is not None:
                w, side = jnp.where(keep, w, 0.0), jnp.where(keep, side, 0.0)
            seam_w[n, :LAYERS, :COLS] = w
            seam_w[n, :LAYERS, COLS:] = side
        sum_o, sum_s, pot_o, pot_s, to_o, to_s = (jnp.zeros((1, WIDE), jnp.float32) for _ in range(6))
        for k in range(LAYERS):
            wo, ws = seam_w[0, k : k + 1, :], seam_w[1, k : k + 1, :]
            g = jnp.concatenate([g_rows[k : k + 1, :]] * 2, axis=1)
            sum_o, sum_s = sum_o + wo, sum_s + ws
            pot_o, pot_s = pot_o + g * sum_o, pot_s + g * sum_s
            to_o = to_o + wo * pot_s
            to_s = to_s + ws * pot_o
            pots[0, k : k + 1, :] = pot_o[:, :COLS]
            pots[1, k : k + 1, :] = pot_s[:, :COLS]
        safe_o = sum_o + jnp.where(sum_o > 0.0, 0.0, 1.0)
        safe_s = sum_s + jnp.where(sum_s > 0.0, 0.0, 1.0)
        scale = 0.5 * barotropic_step * sign
        row8 = row_index((8, WIDE))
        own_rows = pl.ds(pl.multiple_of(jnp.where(is_north, HALO + ROWS - 8, HALO), 8), 8)
        strip_rows = pl.ds(pl.multiple_of(jnp.where(is_north, HALO + ROWS, HALO - 8), 8), 8)
        last, first = row8 == jnp.where(is_north, 7, 0), row8 == jnp.where(is_north, 0, 7)
        fixed[4, own_rows, :] = fixed[4, own_rows, :] - jnp.where(last, scale * to_o / safe_o, 0.0)
        fixed[4, strip_rows, :] = fixed[4, strip_rows, :] + jnp.where(first, scale * to_s / safe_s, 0.0)
        side = jnp.where(is_north, 0, 3)
        w = seam_w[1, :LAYERS, :COLS]
        seam_rows[side, :LAYERS, :] = (-half * sign) * pots[1, :LAYERS, :]
        seam_rows[side + 1, :LAYERS, :] = w * (got[LAT_C : LAT_C + LAYERS, :] + (half * sign) * pots[0, :LAYERS, :])
        seam_rows[side + 2, :LAYERS, :] = w

    strip(got_x, own_x, 0, even, None)
    fold_copy.wait()

    far[...] = jnp.where(at_top & (g_rows[LAYERS + 2 : LAYERS + 3, :] > 0.0), own_f[...], far[...])
    strip(far, own_y, 1, jnp.logical_not(even), jnp.logical_not(at_bottom))

    for step in range(SUBSTEPS):
        depth, u, v = fixed[0], state[0], state[1]
        trans_u = depth * u
        v_pad[8 : 8 + FULL, :] = depth * v
        dv = v_pad[9 : 9 + FULL, :] - v_pad[7 : 7 + FULL, :]
        du = pltpu.roll(trans_u, WIDE - 1, 1) - pltpu.roll(trans_u, 1, 1)
        level = level_pad[8 : 8 + FULL, :] - fixed[6] * (du + dv)
        level_pad[8 : 8 + FULL, :] = level
        dy = level_pad[9 : 9 + FULL, :] - level_pad[7 : 7 + FULL, :]
        dx = pltpu.roll(level, WIDE - 1, 1) - pltpu.roll(level, 1, 1)
        keep, turn, slope = fixed[1], fixed[2], fixed[5]
        next_u = keep * u + turn * v + fixed[3] - slope * dx
        next_v = keep * v - turn * u + fixed[4] - slope * dy
        state[0] = next_u
        state[1] = next_v
        state[2] = next_u if step == 0 else state[2] + next_u
        state[3] = next_v if step == 0 else state[3] + next_v
    planes[0] = level_pad[8 + HALO : 8 + HALO + ROWS, :COLS]
    planes[1] = state[2, inner, :COLS] * (1.0 / SUBSTEPS)
    planes[2] = state[3, inner, :COLS] * (1.0 / SUBSTEPS)
    plane_copies = [
        pltpu.make_async_copy(planes.at[n], out, plane_sems.at[n])
        for n, out in enumerate((new_lev_hbm, mean_u_hbm, mean_v_hbm))
    ]
    for copy in plane_copies:
        copy.start()

    to_force = baroclinic_step / barotropic_step

    def rest(n, rows, lanes):
        return state[2 + n, rows, lanes] * (1.0 / SUBSTEPS) - to_force * fixed[3 + n, rows, lanes]

    main, beside = slice(0, COLS), slice(COLS, WIDE)
    lane = lane_index((ROWS, COLS))
    row = row_index((ROWS, COLS))
    is_e, is_w = lane == COLS - 1, lane == 0
    is_n, is_s = row == ROWS - 1, row == 0
    is_edge = is_e | is_w
    base_u = rest(0, inner, main) - flat[3]
    base_v = rest(1, inner, main) - flat[4]
    side_u = rest(0, inner, beside)
    rest_e = jnp.sum(jnp.where(is_w, side_u, 0.0), axis=1, keepdims=True)
    rest_w = jnp.sum(jnp.where(is_e, side_u, 0.0), axis=1, keepdims=True)
    pair_flux = edges[1] + edges[2] * jnp.where(lane % 2 == 0, rest_e, rest_w)
    pair_fix = edges[0]
    rest_n = rest(1, slice(HALO + ROWS, HALO + ROWS + 1), main)
    rest_s = rest(1, slice(HALO - 1, HALO), main)
    for side, line in ((0, rest_n), (3, rest_s)):
        seam_rows[side + 1, :LAYERS, :] = seam_rows[side + 1, :LAYERS, :] + seam_rows[side + 2, :LAYERS, :] * line
    levels = jnp.where(floor[0] > 0, floor[1], 0)
    copies = []
    parts = ((0, 4), (4, 8), (8, 11), (11, 12))
    for k in range(LAYERS):
        w = weight[k]
        mask = levels > k
        shift = COLS - 1 - PAIR_LANE - 2 * k
        fix_u = jnp.where(is_edge, roll(pair_fix, shift, 1), 0.0)
        fix_v = jnp.where(is_n, seam_rows[0, k : k + 1, :], jnp.where(is_s, seam_rows[3, k : k + 1, :], 0.0))
        out_u = jnp.where(mask, tail_u[k] + base_u + fix_u, 0.0)
        out_v = jnp.where(mask, tail_v[k] + base_v + fix_v, 0.0)
        new_u[k] = out_u
        new_v[k] = out_v
        flux_u, flux_v = w * out_u, w * out_v
        halo = roll(pair_flux, shift, 1)
        east = jnp.where(is_e, halo, pltpu.roll(flux_u, COLS - 1, 1))
        west = jnp.where(is_w, halo, pltpu.roll(flux_u, 1, 1))
        north = jnp.where(is_n, seam_rows[1, k : k + 1, :], pltpu.roll(flux_v, ROWS - 1, 0))
        south = jnp.where(is_s, seam_rows[4, k : k + 1, :], pltpu.roll(flux_v, 1, 0))
        new_th[k] = th[k] - half * ((east - west) + (north - south))
        for part, (begin, end) in enumerate(parts):
            if k == end - 1:
                rows = pl.ds(begin, end - begin)
                for n, (held, out) in enumerate(((new_u, new_u_hbm), (new_v, new_v_hbm), (new_th, new_th_hbm))):
                    copy = pltpu.make_async_copy(held.at[rows], out.at[rows], sems.at[n, part])
                    copy.start()
                    copies.append(copy)
    for copy in copies + plane_copies:
        copy.wait()


def vmem(count):
    return [pl.BlockSpec(memory_space=pltpu.VMEM)] * count


def hbm(count):
    return [pl.BlockSpec(memory_space=pltpu.HBM)] * count


def in_hbm(*arrays):
    return tuple(pltpu.with_memory_space_constraint(x, pltpu.HBM) for x in arrays)


def f32(*shape):
    return jax.ShapeDtypeStruct(shape, jnp.float32)


PARAMS = pltpu.CompilerParams(vmem_limit_bytes=40 * 2**20)


def local(lu, lv, th, lev, u, v, land, bottom, fold_map, gravity):
    lons, lats = lax.axis_size("lon"), lax.axis_size("lat")
    lon_msg, lat_msg = f32(LON_ROWS, COLS), f32(LAT_ROWS, COLS)
    layers, plane = f32(LAYERS, ROWS, COLS), f32(ROWS, COLS)
    held = pltpu.VMEM((LAYERS, ROWS, COLS), jnp.float32)
    total = lons * COLS
    pivot = fold_map[0] + lax.axis_index("lon") * COLS
    shift = jnp.mod(pivot - COLS // 2, total) // COLS

    msg_a, msg_b, own_pairs, own_rows, flat, cor, g_rows, tail_u, tail_v, weight, th, floor = pl.pallas_call(
        first_kernel,
        out_shape=(
            lon_msg, lon_msg, plane, f32(16, COLS), f32(8, ROWS, COLS), f32(FULL, COLS), f32(16, COLS),
            layers, layers, layers, layers,
            jax.ShapeDtypeStruct((2, ROWS, COLS), jnp.int32),
        ),
        in_specs=hbm(10),
        out_specs=vmem(12),
        scratch_shapes=[
            held,
            held,
            pltpu.SMEM((LAYERS,), jnp.float32),
            pltpu.SMEM((COLS,), jnp.int32),
            pltpu.SemaphoreType.DMA((10,)),
        ],
        compiler_params=PARAMS,
        name="edges",
    )(*in_hbm(gravity, lu, lv, th, lev, u, v, land, bottom, fold_map))

    got_a = lax.ppermute(msg_a, "lon", [(i, i ^ 1) for i in range(lons)])
    got_b = lax.ppermute(msg_b, "lon", [(i, (((i + 1) ^ 1) - 1) % lons) for i in range(lons)])
    got_a, got_b, shift = lax.optimization_barrier((got_a, got_b, shift))

    ext, edges, msg_x, msg_y, msg_f = pl.pallas_call(
        second_kernel,
        out_shape=(f32(6, ROWS, WIDE), f32(3, ROWS, COLS), lat_msg, lat_msg, lat_msg),
        in_specs=vmem(7),
        out_specs=vmem(5),
        compiler_params=PARAMS,
        name="extend",
    )(g_rows, flat, own_pairs, own_rows, msg_a, got_a, got_b)

    got_x = lax.ppermute(msg_x, "lat", [(i, i ^ 1) for i in range(lats)])
    top = lats - 1
    rows = [(b * lats + i, b * lats + ((i + 1) ^ 1) - 1) for b in range(lons) for i in range(1, top)]
    rows += [(b * lats, (b ^ 1) * lats) for b in range(lons)]

    def exchange(q):
        pairs = list(rows)
        for b in range(lons):
            source = (q - b) % lons
            source = (b + lons // 2) % lons if source == b else source
            pairs.append((source * lats + top, b * lats + top))
        return lambda x: lax.ppermute(x, ("lon", "lat"), pairs)

    got_f = lax.switch(shift, [exchange(q) for q in range(lons)], msg_f)

    padded = pltpu.VMEM((FULL + 16, WIDE), jnp.float32)
    rows16 = pltpu.VMEM((6, 16, COLS), jnp.float32)
    return pl.pallas_call(
        third_kernel,
        out_shape=(layers, layers, layers, plane, plane, plane),
        in_specs=vmem(14) + hbm(1),
        out_specs=hbm(6),
        scratch_shapes=[
            pltpu.VMEM((LAT_ROWS, COLS), jnp.float32),
            padded,
            padded,
            pltpu.VMEM((4, FULL, WIDE), jnp.float32),
            pltpu.VMEM((7, FULL, WIDE), jnp.float32),
            rows16,
            pltpu.VMEM((2, 16, WIDE), jnp.float32),
            rows16,
            held,
            held,
            held,
            pltpu.VMEM((3, ROWS, COLS), jnp.float32),
            pltpu.SemaphoreType.DMA((3, 4)),
            pltpu.SemaphoreType.DMA((3,)),
            pltpu.SemaphoreType.DMA((1,)),
        ],
        compiler_params=PARAMS,
        name="advance",
    )(g_rows, tail_u, tail_v, weight, th, floor, flat, cor, edges, ext, msg_x, msg_y, msg_f, got_x, *in_hbm(got_f))


def solution(mesh):
    layered, plane = P(None, "lat", "lon"), P("lat", "lon")
    return jax.shard_map(
        local,
        mesh=mesh,
        in_specs=(layered,) * 3 + (plane,) * 5 + (P("lon"), P()),
        out_specs=(layered,) * 3 + (plane,) * 3,
        check_vma=False,
    )
```

```python
import jax
import jax.numpy as jnp
from jax import lax
from jax.experimental import pallas as pl
from jax.experimental.pallas import tpu as pltpu
from jax.sharding import PartitionSpec as P

SUBSTEPS = 8
LAYERS = 12
TOTAL_ROWS = 512
ROWS, COLS = 64, 128
HALO = 16

barotropic_step = 0.45
baroclinic_step = 0.1
coriolis_scale = 0.3
bottom_drag = 0.05

PAIR_LANE, EAST_PAIR_LANE = 96, 80
PAIR_END = PAIR_LANE + 2 * LAYERS
TOP_ROW, W_TOP, C_TOP, V_TOP, W_BOTTOM, LON_ROWS = 64, 112, 124, 136, 137, 152
V_BOTTOM = LAYERS
LAT_W, LAT_C, LAT_V, LAT_SIDE, LAT_ROWS = 96, 108, 120, 128, 160
FULL = ROWS + 2 * HALO
WIDE = 2 * COLS
half = 0.5 * baroclinic_step
FAR_PARTS = 5


def lane_index(shape):
    return lax.broadcasted_iota(jnp.int32, shape, 1)


def row_index(shape):
    return lax.broadcasted_iota(jnp.int32, shape, 0)


def roll(x, shift, axis):
    shift = shift % x.shape[axis]
    return x if shift == 0 else pltpu.roll(x, shift, axis)


def first_kernel(
    gravity_hbm, lu_hbm, lv_hbm, th_hbm, lev_hbm, u_hbm, v_hbm, land_hbm, bottom_hbm, fold_hbm,
    msg_a, msg_b, own_pairs, own_rows, flat, cor_out, g_rows, to_potential, tail_u, tail_v, weight, th, floor,
    lu, lv, gravity, fold, sems,
):
    pairs = (
        (th_hbm, th), (land_hbm, floor.at[0]), (bottom_hbm, floor.at[1]), (gravity_hbm, gravity), (lu_hbm, lu),
        (lv_hbm, lv), (lev_hbm, flat.at[5]), (u_hbm, flat.at[6]), (v_hbm, flat.at[7]),
        (fold_hbm, fold),
    )
    copies = [pltpu.make_async_copy(a, b, sems.at[n]) for n, (a, b) in enumerate(pairs)]
    for copy in copies:
        copy.start()
    lon, lat = lax.axis_index("lon"), lax.axis_index("lat")
    even = lax.rem(lon, 2) == 0
    rows = (row_index((FULL, COLS)) + (lat * ROWS - HALO)).astype(jnp.float32)
    cor_all = -coriolis_scale * jnp.cos((rows + 0.5) * (jnp.pi / TOTAL_ROWS))
    cor_out[...] = cor_all
    cor = cor_all[HALO : HALO + ROWS]
    lane = lane_index((ROWS, COLS))
    row = row_index((ROWS, COLS))
    copies[3].wait()
    line = (lane_index((COLS, COLS)) - PAIR_LANE) >> 1
    at = (row_index((COLS, COLS)) - PAIR_LANE) >> 1
    upper, lower = jnp.zeros((COLS, COLS), jnp.float32), jnp.zeros((COLS, COLS), jnp.float32)
    total = 0.0
    for k in range(LAYERS):
        g_rows[k : k + 1, :] = jnp.full((1, COLS), gravity[k], jnp.float32)
        lower = jnp.where(at == k, total, lower)
        total = total + gravity[k]
        upper = jnp.where(line == k, total, upper)
    used = (at >= 0) & (at <= line) & (line < LAYERS) & (((lane_index((COLS, COLS)) - row_index((COLS, COLS))) & 1) == 0)
    to_potential[...] = jnp.where(used, upper - lower, 0.0)
    for copy in copies[:3] + copies[4:]:
        copy.wait()
    wet = floor[0].astype(jnp.float32)
    bot = floor[1]
    lev, u, v = flat[5], flat[6], flat[7]
    zero = jnp.zeros((ROWS, COLS), jnp.float32)
    g_rows[LAYERS : LAYERS + 1, :] = jnp.zeros((1, COLS), jnp.float32)
    offset = 64 + ((fold[0] + 64) & (COLS - 1))
    g_rows[LAYERS + 1 : LAYERS + 2, :] = jnp.full((1, COLS), offset, jnp.int32).astype(jnp.float32)
    lons = lax.axis_size("lon")
    apart = lax.rem((fold[0] + lons * COLS - 64) // COLS - lon + lons, lons)
    g_rows[LAYERS + 2 : LAYERS + 3, :] = jnp.full((1, COLS), jnp.where(apart == 0, 1.0, 0.0), jnp.float32)
    g_rows[LAYERS + 3 :, :] = jnp.zeros((1, COLS), jnp.float32)

    depth, potential = zero, zero
    grad_u, grad_v, sum_u, sum_v = zero, zero, zero, zero
    for k in range(LAYERS):
        w = jnp.where(bot > k, wet, 0.0) * th[k]
        depth = depth + w
        potential = potential + gravity[k] * depth
        right = jnp.where(lane == COLS - 1, 0.0, roll(potential, -1, 1))
        left = jnp.where(lane == 0, 0.0, roll(potential, 1, 1))
        above = jnp.where(row == ROWS - 1, 0.0, roll(potential, -1, 0))
        below = jnp.where(row == 0, 0.0, roll(potential, 1, 0))
        du = 0.5 * (left - right)
        dv = 0.5 * (below - above)
        grad_u = grad_u + w * du
        grad_v = grad_v + w * dv
        sum_u = sum_u + w * lu[k]
        sum_v = sum_v + w * lv[k]
        rest_u = lu[k] + baroclinic_step * (du + cor * lv[k])
        rest_v = lv[k] + baroclinic_step * (dv - cor * lu[k])
        tail_u[k] = rest_u
        tail_v[k] = rest_v
        weight[k] = w
        for msg in (msg_a, msg_b):
            msg[W_TOP + k : W_TOP + k + 1, :] = w[ROWS - 1 :]
            msg[W_BOTTOM + k : W_BOTTOM + k + 1, :] = w[:1]
            msg[C_TOP + k : C_TOP + k + 1, :] = rest_v[ROWS - 1 :]
        own_rows[k : k + 1, :] = rest_v[:1]
    edge_w, edge_c = zero, zero
    for k in range(LAYERS):
        here = lane >> 1 == k
        edge_w = jnp.where(here, roll(weight[k], 2 * k + 1, 1), edge_w)
        edge_c = jnp.where(here, roll(tail_u[k], 2 * k + 1, 1), edge_c)
    own_pairs[...] = edge_w
    inverse = 1.0 / (depth + (1.0 - wet))
    column_u = sum_u * inverse
    column_v = sum_v * inverse
    force_u = grad_u * inverse + cor * column_v
    force_v = grad_v * inverse - cor * column_u
    fields = (depth, u, v, lev, force_u, force_v)
    flat[0] = depth
    flat[1] = force_u
    flat[2] = force_v
    flat[3] = column_u
    flat[4] = column_v
    transport_u = depth * u
    transport_v = depth * v
    is_odd = lane % 2 == 1
    west, east = zero, zero
    for f, field in enumerate(fields):
        moved = roll(field, HALO * f, 1)
        west = jnp.where(lane // HALO == f, moved, west)
        east = jnp.where(lane // HALO == (f - 1) % 8, moved, east)
    in_west = (lane >= PAIR_LANE) & (lane < PAIR_END)
    in_east = (lane >= EAST_PAIR_LANE) & (lane < EAST_PAIR_LANE + 2 * LAYERS)

    def pairs_of(w, rest, edge):
        column = jnp.sum(jnp.where(lane == edge, column_u, 0.0), axis=1, keepdims=True)
        return jnp.where(is_odd, rest - column, w)

    west = jnp.where(in_west, pairs_of(roll(edge_w, PAIR_LANE - 1, 1), roll(edge_c, PAIR_LANE, 1), 0), west)
    west = jnp.where(lane == PAIR_END, roll(transport_u, PAIR_END - HALO, 1), west)
    at = EAST_PAIR_LANE
    east = jnp.where(in_east, pairs_of(roll(edge_w, at, 1), roll(edge_c, at + 1, 1), COLS - 1), east)
    at = PAIR_END - HALO
    east = jnp.where(lane == at, roll(transport_u, at - (COLS - 1 - HALO), 1), east)
    msg_a[:ROWS] = jnp.where(even, east, west)
    msg_b[:ROWS] = jnp.where(even, west, east)
    low = lane_index((8, COLS)) < 64
    for f, field in enumerate(fields):
        lower, upper = field[ROWS - HALO : ROWS - 8], field[ROWS - 8 :]
        west = jnp.where(low, roll(lower, -16, 1), roll(upper, 48, 1))
        east = jnp.where(low, roll(lower, -48, 1), roll(upper, 16, 1))
        msg_a[TOP_ROW + 8 * f : TOP_ROW + 8 * (f + 1)] = jnp.where(even, east, west)
        msg_b[TOP_ROW + 8 * f : TOP_ROW + 8 * (f + 1)] = jnp.where(even, west, east)
    for msg in (msg_a, msg_b):
        msg[C_TOP : C_TOP + LAYERS] = msg[C_TOP : C_TOP + LAYERS] - column_v[ROWS - 1 :]
        msg[V_TOP : V_TOP + 1] = transport_v[ROWS - 1 - HALO : ROWS - HALO]
        msg[W_BOTTOM + LAYERS :] = jnp.zeros((LON_ROWS - W_BOTTOM - LAYERS, COLS), jnp.float32)
    own_rows[:LAYERS] = own_rows[:LAYERS] - column_v[:1]
    own_rows[V_BOTTOM : V_BOTTOM + 1] = transport_v[HALO : HALO + 1]
    own_rows[V_BOTTOM + 1 :] = jnp.zeros((16 - V_BOTTOM - 1, COLS), jnp.float32)


def second_kernel(g_rows, to_potential, flat, own_pairs, own_rows, own_a, got_a, got_b, ext, edges, msg_x, msg_y, msg_f):
    lon, lat = lax.axis_index("lon"), lax.axis_index("lat")
    even_lon = lax.rem(lon, 2) == 0
    even_lat = lax.rem(lat, 2) == 0
    lane = lane_index((ROWS, COLS))
    is_pair = (lane >= PAIR_LANE) & (lane < PAIR_END)
    is_odd = lane % 2 == 1
    sign = jnp.where(is_odd, -1.0, 1.0)
    east = jnp.where(even_lon, got_a[:ROWS], got_b[:ROWS])
    west = jnp.where(even_lon, got_b[:ROWS], got_a[:ROWS])

    def dots(x):
        even_sum = jnp.sum(jnp.where(is_odd, 0.0, x), axis=1, keepdims=True)
        odd_sum = jnp.sum(jnp.where(is_odd, x, 0.0), axis=1, keepdims=True)
        return 0.5 * even_sum, 0.5 * odd_sum

    apart = PAIR_LANE - EAST_PAIR_LANE
    w_halo = jnp.where(is_pair, jnp.where(is_odd, roll(west, apart + 1, 1), east), 0.0)
    c_halo = jnp.where(is_odd, roll(west, apart, 1), roll(east, -1, 1))
    w_own = roll(own_pairs[...], PAIR_LANE, 1)
    both = jnp.concatenate([w_halo, w_own], axis=0)
    both = jnp.dot(both, to_potential[...], precision=lax.Precision.HIGHEST, preferred_element_type=jnp.float32)
    p_halo, p_own = both[:ROWS], both[ROWS:]
    edges[0] = (-half * sign) * p_halo
    edges[1] = w_halo * (c_halo + (half * sign) * p_own)
    edges[2] = w_halo

    depth = flat[0]
    safe = depth + jnp.where(depth > 0.0, 0.0, 1.0)
    to_e, to_w = dots(w_own * p_halo)
    force_u = flat[1] + jnp.where(lane == COLS - 1, -to_e, jnp.where(lane == 0, to_w, 0.0)) / safe

    sides = [roll(jnp.where(lane // HALO == f, east, west), -HALO * f, 1) for f in range(6)]
    sides[1] = jnp.where(lane == HALO, roll(east, HALO - PAIR_END, 1), sides[1])
    at = COLS - HALO - 1
    sides[1] = jnp.where(lane == at, roll(west, at - (PAIR_END - HALO), 1), sides[1])
    safe = sides[0] + jnp.where(sides[0] > 0.0, 0.0, 1.0)
    to_e, to_w = dots(w_halo * p_own)
    sides[4] = sides[4] + jnp.where(lane == 0, to_e, jnp.where(lane == COLS - 1, -to_w, 0.0)) / safe
    sides[0] = jnp.where((lane == HALO) | (lane == at), 1.0, sides[0])

    for f, field in enumerate((depth, flat[6], flat[7], flat[5], force_u, flat[2])):
        ext[f, :, :COLS] = field
        ext[f, :, COLS:] = sides[f]

    lane12 = lane_index((LAYERS, COLS))
    lane16 = lane_index((HALO, COLS))

    def lat_message(msg, north):
        start, w_at = (ROWS - HALO, W_TOP) if north else (0, W_BOTTOM)
        edge, c_at, v_at = (own_a, C_TOP, V_TOP) if north else (own_rows, 0, V_BOTTOM)
        packed = [jnp.zeros((HALO, COLS), jnp.float32)] * 2
        for f in range(6):
            msg[HALO * f : HALO * (f + 1), :] = ext[f, start : start + HALO, :COLS]
            side = roll(ext[f, start : start + HALO, COLS:], HALO + 32 * (f % 4), 1)
            packed[f // 4] = jnp.where(lane16 // 32 == f % 4, side, packed[f // 4])
        msg[LAT_SIDE : LAT_SIDE + HALO, :] = packed[0]
        msg[LAT_SIDE + HALO :, :] = packed[1]
        msg[LAT_W : LAT_W + LAYERS, :] = own_a[w_at : w_at + LAYERS, :]
        beside_e = jnp.where(even_lon, got_a[w_at : w_at + LAYERS, :], got_b[w_at : w_at + LAYERS, :])
        beside_w = jnp.where(even_lon, got_b[w_at : w_at + LAYERS, :], got_a[w_at : w_at + LAYERS, :])
        beside = roll(jnp.where(lane12 < HALO, beside_e, beside_w), HALO + 64, 1)
        held = msg[LAT_SIDE + HALO : LAT_SIDE + HALO + LAYERS, :]
        msg[LAT_SIDE + HALO : LAT_SIDE + HALO + LAYERS, :] = jnp.where(lane12 // 32 == 2, beside, held)
        msg[LAT_C : LAT_C + LAYERS, :] = edge[c_at : c_at + LAYERS, :]
        msg[LAT_V : LAT_V + 1, :] = edge[v_at : v_at + 1, :]
        msg[LAT_V + 1 : LAT_SIDE, :] = jnp.zeros((LAT_SIDE - LAT_V - 1, COLS), jnp.float32)

    @pl.when(even_lat)
    def _():
        lat_message(msg_x, True)
        lat_message(msg_y, False)

    @pl.when(jnp.logical_not(even_lat))
    def _():
        lat_message(msg_x, False)
        lat_message(msg_y, True)


    @pl.when(lat == lax.axis_size("lat") - 1)
    def _():
        lane8 = lane_index((8, COLS))
        row8 = row_index((8, COLS))
        offset = jnp.broadcast_to(g_rows[LAYERS + 1 : LAYERS + 2, :].astype(jnp.int32), (8, COLS))
        source = (offset - lane8) & (COLS - 1)
        taker = source
        block = (COLS + offset - taker) >> 7
        side_block = jnp.where(taker < HALO, offset - taker, 2 * COLS + offset - taker) >> 7

        def gather(x, index, axis):
            return jnp.take_along_axis(x, index, axis=axis, mode="promise_in_bounds")

        def window(w_tile, o_tile, e_tile):
            main = jnp.where(block == 0, w_tile, jnp.where(block == 1, o_tile, e_tile))
            side = jnp.where(side_block == 0, w_tile, jnp.where(side_block == 1, o_tile, e_tile))
            return gather(main, source, 1), gather(side, source, 1)

        def tiles(at):
            on_e = jnp.where(even_lon, got_a[at : at + 8, :], got_b[at : at + 8, :])
            on_w = jnp.where(even_lon, got_b[at : at + 8, :], got_a[at : at + 8, :])
            return on_w, own_a[at : at + 8, :], on_e

        packed = {}

        def pack(at, group, x):
            x = roll(x, HALO + 32 * group, 1)
            packed[at] = jnp.where(lane8 // 32 == group, x, packed[at]) if at in packed else x

        for f in range(6):
            sign = 1.0 if f in (0, 3) else -1.0
            for t in range(2):
                at = ROWS - 8 * (t + 1)
                mine = ext[f, at : at + 8, :COLS]
                side = ext[f, at : at + 8, COLS:]
                on_w, _, on_e = tiles(TOP_ROW + 8 * f)
                on_e = jnp.where(lane8 < HALO, side, roll(on_e, -48 if t == 0 else 16, 1))
                on_w = jnp.where(lane8 >= COLS - HALO, side, roll(on_w, -16 if t == 0 else 48, 1))
                main, beside = window(on_w, mine, on_e)
                msg_f[HALO * f + 8 * t : HALO * f + 8 * (t + 1), :] = sign * gather(main, 7 - row8, 0)
                pack(LAT_SIDE + HALO * (f // 4) + 8 * t, f % 4, sign * gather(beside, 7 - row8, 0))
        for t in range(3):
            main, beside = window(*tiles(W_TOP + 8 * t))
            sign = jnp.where(row8 + 8 * t < LAYERS, 1.0, -1.0)
            msg_f[LAT_W + 8 * t : LAT_W + 8 * (t + 1), :] = sign * main
            if t < 2:
                pack(LAT_SIDE + HALO + 8 * t, 2, beside)
        main, _ = window(*tiles(V_TOP))
        msg_f[LAT_V : LAT_V + 8, :] = -main
        for at, x in packed.items():
            msg_f[at : at + 8, :] = x

    @pl.when(lat != lax.axis_size("lat") - 1)
    def _():
        msg_f[...] = msg_y[...]


def third_kernel(
    g_rows, tail_u, tail_v, weight, th, floor, flat, cor_ref, edges, ext, own_x, own_y, own_f, got_x, got_f_hbm,
    new_u_hbm, new_v_hbm, new_th_hbm, new_lev_hbm, mean_u_hbm, mean_v_hbm,
    far, level_pad, v_pad, state, fixed, pots, seam_w, seam_rows, new_u, new_v, new_th, planes,
    sems, plane_sems, far_sem,
):
    lat = lax.axis_index("lat")
    even = lax.rem(lat, 2) == 0
    at_top = lat == lax.axis_size("lat") - 1
    at_bottom = lat == 0

    far_copies = []
    for n in range(FAR_PARTS):
        part = pl.ds(n * (LAT_ROWS // FAR_PARTS), LAT_ROWS // FAR_PARTS)
        far_copies.append(pltpu.make_async_copy(got_f_hbm.at[part], far.at[part], far_sem.at[n]))
    for copy in far_copies:
        copy.start()
    inner = slice(HALO, HALO + ROWS)

    def place(at, count, depth, u, v, level, force_u, force_v, rate):
        rows = pl.ds(at, count)
        cor = cor_ref[rows, :]
        cor = jnp.concatenate([cor, cor], axis=1)
        wet = jnp.where(depth > 0.0, 1.0, 0.0)
        fixed[0, rows, :] = depth
        fixed[1, rows, :] = wet * (1.0 - barotropic_step * bottom_drag)
        fixed[2, rows, :] = wet * (barotropic_step * cor)
        fixed[3, rows, :] = wet * (barotropic_step * force_u)
        fixed[4, rows, :] = wet * (barotropic_step * force_v)
        fixed[5, rows, :] = wet * (0.5 * barotropic_step)
        fixed[6, rows, :] = jnp.full((count, WIDE), rate, jnp.float32)
        state[0, rows, :] = u
        state[1, rows, :] = v
        level_pad[pl.ds(at + 8, count), :] = level

    place(HALO, ROWS, *(ext[f] for f in range(6)), 0.5 * barotropic_step)

    def strip(got, mine, slot, is_north, keep):
        at = pl.multiple_of(jnp.where(is_north, HALO + ROWS, 0), HALO)
        sign = jnp.where(is_north, 1.0, -1.0)
        fields = []
        for f in range(6):
            main = got[HALO * f : HALO * (f + 1), :]
            side = got[LAT_SIDE + HALO * (f // 4) : LAT_SIDE + HALO * (f // 4 + 1), :]
            side = roll(side, -HALO - 32 * (f % 4), 1)
            fields.append(jnp.concatenate([main, side], axis=1))
        if keep is not None:
            fields = [jnp.where(keep, field, 0.0) for field in fields]
        rate = 0.5 * barotropic_step
        place(at, HALO, *fields, rate if keep is None else jnp.where(keep, rate, 0.0))
        v_row = got[LAT_V : LAT_V + 1, :]
        if keep is not None:
            v_row = jnp.where(keep, v_row, 0.0)
        v_rows = pl.ds(pl.multiple_of(jnp.where(is_north, 8 + FULL, 0), 8), 8)
        v_pad[v_rows, :COLS] = jnp.broadcast_to(v_row, (8, COLS))
        v_pad[v_rows, COLS:] = jnp.zeros((8, COLS), jnp.float32)
        for n, ref in enumerate((mine, got)):
            w = ref[LAT_W : LAT_W + LAYERS, :]
            side = roll(ref[LAT_SIDE + HALO : LAT_SIDE + HALO + LAYERS, :], -HALO - 64, 1)
            if n == 1 and keep is not None:
                w, side = jnp.where(keep, w, 0.0), jnp.where(keep, side, 0.0)
            seam_w[n, :LAYERS, :COLS] = w
            seam_w[n, :LAYERS, COLS:] = side
        sum_o, sum_s, pot_o, pot_s, to_o, to_s = (jnp.zeros((1, WIDE), jnp.float32) for _ in range(6))
        for k in range(LAYERS):
            wo, ws = seam_w[0, k : k + 1, :], seam_w[1, k : k + 1, :]
            g = jnp.concatenate([g_rows[k : k + 1, :]] * 2, axis=1)
            sum_o, sum_s = sum_o + wo, sum_s + ws
            pot_o, pot_s = pot_o + g * sum_o, pot_s + g * sum_s
            to_o = to_o + wo * pot_s
            to_s = to_s + ws * pot_o
            pots[0, k : k + 1, :] = pot_o[:, :COLS]
            pots[1, k : k + 1, :] = pot_s[:, :COLS]
        safe_o = sum_o + jnp.where(sum_o > 0.0, 0.0, 1.0)
        safe_s = sum_s + jnp.where(sum_s > 0.0, 0.0, 1.0)
        scale = 0.5 * barotropic_step * sign
        row8 = row_index((8, WIDE))
        own_rows = pl.ds(pl.multiple_of(jnp.where(is_north, HALO + ROWS - 8, HALO), 8), 8)
        strip_rows = pl.ds(pl.multiple_of(jnp.where(is_north, HALO + ROWS, HALO - 8), 8), 8)
        last, first = row8 == jnp.where(is_north, 7, 0), row8 == jnp.where(is_north, 0, 7)
        fixed[4, own_rows, :] = fixed[4, own_rows, :] - jnp.where(last, scale * to_o / safe_o, 0.0)
        fixed[4, strip_rows, :] = fixed[4, strip_rows, :] + jnp.where(first, scale * to_s / safe_s, 0.0)
        side = jnp.where(is_north, 0, 3)
        w = seam_w[1, :LAYERS, :COLS]
        seam_rows[side, :LAYERS, :] = (-half * sign) * pots[1, :LAYERS, :]
        seam_rows[side + 1, :LAYERS, :] = w * (got[LAT_C : LAT_C + LAYERS, :] + (half * sign) * pots[0, :LAYERS, :])
        seam_rows[side + 2, :LAYERS, :] = w

    strip(got_x, own_x, 0, even, None)
    for copy in far_copies:
        copy.wait()

    far[...] = jnp.where(at_top & (g_rows[LAYERS + 2 : LAYERS + 3, :] > 0.0), own_f[...], far[...])
    strip(far, own_y, 1, jnp.logical_not(even), jnp.logical_not(at_bottom))

    for step in range(SUBSTEPS):
        skip = (2 * step) // 8 * 8
        count = FULL - 2 * skip
        rows = slice(skip, skip + count)
        depth, u, v = fixed[0, rows, :], state[0, rows, :], state[1, rows, :]
        trans_u = depth * u
        v_pad[8 + skip : 8 + skip + count, :] = depth * v
        dv = v_pad[9 + skip : 9 + skip + count, :] - v_pad[7 + skip : 7 + skip + count, :]
        du = pltpu.roll(trans_u, WIDE - 1, 1) - pltpu.roll(trans_u, 1, 1)
        level = level_pad[8 + skip : 8 + skip + count, :] - fixed[6, rows, :] * (du + dv)
        level_pad[8 + skip : 8 + skip + count, :] = level
        dy = level_pad[9 + skip : 9 + skip + count, :] - level_pad[7 + skip : 7 + skip + count, :]
        dx = pltpu.roll(level, WIDE - 1, 1) - pltpu.roll(level, 1, 1)
        keep, turn, slope = fixed[1, rows, :], fixed[2, rows, :], fixed[5, rows, :]
        next_u = keep * u + turn * v + fixed[3, rows, :] - slope * dx
        next_v = keep * v - turn * u + fixed[4, rows, :] - slope * dy
        state[0, rows, :] = next_u
        state[1, rows, :] = next_v
        state[2, rows, :] = next_u if step == 0 else state[2, rows, :] + next_u
        state[3, rows, :] = next_v if step == 0 else state[3, rows, :] + next_v
    planes[0] = level_pad[8 + HALO : 8 + HALO + ROWS, :COLS]
    planes[1] = state[2, inner, :COLS] * (1.0 / SUBSTEPS)
    planes[2] = state[3, inner, :COLS] * (1.0 / SUBSTEPS)
    plane_copies = [
        pltpu.make_async_copy(planes.at[n], out, plane_sems.at[n])
        for n, out in enumerate((new_lev_hbm, mean_u_hbm, mean_v_hbm))
    ]
    for copy in plane_copies:
        copy.start()

    to_force = baroclinic_step / barotropic_step

    def rest(n, rows, lanes):
        return state[2 + n, rows, lanes] * (1.0 / SUBSTEPS) - to_force * fixed[3 + n, rows, lanes]

    main, beside = slice(0, COLS), slice(COLS, WIDE)
    lane = lane_index((ROWS, COLS))
    row = row_index((ROWS, COLS))
    is_e, is_w = lane == COLS - 1, lane == 0
    is_n, is_s = row == ROWS - 1, row == 0
    is_edge = is_e | is_w
    base_u = rest(0, inner, main) - flat[3]
    base_v = rest(1, inner, main) - flat[4]
    side_u = rest(0, inner, beside)
    rest_e = jnp.sum(jnp.where(is_w, side_u, 0.0), axis=1, keepdims=True)
    rest_w = jnp.sum(jnp.where(is_e, side_u, 0.0), axis=1, keepdims=True)
    pair_flux = edges[1] + edges[2] * jnp.where(lane % 2 == 0, rest_e, rest_w)
    pair_fix = edges[0]
    rest_n = rest(1, slice(HALO + ROWS, HALO + ROWS + 1), main)
    rest_s = rest(1, slice(HALO - 1, HALO), main)
    for side, line in ((0, rest_n), (3, rest_s)):
        seam_rows[side + 1, :LAYERS, :] = seam_rows[side + 1, :LAYERS, :] + seam_rows[side + 2, :LAYERS, :] * line
    levels = jnp.where(floor[0] > 0, floor[1], 0)
    copies = []
    parts = ((0, 4), (4, 8), (8, 11), (11, 12))
    for k in range(LAYERS):
        w = weight[k]
        mask = levels > k
        shift = COLS - 1 - PAIR_LANE - 2 * k
        fix_u = jnp.where(is_edge, roll(pair_fix, shift, 1), 0.0)
        fix_v = jnp.where(is_n, seam_rows[0, k : k + 1, :], jnp.where(is_s, seam_rows[3, k : k + 1, :], 0.0))
        out_u = jnp.where(mask, tail_u[k] + base_u + fix_u, 0.0)
        out_v = jnp.where(mask, tail_v[k] + base_v + fix_v, 0.0)
        new_u[k] = out_u
        new_v[k] = out_v
        flux_u, flux_v = w * out_u, w * out_v
        halo = roll(pair_flux, shift, 1)
        east = jnp.where(is_e, halo, pltpu.roll(flux_u, COLS - 1, 1))
        west = jnp.where(is_w, halo, pltpu.roll(flux_u, 1, 1))
        north = jnp.where(is_n, seam_rows[1, k : k + 1, :], pltpu.roll(flux_v, ROWS - 1, 0))
        south = jnp.where(is_s, seam_rows[4, k : k + 1, :], pltpu.roll(flux_v, 1, 0))
        new_th[k] = th[k] - half * ((east - west) + (north - south))
        for part, (begin, end) in enumerate(parts):
            if k == end - 1:
                rows = pl.ds(begin, end - begin)
                for n, (held, out) in enumerate(((new_u, new_u_hbm), (new_v, new_v_hbm), (new_th, new_th_hbm))):
                    copy = pltpu.make_async_copy(held.at[rows], out.at[rows], sems.at[n, part])
                    copy.start()
                    copies.append(copy)
    for copy in copies + plane_copies:
        copy.wait()


def vmem(count):
    return [pl.BlockSpec(memory_space=pltpu.VMEM)] * count


def hbm(count):
    return [pl.BlockSpec(memory_space=pltpu.HBM)] * count


def in_hbm(*arrays):
    return tuple(pltpu.with_memory_space_constraint(x, pltpu.HBM) for x in arrays)


def f32(*shape):
    return jax.ShapeDtypeStruct(shape, jnp.float32)


PARAMS = pltpu.CompilerParams(vmem_limit_bytes=40 * 2**20)


def local(lu, lv, th, lev, u, v, land, bottom, fold_map, gravity):
    lons, lats = lax.axis_size("lon"), lax.axis_size("lat")
    lon_msg, lat_msg = f32(LON_ROWS, COLS), f32(LAT_ROWS, COLS)
    layers, plane = f32(LAYERS, ROWS, COLS), f32(ROWS, COLS)
    held = pltpu.VMEM((LAYERS, ROWS, COLS), jnp.float32)
    total = lons * COLS
    pivot = fold_map[0] + lax.axis_index("lon") * COLS
    shift = jnp.mod(pivot - COLS // 2, total) // COLS

    msg_a, msg_b, own_pairs, own_rows, flat, cor, g_rows, to_potential, tail_u, tail_v, weight, th, floor = pl.pallas_call(
        first_kernel,
        out_shape=(
            lon_msg, lon_msg, plane, f32(16, COLS), f32(8, ROWS, COLS), f32(FULL, COLS), f32(16, COLS), f32(COLS, COLS),
            layers, layers, layers, layers,
            jax.ShapeDtypeStruct((2, ROWS, COLS), jnp.int32),
        ),
        in_specs=hbm(10),
        out_specs=vmem(13),
        scratch_shapes=[
            held,
            held,
            pltpu.SMEM((LAYERS,), jnp.float32),
            pltpu.SMEM((COLS,), jnp.int32),
            pltpu.SemaphoreType.DMA((10,)),
        ],
        compiler_params=PARAMS,
        name="edges",
    )(*in_hbm(gravity, lu, lv, th, lev, u, v, land, bottom, fold_map))

    got_a = lax.ppermute(msg_a, "lon", [(i, i ^ 1) for i in range(lons)])
    got_b = lax.ppermute(msg_b, "lon", [(i, (((i + 1) ^ 1) - 1) % lons) for i in range(lons)])
    got_a, got_b, shift = lax.optimization_barrier((got_a, got_b, shift))

    ext, edges, msg_x, msg_y, msg_f = pl.pallas_call(
        second_kernel,
        out_shape=(f32(6, ROWS, WIDE), f32(3, ROWS, COLS), lat_msg, lat_msg, lat_msg),
        in_specs=vmem(8),
        out_specs=vmem(5),
        compiler_params=PARAMS,
        name="extend",
    )(g_rows, to_potential, flat, own_pairs, own_rows, msg_a, got_a, got_b)

    got_x = lax.ppermute(msg_x, "lat", [(i, i ^ 1) for i in range(lats)])
    top = lats - 1
    rows = [(b * lats + i, b * lats + ((i + 1) ^ 1) - 1) for b in range(lons) for i in range(1, top)]
    rows += [(b * lats, (b ^ 1) * lats) for b in range(lons)]

    def exchange(q):
        pairs = list(rows)
        for b in range(lons):
            source = (q - b) % lons
            source = (b + lons // 2) % lons if source == b else source
            pairs.append((source * lats + top, b * lats + top))
        return lambda x: lax.ppermute(x, ("lon", "lat"), pairs)

    got_f = lax.switch(shift, [exchange(q) for q in range(lons)], msg_f)

    padded = pltpu.VMEM((FULL + 16, WIDE), jnp.float32)
    rows16 = pltpu.VMEM((6, 16, COLS), jnp.float32)
    return pl.pallas_call(
        third_kernel,
        out_shape=(layers, layers, layers, plane, plane, plane),
        in_specs=vmem(14) + hbm(1),
        out_specs=hbm(6),
        scratch_shapes=[
            pltpu.VMEM((LAT_ROWS, COLS), jnp.float32),
            padded,
            padded,
            pltpu.VMEM((4, FULL, WIDE), jnp.float32),
            pltpu.VMEM((7, FULL, WIDE), jnp.float32),
            rows16,
            pltpu.VMEM((2, 16, WIDE), jnp.float32),
            rows16,
            held,
            held,
            held,
            pltpu.VMEM((3, ROWS, COLS), jnp.float32),
            pltpu.SemaphoreType.DMA((3, 4)),
            pltpu.SemaphoreType.DMA((3,)),
            pltpu.SemaphoreType.DMA((FAR_PARTS,)),
        ],
        compiler_params=PARAMS,
        name="advance",
    )(g_rows, tail_u, tail_v, weight, th, floor, flat, cor, edges, ext, msg_x, msg_y, msg_f, got_x, *in_hbm(got_f))


def solution(mesh):
    layered, plane = P(None, "lat", "lon"), P("lat", "lon")
    return jax.shard_map(
        local,
        mesh=mesh,
        in_specs=(layered,) * 3 + (plane,) * 5 + (P("lon"), P()),
        out_specs=(layered,) * 3 + (plane,) * 3,
        check_vma=False,
    )
```

```python
import jax
import jax.numpy as jnp
from jax import lax
from jax.experimental import pallas as pl
from jax.experimental.pallas import tpu as pltpu
from jax.sharding import PartitionSpec as P

SUBSTEPS = 8
LAYERS = 12
TOTAL_ROWS = 512
ROWS, COLS = 64, 128
HALO = 16

barotropic_step = 0.45
baroclinic_step = 0.1
coriolis_scale = 0.3
bottom_drag = 0.05

PAIR_LANE, EAST_PAIR_LANE = 96, 80
PAIR_END = PAIR_LANE + 2 * LAYERS
TOP_ROW, W_TOP, C_TOP, V_TOP, W_BOTTOM, LON_ROWS = 64, 112, 124, 136, 137, 152
V_BOTTOM = LAYERS
LAT_W, LAT_C, LAT_V, LAT_SIDE, LAT_ROWS = 96, 108, 120, 128, 160
FULL = ROWS + 2 * HALO
WIDE = 2 * COLS
half = 0.5 * baroclinic_step
FAR_PARTS = 5


def lane_index(shape):
    return lax.broadcasted_iota(jnp.int32, shape, 1)


def row_index(shape):
    return lax.broadcasted_iota(jnp.int32, shape, 0)


def roll(x, shift, axis):
    shift = shift % x.shape[axis]
    return x if shift == 0 else pltpu.roll(x, shift, axis)


def first_kernel(
    gravity_hbm, lu_hbm, lv_hbm, th_hbm, lev_hbm, u_hbm, v_hbm, land_hbm, bottom_hbm, fold_hbm,
    msg_a, msg_b, own_pairs, own_rows, flat, cor_out, g_rows, to_potential, tail_u, tail_v, weight, th, floor,
    lu, lv, gravity, fold, sems,
):
    pairs = (
        (th_hbm, th), (land_hbm, floor.at[0]), (bottom_hbm, floor.at[1]), (gravity_hbm, gravity), (lu_hbm, lu),
        (lv_hbm, lv), (lev_hbm, flat.at[5]), (u_hbm, flat.at[6]), (v_hbm, flat.at[7]),
        (fold_hbm, fold),
    )
    copies = [pltpu.make_async_copy(a, b, sems.at[n]) for n, (a, b) in enumerate(pairs)]
    for copy in copies:
        copy.start()
    lon, lat = lax.axis_index("lon"), lax.axis_index("lat")
    even = lax.rem(lon, 2) == 0
    rows = (row_index((FULL, COLS)) + (lat * ROWS - HALO)).astype(jnp.float32)
    cor_all = -coriolis_scale * jnp.cos((rows + 0.5) * (jnp.pi / TOTAL_ROWS))
    cor_out[...] = cor_all
    cor = cor_all[HALO : HALO + ROWS]
    lane = lane_index((ROWS, COLS))
    row = row_index((ROWS, COLS))
    copies[3].wait()
    line = (lane_index((COLS, COLS)) - PAIR_LANE) >> 1
    at = (row_index((COLS, COLS)) - PAIR_LANE) >> 1
    upper, lower = jnp.zeros((COLS, COLS), jnp.float32), jnp.zeros((COLS, COLS), jnp.float32)
    total = 0.0
    for k in range(LAYERS):
        g_rows[k : k + 1, :] = jnp.full((1, COLS), gravity[k], jnp.float32)
        lower = jnp.where(at == k, total, lower)
        total = total + gravity[k]
        upper = jnp.where(line == k, total, upper)
    used = (at >= 0) & (at <= line) & (line < LAYERS) & (((lane_index((COLS, COLS)) - row_index((COLS, COLS))) & 1) == 0)
    to_potential[...] = jnp.where(used, upper - lower, 0.0)
    for copy in copies[:3] + copies[4:]:
        copy.wait()
    wet = floor[0].astype(jnp.float32)
    bot = floor[1]
    lev, u, v = flat[5], flat[6], flat[7]
    zero = jnp.zeros((ROWS, COLS), jnp.float32)
    g_rows[LAYERS : LAYERS + 1, :] = jnp.zeros((1, COLS), jnp.float32)
    offset = 64 + ((fold[0] + 64) & (COLS - 1))
    g_rows[LAYERS + 1 : LAYERS + 2, :] = jnp.full((1, COLS), offset, jnp.int32).astype(jnp.float32)
    lons = lax.axis_size("lon")
    apart = lax.rem((fold[0] + lons * COLS - 64) // COLS - lon + lons, lons)
    g_rows[LAYERS + 2 : LAYERS + 3, :] = jnp.full((1, COLS), jnp.where(apart == 0, 1.0, 0.0), jnp.float32)
    g_rows[LAYERS + 3 :, :] = jnp.zeros((1, COLS), jnp.float32)

    depth, potential = zero, zero
    grad_u, grad_v, sum_u, sum_v = zero, zero, zero, zero
    for k in range(LAYERS):
        w = jnp.where(bot > k, wet, 0.0) * th[k]
        depth = depth + w
        potential = potential + gravity[k] * depth
        right = jnp.where(lane == COLS - 1, 0.0, roll(potential, -1, 1))
        left = jnp.where(lane == 0, 0.0, roll(potential, 1, 1))
        above = jnp.where(row == ROWS - 1, 0.0, roll(potential, -1, 0))
        below = jnp.where(row == 0, 0.0, roll(potential, 1, 0))
        du = 0.5 * (left - right)
        dv = 0.5 * (below - above)
        grad_u = grad_u + w * du
        grad_v = grad_v + w * dv
        sum_u = sum_u + w * lu[k]
        sum_v = sum_v + w * lv[k]
        rest_u = lu[k] + baroclinic_step * (du + cor * lv[k])
        rest_v = lv[k] + baroclinic_step * (dv - cor * lu[k])
        tail_u[k] = rest_u
        tail_v[k] = rest_v
        weight[k] = w
        for msg in (msg_a, msg_b):
            msg[W_TOP + k : W_TOP + k + 1, :] = w[ROWS - 1 :]
            msg[W_BOTTOM + k : W_BOTTOM + k + 1, :] = w[:1]
            msg[C_TOP + k : C_TOP + k + 1, :] = rest_v[ROWS - 1 :]
        own_rows[k : k + 1, :] = rest_v[:1]
    edge_w, edge_c = zero, zero
    for k in range(LAYERS):
        here = lane >> 1 == k
        edge_w = jnp.where(here, roll(weight[k], 2 * k + 1, 1), edge_w)
        edge_c = jnp.where(here, roll(tail_u[k], 2 * k + 1, 1), edge_c)
    own_pairs[...] = edge_w
    inverse = 1.0 / (depth + (1.0 - wet))
    column_u = sum_u * inverse
    column_v = sum_v * inverse
    force_u = grad_u * inverse + cor * column_v
    force_v = grad_v * inverse - cor * column_u
    fields = (depth, u, v, lev, force_u, force_v)
    flat[0] = depth
    flat[1] = force_u
    flat[2] = force_v
    flat[3] = column_u
    flat[4] = column_v
    transport_u = depth * u
    transport_v = depth * v
    is_odd = lane % 2 == 1
    west, east = zero, zero
    for f, field in enumerate(fields):
        moved = roll(field, HALO * f, 1)
        west = jnp.where(lane // HALO == f, moved, west)
        east = jnp.where(lane // HALO == (f - 1) % 8, moved, east)
    in_west = (lane >= PAIR_LANE) & (lane < PAIR_END)
    in_east = (lane >= EAST_PAIR_LANE) & (lane < EAST_PAIR_LANE + 2 * LAYERS)

    def pairs_of(w, rest, edge):
        column = jnp.sum(jnp.where(lane == edge, column_u, 0.0), axis=1, keepdims=True)
        return jnp.where(is_odd, rest - column, w)

    west = jnp.where(in_west, pairs_of(roll(edge_w, PAIR_LANE - 1, 1), roll(edge_c, PAIR_LANE, 1), 0), west)
    west = jnp.where(lane == PAIR_END, roll(transport_u, PAIR_END - HALO, 1), west)
    at = EAST_PAIR_LANE
    east = jnp.where(in_east, pairs_of(roll(edge_w, at, 1), roll(edge_c, at + 1, 1), COLS - 1), east)
    at = PAIR_END - HALO
    east = jnp.where(lane == at, roll(transport_u, at - (COLS - 1 - HALO), 1), east)
    msg_a[:ROWS] = jnp.where(even, east, west)
    msg_b[:ROWS] = jnp.where(even, west, east)
    low = lane_index((8, COLS)) < 64
    for f, field in enumerate(fields):
        lower, upper = field[ROWS - HALO : ROWS - 8], field[ROWS - 8 :]
        west = jnp.where(low, roll(lower, -16, 1), roll(upper, 48, 1))
        east = jnp.where(low, roll(lower, -48, 1), roll(upper, 16, 1))
        msg_a[TOP_ROW + 8 * f : TOP_ROW + 8 * (f + 1)] = jnp.where(even, east, west)
        msg_b[TOP_ROW + 8 * f : TOP_ROW + 8 * (f + 1)] = jnp.where(even, west, east)
    for msg in (msg_a, msg_b):
        msg[C_TOP : C_TOP + LAYERS] = msg[C_TOP : C_TOP + LAYERS] - column_v[ROWS - 1 :]
        msg[V_TOP : V_TOP + 1] = transport_v[ROWS - 1 - HALO : ROWS - HALO]
        msg[W_BOTTOM + LAYERS :] = jnp.zeros((LON_ROWS - W_BOTTOM - LAYERS, COLS), jnp.float32)
    own_rows[:LAYERS] = own_rows[:LAYERS] - column_v[:1]
    own_rows[V_BOTTOM : V_BOTTOM + 1] = transport_v[HALO : HALO + 1]
    own_rows[V_BOTTOM + 1 :] = jnp.zeros((16 - V_BOTTOM - 1, COLS), jnp.float32)


def second_kernel(g_rows, to_potential, flat, own_pairs, own_rows, own_a, got_a, got_b, ext, edges, msg_x, msg_y, msg_f):
    lon, lat = lax.axis_index("lon"), lax.axis_index("lat")
    even_lon = lax.rem(lon, 2) == 0
    even_lat = lax.rem(lat, 2) == 0
    lane = lane_index((ROWS, COLS))
    is_pair = (lane >= PAIR_LANE) & (lane < PAIR_END)
    is_odd = lane % 2 == 1
    sign = jnp.where(is_odd, -1.0, 1.0)
    east = jnp.where(even_lon, got_a[:ROWS], got_b[:ROWS])
    west = jnp.where(even_lon, got_b[:ROWS], got_a[:ROWS])

    def dots(x):
        even_sum = jnp.sum(jnp.where(is_odd, 0.0, x), axis=1, keepdims=True)
        odd_sum = jnp.sum(jnp.where(is_odd, x, 0.0), axis=1, keepdims=True)
        return 0.5 * even_sum, 0.5 * odd_sum

    apart = PAIR_LANE - EAST_PAIR_LANE
    w_halo = jnp.where(is_pair, jnp.where(is_odd, roll(west, apart + 1, 1), east), 0.0)
    c_halo = jnp.where(is_odd, roll(west, apart, 1), roll(east, -1, 1))
    w_own = roll(own_pairs[...], PAIR_LANE, 1)
    both = jnp.concatenate([w_halo, w_own], axis=0)
    both = jnp.dot(both, to_potential[...], precision=lax.Precision.HIGHEST, preferred_element_type=jnp.float32)
    p_halo, p_own = both[:ROWS], both[ROWS:]
    edges[0] = (-half * sign) * p_halo
    edges[1] = w_halo * (c_halo + (half * sign) * p_own)
    edges[2] = w_halo

    depth = flat[0]
    safe = depth + jnp.where(depth > 0.0, 0.0, 1.0)
    to_e, to_w = dots(w_own * p_halo)
    force_u = flat[1] + jnp.where(lane == COLS - 1, -to_e, jnp.where(lane == 0, to_w, 0.0)) / safe

    sides = [roll(jnp.where(lane // HALO == f, east, west), -HALO * f, 1) for f in range(6)]
    sides[1] = jnp.where(lane == HALO, roll(east, HALO - PAIR_END, 1), sides[1])
    at = COLS - HALO - 1
    sides[1] = jnp.where(lane == at, roll(west, at - (PAIR_END - HALO), 1), sides[1])
    safe = sides[0] + jnp.where(sides[0] > 0.0, 0.0, 1.0)
    to_e, to_w = dots(w_halo * p_own)
    sides[4] = sides[4] + jnp.where(lane == 0, to_e, jnp.where(lane == COLS - 1, -to_w, 0.0)) / safe
    sides[0] = jnp.where((lane == HALO) | (lane == at), 1.0, sides[0])

    for f, field in enumerate((depth, flat[6], flat[7], flat[5], force_u, flat[2])):
        ext[f, :, :COLS] = field
        ext[f, :, COLS:] = sides[f]

    lane12 = lane_index((LAYERS, COLS))
    lane16 = lane_index((HALO, COLS))

    def lat_message(msg, north):
        start, w_at = (ROWS - HALO, W_TOP) if north else (0, W_BOTTOM)
        edge, c_at, v_at = (own_a, C_TOP, V_TOP) if north else (own_rows, 0, V_BOTTOM)
        packed = [jnp.zeros((HALO, COLS), jnp.float32)] * 2
        for f in range(6):
            msg[HALO * f : HALO * (f + 1), :] = ext[f, start : start + HALO, :COLS]
            side = roll(ext[f, start : start + HALO, COLS:], HALO + 32 * (f % 4), 1)
            packed[f // 4] = jnp.where(lane16 // 32 == f % 4, side, packed[f // 4])
        msg[LAT_SIDE : LAT_SIDE + HALO, :] = packed[0]
        msg[LAT_SIDE + HALO :, :] = packed[1]
        msg[LAT_W : LAT_W + LAYERS, :] = own_a[w_at : w_at + LAYERS, :]
        beside_e = jnp.where(even_lon, got_a[w_at : w_at + LAYERS, :], got_b[w_at : w_at + LAYERS, :])
        beside_w = jnp.where(even_lon, got_b[w_at : w_at + LAYERS, :], got_a[w_at : w_at + LAYERS, :])
        beside = roll(jnp.where(lane12 < HALO, beside_e, beside_w), HALO + 64, 1)
        held = msg[LAT_SIDE + HALO : LAT_SIDE + HALO + LAYERS, :]
        msg[LAT_SIDE + HALO : LAT_SIDE + HALO + LAYERS, :] = jnp.where(lane12 // 32 == 2, beside, held)
        msg[LAT_C : LAT_C + LAYERS, :] = edge[c_at : c_at + LAYERS, :]
        msg[LAT_V : LAT_V + 1, :] = edge[v_at : v_at + 1, :]
        msg[LAT_V + 1 : LAT_SIDE, :] = jnp.zeros((LAT_SIDE - LAT_V - 1, COLS), jnp.float32)

    @pl.when(even_lat)
    def _():
        lat_message(msg_x, True)
        lat_message(msg_y, False)

    @pl.when(jnp.logical_not(even_lat))
    def _():
        lat_message(msg_x, False)
        lat_message(msg_y, True)


    @pl.when(lat == lax.axis_size("lat") - 1)
    def _():
        lane8 = lane_index((8, COLS))
        row8 = row_index((8, COLS))
        offset = jnp.broadcast_to(g_rows[LAYERS + 1 : LAYERS + 2, :].astype(jnp.int32), (8, COLS))
        source = (offset - lane8) & (COLS - 1)
        taker = source
        block = (COLS + offset - taker) >> 7
        side_block = jnp.where(taker < HALO, offset - taker, 2 * COLS + offset - taker) >> 7

        def gather(x, index, axis):
            return jnp.take_along_axis(x, index, axis=axis, mode="promise_in_bounds")

        def window(w_tile, o_tile, e_tile):
            main = jnp.where(block == 0, w_tile, jnp.where(block == 1, o_tile, e_tile))
            side = jnp.where(side_block == 0, w_tile, jnp.where(side_block == 1, o_tile, e_tile))
            return gather(main, source, 1), gather(side, source, 1)

        def tiles(at):
            on_e = jnp.where(even_lon, got_a[at : at + 8, :], got_b[at : at + 8, :])
            on_w = jnp.where(even_lon, got_b[at : at + 8, :], got_a[at : at + 8, :])
            return on_w, own_a[at : at + 8, :], on_e

        packed = {}

        def pack(at, group, x):
            x = roll(x, HALO + 32 * group, 1)
            packed[at] = jnp.where(lane8 // 32 == group, x, packed[at]) if at in packed else x

        for f in range(6):
            sign = 1.0 if f in (0, 3) else -1.0
            for t in range(2):
                at = ROWS - 8 * (t + 1)
                mine = ext[f, at : at + 8, :COLS]
                side = ext[f, at : at + 8, COLS:]
                on_w, _, on_e = tiles(TOP_ROW + 8 * f)
                on_e = jnp.where(lane8 < HALO, side, roll(on_e, -48 if t == 0 else 16, 1))
                on_w = jnp.where(lane8 >= COLS - HALO, side, roll(on_w, -16 if t == 0 else 48, 1))
                main, beside = window(on_w, mine, on_e)
                msg_f[HALO * f + 8 * t : HALO * f + 8 * (t + 1), :] = sign * gather(main, 7 - row8, 0)
                pack(LAT_SIDE + HALO * (f // 4) + 8 * t, f % 4, sign * gather(beside, 7 - row8, 0))
        for t in range(3):
            main, beside = window(*tiles(W_TOP + 8 * t))
            sign = jnp.where(row8 + 8 * t < LAYERS, 1.0, -1.0)
            msg_f[LAT_W + 8 * t : LAT_W + 8 * (t + 1), :] = sign * main
            if t < 2:
                pack(LAT_SIDE + HALO + 8 * t, 2, beside)
        main, _ = window(*tiles(V_TOP))
        msg_f[LAT_V : LAT_V + 8, :] = -main
        for at, x in packed.items():
            msg_f[at : at + 8, :] = x

    @pl.when(lat != lax.axis_size("lat") - 1)
    def _():
        msg_f[...] = msg_y[...]


def third_kernel(
    g_rows, tail_u, tail_v, weight, th, floor, flat, cor_ref, edges, ext, own_x, own_y, own_f, got_x, got_f_hbm,
    new_u_hbm, new_v_hbm, new_th_hbm, new_lev_hbm, mean_u_hbm, mean_v_hbm,
    far, level_pad, v_pad, state, fixed, pots, seam_w, seam_rows, new_u, new_v, new_th, flux_v_pad, planes,
    sems, plane_sems, far_sem,
):
    lat = lax.axis_index("lat")
    even = lax.rem(lat, 2) == 0
    at_top = lat == lax.axis_size("lat") - 1
    at_bottom = lat == 0

    far_copies = []
    for n in range(FAR_PARTS):
        part = pl.ds(n * (LAT_ROWS // FAR_PARTS), LAT_ROWS // FAR_PARTS)
        far_copies.append(pltpu.make_async_copy(got_f_hbm.at[part], far.at[part], far_sem.at[n]))
    for copy in far_copies:
        copy.start()
    inner = slice(HALO, HALO + ROWS)

    def place(at, count, depth, u, v, level, force_u, force_v, rate):
        rows = pl.ds(at, count)
        cor = cor_ref[rows, :]
        cor = jnp.concatenate([cor, cor], axis=1)
        wet = jnp.where(depth > 0.0, 1.0, 0.0)
        fixed[0, rows, :] = depth
        fixed[1, rows, :] = wet * (1.0 - barotropic_step * bottom_drag)
        fixed[2, rows, :] = wet * (barotropic_step * cor)
        fixed[3, rows, :] = wet * (barotropic_step * force_u)
        fixed[4, rows, :] = wet * (barotropic_step * force_v)
        fixed[5, rows, :] = wet * (0.5 * barotropic_step)
        fixed[6, rows, :] = jnp.full((count, WIDE), rate, jnp.float32)
        state[0, rows, :] = u
        state[1, rows, :] = v
        level_pad[pl.ds(at + 8, count), :] = level

    place(HALO, ROWS, *(ext[f] for f in range(6)), 0.5 * barotropic_step)

    def strip(got, mine, slot, is_north, keep):
        at = pl.multiple_of(jnp.where(is_north, HALO + ROWS, 0), HALO)
        sign = jnp.where(is_north, 1.0, -1.0)
        fields = []
        for f in range(6):
            main = got[HALO * f : HALO * (f + 1), :]
            side = got[LAT_SIDE + HALO * (f // 4) : LAT_SIDE + HALO * (f // 4 + 1), :]
            side = roll(side, -HALO - 32 * (f % 4), 1)
            fields.append(jnp.concatenate([main, side], axis=1))
        if keep is not None:
            fields = [jnp.where(keep, field, 0.0) for field in fields]
        rate = 0.5 * barotropic_step
        place(at, HALO, *fields, rate if keep is None else jnp.where(keep, rate, 0.0))
        v_row = got[LAT_V : LAT_V + 1, :]
        if keep is not None:
            v_row = jnp.where(keep, v_row, 0.0)
        v_rows = pl.ds(pl.multiple_of(jnp.where(is_north, 8 + FULL, 0), 8), 8)
        v_pad[v_rows, :COLS] = jnp.broadcast_to(v_row, (8, COLS))
        v_pad[v_rows, COLS:] = jnp.zeros((8, COLS), jnp.float32)
        for n, ref in enumerate((mine, got)):
            w = ref[LAT_W : LAT_W + LAYERS, :]
            side = roll(ref[LAT_SIDE + HALO : LAT_SIDE + HALO + LAYERS, :], -HALO - 64, 1)
            if n == 1 and keep is not None:
                w, side = jnp.where(keep, w, 0.0), jnp.where(keep, side, 0.0)
            seam_w[n, :LAYERS, :COLS] = w
            seam_w[n, :LAYERS, COLS:] = side
        sum_o, sum_s, pot_o, pot_s, to_o, to_s = (jnp.zeros((1, WIDE), jnp.float32) for _ in range(6))
        for k in range(LAYERS):
            wo, ws = seam_w[0, k : k + 1, :], seam_w[1, k : k + 1, :]
            g = jnp.concatenate([g_rows[k : k + 1, :]] * 2, axis=1)
            sum_o, sum_s = sum_o + wo, sum_s + ws
            pot_o, pot_s = pot_o + g * sum_o, pot_s + g * sum_s
            to_o = to_o + wo * pot_s
            to_s = to_s + ws * pot_o
            pots[0, k : k + 1, :] = pot_o[:, :COLS]
            pots[1, k : k + 1, :] = pot_s[:, :COLS]
        safe_o = sum_o + jnp.where(sum_o > 0.0, 0.0, 1.0)
        safe_s = sum_s + jnp.where(sum_s > 0.0, 0.0, 1.0)
        scale = 0.5 * barotropic_step * sign
        row8 = row_index((8, WIDE))
        own_rows = pl.ds(pl.multiple_of(jnp.where(is_north, HALO + ROWS - 8, HALO), 8), 8)
        strip_rows = pl.ds(pl.multiple_of(jnp.where(is_north, HALO + ROWS, HALO - 8), 8), 8)
        last, first = row8 == jnp.where(is_north, 7, 0), row8 == jnp.where(is_north, 0, 7)
        fixed[4, own_rows, :] = fixed[4, own_rows, :] - jnp.where(last, scale * to_o / safe_o, 0.0)
        fixed[4, strip_rows, :] = fixed[4, strip_rows, :] + jnp.where(first, scale * to_s / safe_s, 0.0)
        side = jnp.where(is_north, 0, 3)
        w = seam_w[1, :LAYERS, :COLS]
        seam_rows[side, :LAYERS, :] = (-half * sign) * pots[1, :LAYERS, :]
        seam_rows[side + 1, :LAYERS, :] = w * (got[LAT_C : LAT_C + LAYERS, :] + (half * sign) * pots[0, :LAYERS, :])
        seam_rows[side + 2, :LAYERS, :] = w

    strip(got_x, own_x, 0, even, None)
    for copy in far_copies:
        copy.wait()

    far[...] = jnp.where(at_top & (g_rows[LAYERS + 2 : LAYERS + 3, :] > 0.0), own_f[...], far[...])
    strip(far, own_y, 1, jnp.logical_not(even), jnp.logical_not(at_bottom))

    def blocks(skip):
        edges_at = list(range(skip, FULL - skip, 8)) + [FULL - skip]
        return list(zip(edges_at[:-1], edges_at[1:]))

    for begin, end in blocks(0):
        v_pad[8 + begin : 8 + end, :] = fixed[0, begin:end, :] * state[1, begin:end, :]
    for step in range(SUBSTEPS):
        skip = (2 * step) // 8 * 8
        for begin, end in blocks(skip):
            trans_u = fixed[0, begin:end, :] * state[0, begin:end, :]
            dv = v_pad[9 + begin : 9 + end, :] - v_pad[7 + begin : 7 + end, :]
            du = pltpu.roll(trans_u, WIDE - 1, 1) - pltpu.roll(trans_u, 1, 1)
            held = level_pad[8 + begin : 8 + end, :]
            level_pad[8 + begin : 8 + end, :] = held - fixed[6, begin:end, :] * (du + dv)
        for begin, end in blocks(skip):
            u, v = state[0, begin:end, :], state[1, begin:end, :]
            level = level_pad[8 + begin : 8 + end, :]
            dy = level_pad[9 + begin : 9 + end, :] - level_pad[7 + begin : 7 + end, :]
            dx = pltpu.roll(level, WIDE - 1, 1) - pltpu.roll(level, 1, 1)
            keep, turn, slope = fixed[1, begin:end, :], fixed[2, begin:end, :], fixed[5, begin:end, :]
            next_u = keep * u + turn * v + fixed[3, begin:end, :] - slope * dx
            next_v = keep * v - turn * u + fixed[4, begin:end, :] - slope * dy
            state[0, begin:end, :] = next_u
            state[1, begin:end, :] = next_v
            state[2, begin:end, :] = next_u if step == 0 else state[2, begin:end, :] + next_u
            state[3, begin:end, :] = next_v if step == 0 else state[3, begin:end, :] + next_v
            v_pad[8 + begin : 8 + end, :] = fixed[0, begin:end, :] * next_v
    planes[0] = level_pad[8 + HALO : 8 + HALO + ROWS, :COLS]
    planes[1] = state[2, inner, :COLS] * (1.0 / SUBSTEPS)
    planes[2] = state[3, inner, :COLS] * (1.0 / SUBSTEPS)
    plane_copies = [
        pltpu.make_async_copy(planes.at[n], out, plane_sems.at[n])
        for n, out in enumerate((new_lev_hbm, mean_u_hbm, mean_v_hbm))
    ]
    for copy in plane_copies:
        copy.start()

    to_force = baroclinic_step / barotropic_step

    def rest(n, rows, lanes):
        return state[2 + n, rows, lanes] * (1.0 / SUBSTEPS) - to_force * fixed[3 + n, rows, lanes]

    main, beside = slice(0, COLS), slice(COLS, WIDE)
    lane = lane_index((ROWS, COLS))
    row = row_index((ROWS, COLS))
    is_e, is_w = lane == COLS - 1, lane == 0
    base_u = rest(0, inner, main) - flat[3]
    base_v = rest(1, inner, main) - flat[4]
    side_u = rest(0, inner, beside)
    rest_e = jnp.sum(jnp.where(is_w, side_u, 0.0), axis=1, keepdims=True)
    rest_w = jnp.sum(jnp.where(is_e, side_u, 0.0), axis=1, keepdims=True)
    pair_flux = edges[1] + edges[2] * jnp.where(lane % 2 == 0, rest_e, rest_w)
    pair_fix = edges[0]
    rest_n = rest(1, slice(HALO + ROWS, HALO + ROWS + 1), main)
    rest_s = rest(1, slice(HALO - 1, HALO), main)
    for side, line in ((0, rest_n), (3, rest_s)):
        seam_rows[side + 1, :LAYERS, :] = seam_rows[side + 1, :LAYERS, :] + seam_rows[side + 2, :LAYERS, :] * line
    levels = jnp.where(floor[0] > 0, floor[1], 0)
    copies = []
    parts = ((0, 4), (4, 8), (8, 11), (11, 12))
    lanes16 = lane_index((32, COLS))
    rows16 = row_index((32, COLS))
    is_e, is_w = lanes16 == COLS - 1, lanes16 == 0
    is_edge = is_e | is_w
    for k in range(LAYERS):
        shift = COLS - 1 - PAIR_LANE - 2 * k
        flux_v_pad[k, 7:8, :] = seam_rows[4, k : k + 1, :]
        flux_v_pad[k, 8 + ROWS : 9 + ROWS, :] = seam_rows[1, k : k + 1, :]
        for begin in range(0, ROWS, 32):
            at = slice(begin, begin + 32)
            w = weight[k, at, :]
            mask = levels[at] > k
            rest_u = tail_u[k, at, :] + base_u[at] + jnp.where(is_edge, roll(pair_fix[at], shift, 1), 0.0)
            rest_v = tail_v[k, at, :] + base_v[at]
            if begin == 0:
                rest_v = rest_v + jnp.where(rows16 == 0, seam_rows[3, k : k + 1, :], 0.0)
            if begin == ROWS - 32:
                rest_v = rest_v + jnp.where(rows16 == 32 - 1, seam_rows[0, k : k + 1, :], 0.0)
            out_u = jnp.where(mask, rest_u, 0.0)
            out_v = jnp.where(mask, rest_v, 0.0)
            new_u[k, at, :] = out_u
            new_v[k, at, :] = out_v
            flux_u = w * out_u
            flux_v_pad[k, 8 + begin : 8 + begin + 32, :] = w * out_v
            halo = roll(pair_flux[at], shift, 1)
            east = jnp.where(is_e, halo, pltpu.roll(flux_u, COLS - 1, 1))
            west = jnp.where(is_w, halo, pltpu.roll(flux_u, 1, 1))
            new_th[k, at, :] = th[k, at, :] - half * (east - west)
        north = flux_v_pad[k, 9 : 9 + ROWS, :]
        south = flux_v_pad[k, 7 : 7 + ROWS, :]
        new_th[k] = new_th[k] - half * (north - south)
        for part, (begin, end) in enumerate(parts):
            if k == end - 1:
                rows = pl.ds(begin, end - begin)
                for n, (held, out) in enumerate(((new_u, new_u_hbm), (new_v, new_v_hbm), (new_th, new_th_hbm))):
                    copy = pltpu.make_async_copy(held.at[rows], out.at[rows], sems.at[n, part])
                    copy.start()
                    copies.append(copy)
    for copy in copies + plane_copies:
        copy.wait()


def vmem(count):
    return [pl.BlockSpec(memory_space=pltpu.VMEM)] * count


def hbm(count):
    return [pl.BlockSpec(memory_space=pltpu.HBM)] * count


def in_hbm(*arrays):
    return tuple(pltpu.with_memory_space_constraint(x, pltpu.HBM) for x in arrays)


def f32(*shape):
    return jax.ShapeDtypeStruct(shape, jnp.float32)


PARAMS = pltpu.CompilerParams(vmem_limit_bytes=40 * 2**20)


def local(lu, lv, th, lev, u, v, land, bottom, fold_map, gravity):
    lons, lats = lax.axis_size("lon"), lax.axis_size("lat")
    lon_msg, lat_msg = f32(LON_ROWS, COLS), f32(LAT_ROWS, COLS)
    layers, plane = f32(LAYERS, ROWS, COLS), f32(ROWS, COLS)
    held = pltpu.VMEM((LAYERS, ROWS, COLS), jnp.float32)
    total = lons * COLS
    pivot = fold_map[0] + lax.axis_index("lon") * COLS
    shift = jnp.mod(pivot - COLS // 2, total) // COLS

    msg_a, msg_b, own_pairs, own_rows, flat, cor, g_rows, to_potential, tail_u, tail_v, weight, th, floor = pl.pallas_call(
        first_kernel,
        out_shape=(
            lon_msg, lon_msg, plane, f32(16, COLS), f32(8, ROWS, COLS), f32(FULL, COLS), f32(16, COLS), f32(COLS, COLS),
            layers, layers, layers, layers,
            jax.ShapeDtypeStruct((2, ROWS, COLS), jnp.int32),
        ),
        in_specs=hbm(10),
        out_specs=vmem(13),
        scratch_shapes=[
            held,
            held,
            pltpu.SMEM((LAYERS,), jnp.float32),
            pltpu.SMEM((COLS,), jnp.int32),
            pltpu.SemaphoreType.DMA((10,)),
        ],
        compiler_params=PARAMS,
        name="edges",
    )(*in_hbm(gravity, lu, lv, th, lev, u, v, land, bottom, fold_map))

    got_a = lax.ppermute(msg_a, "lon", [(i, i ^ 1) for i in range(lons)])
    got_b = lax.ppermute(msg_b, "lon", [(i, (((i + 1) ^ 1) - 1) % lons) for i in range(lons)])
    got_a, got_b, shift = lax.optimization_barrier((got_a, got_b, shift))

    ext, edges, msg_x, msg_y, msg_f = pl.pallas_call(
        second_kernel,
        out_shape=(f32(6, ROWS, WIDE), f32(3, ROWS, COLS), lat_msg, lat_msg, lat_msg),
        in_specs=vmem(8),
        out_specs=vmem(5),
        compiler_params=PARAMS,
        name="extend",
    )(g_rows, to_potential, flat, own_pairs, own_rows, msg_a, got_a, got_b)

    got_x = lax.ppermute(msg_x, "lat", [(i, i ^ 1) for i in range(lats)])
    top = lats - 1
    rows = [(b * lats + i, b * lats + ((i + 1) ^ 1) - 1) for b in range(lons) for i in range(1, top)]
    rows += [(b * lats, (b ^ 1) * lats) for b in range(lons)]

    def exchange(q):
        pairs = list(rows)
        for b in range(lons):
            source = (q - b) % lons
            source = (b + lons // 2) % lons if source == b else source
            pairs.append((source * lats + top, b * lats + top))
        return lambda x: lax.ppermute(x, ("lon", "lat"), pairs)

    got_f = lax.switch(shift, [exchange(q) for q in range(lons)], msg_f)

    padded = pltpu.VMEM((FULL + 16, WIDE), jnp.float32)
    rows16 = pltpu.VMEM((6, 16, COLS), jnp.float32)
    return pl.pallas_call(
        third_kernel,
        out_shape=(layers, layers, layers, plane, plane, plane),
        in_specs=vmem(14) + hbm(1),
        out_specs=hbm(6),
        scratch_shapes=[
            pltpu.VMEM((LAT_ROWS, COLS), jnp.float32),
            padded,
            padded,
            pltpu.VMEM((4, FULL, WIDE), jnp.float32),
            pltpu.VMEM((7, FULL, WIDE), jnp.float32),
            rows16,
            pltpu.VMEM((2, 16, WIDE), jnp.float32),
            rows16,
            held,
            held,
            held,
            pltpu.VMEM((LAYERS, ROWS + 16, COLS), jnp.float32),
            pltpu.VMEM((3, ROWS, COLS), jnp.float32),
            pltpu.SemaphoreType.DMA((3, 4)),
            pltpu.SemaphoreType.DMA((3,)),
            pltpu.SemaphoreType.DMA((FAR_PARTS,)),
        ],
        compiler_params=PARAMS,
        name="advance",
    )(g_rows, tail_u, tail_v, weight, th, floor, flat, cor, edges, ext, msg_x, msg_y, msg_f, got_x, *in_hbm(got_f))


def solution(mesh):
    layered, plane = P(None, "lat", "lon"), P("lat", "lon")
    return jax.shard_map(
        local,
        mesh=mesh,
        in_specs=(layered,) * 3 + (plane,) * 5 + (P("lon"), P()),
        out_specs=(layered,) * 3 + (plane,) * 3,
        check_vma=False,
    )
```

```python
import jax
import jax.numpy as jnp
from jax import lax
from jax.experimental import pallas as pl
from jax.experimental.pallas import tpu as pltpu
from jax.sharding import PartitionSpec as P

SUBSTEPS = 8
LAYERS = 12
TOTAL_ROWS = 512
ROWS, COLS = 64, 128
HALO = 16

barotropic_step = 0.45
baroclinic_step = 0.1
coriolis_scale = 0.3
bottom_drag = 0.05

PAIR_LANE, EAST_PAIR_LANE = 96, 80
PAIR_END = PAIR_LANE + 2 * LAYERS
TOP_ROW, W_TOP, C_TOP, V_TOP, W_BOTTOM, LON_ROWS = 64, 112, 124, 136, 137, 152
V_BOTTOM = LAYERS
LAT_W, LAT_C, LAT_V, LAT_SIDE, LAT_ROWS = 96, 108, 120, 128, 160
FULL = ROWS + 2 * HALO
WIDE = 2 * COLS
half = 0.5 * baroclinic_step
FAR_PARTS = 5


def lane_index(shape):
    return lax.broadcasted_iota(jnp.int32, shape, 1)


def row_index(shape):
    return lax.broadcasted_iota(jnp.int32, shape, 0)


def roll(x, shift, axis):
    shift = shift % x.shape[axis]
    return x if shift == 0 else pltpu.roll(x, shift, axis)


def first_kernel(
    gravity_hbm, lu_hbm, lv_hbm, th_hbm, lev_hbm, u_hbm, v_hbm, land_hbm, bottom_hbm, fold_hbm,
    msg_a, msg_b, own_pairs, own_rows, flat, cor_out, g_rows, to_potential, tail_u, tail_v, weight, th, floor,
    lu, lv, gravity, fold, sems,
):
    pairs = (
        (th_hbm, th), (land_hbm, floor.at[0]), (bottom_hbm, floor.at[1]), (gravity_hbm, gravity), (lu_hbm, lu),
        (lv_hbm, lv), (lev_hbm, flat.at[5]), (u_hbm, flat.at[6]), (v_hbm, flat.at[7]),
        (fold_hbm, fold),
    )
    copies = [pltpu.make_async_copy(a, b, sems.at[n]) for n, (a, b) in enumerate(pairs)]
    for copy in copies:
        copy.start()
    lon, lat = lax.axis_index("lon"), lax.axis_index("lat")
    even = lax.rem(lon, 2) == 0
    rows = (row_index((FULL, COLS)) + (lat * ROWS - HALO)).astype(jnp.float32)
    cor_all = -coriolis_scale * jnp.cos((rows + 0.5) * (jnp.pi / TOTAL_ROWS))
    cor_out[...] = cor_all
    cor = cor_all[HALO : HALO + ROWS]
    lane = lane_index((ROWS, COLS))
    row = row_index((ROWS, COLS))
    copies[3].wait()
    line = (lane_index((COLS, COLS)) - PAIR_LANE) >> 1
    at = (row_index((COLS, COLS)) - PAIR_LANE) >> 1
    upper, lower = jnp.zeros((COLS, COLS), jnp.float32), jnp.zeros((COLS, COLS), jnp.float32)
    total = 0.0
    for k in range(LAYERS):
        g_rows[k : k + 1, :] = jnp.full((1, COLS), gravity[k], jnp.float32)
        lower = jnp.where(at == k, total, lower)
        total = total + gravity[k]
        upper = jnp.where(line == k, total, upper)
    used = (at >= 0) & (at <= line) & (line < LAYERS) & (((lane_index((COLS, COLS)) - row_index((COLS, COLS))) & 1) == 0)
    to_potential[...] = jnp.where(used, upper - lower, 0.0)
    for copy in copies[:3] + copies[4:]:
        copy.wait()
    wet = floor[0].astype(jnp.float32)
    bot = floor[1]
    lev, u, v = flat[5], flat[6], flat[7]
    zero = jnp.zeros((ROWS, COLS), jnp.float32)
    g_rows[LAYERS : LAYERS + 1, :] = jnp.zeros((1, COLS), jnp.float32)
    offset = 64 + ((fold[0] + 64) & (COLS - 1))
    g_rows[LAYERS + 1 : LAYERS + 2, :] = jnp.full((1, COLS), offset, jnp.int32).astype(jnp.float32)
    lons = lax.axis_size("lon")
    apart = lax.rem((fold[0] + lons * COLS - 64) // COLS - lon + lons, lons)
    g_rows[LAYERS + 2 : LAYERS + 3, :] = jnp.full((1, COLS), jnp.where(apart == 0, 1.0, 0.0), jnp.float32)
    g_rows[LAYERS + 3 :, :] = jnp.zeros((1, COLS), jnp.float32)

    depth, potential = zero, zero
    grad_u, grad_v, sum_u, sum_v = zero, zero, zero, zero
    for k in range(LAYERS):
        w = jnp.where(bot > k, wet, 0.0) * th[k]
        depth = depth + w
        potential = potential + gravity[k] * depth
        right = jnp.where(lane == COLS - 1, 0.0, roll(potential, -1, 1))
        left = jnp.where(lane == 0, 0.0, roll(potential, 1, 1))
        above = jnp.where(row == ROWS - 1, 0.0, roll(potential, -1, 0))
        below = jnp.where(row == 0, 0.0, roll(potential, 1, 0))
        du = 0.5 * (left - right)
        dv = 0.5 * (below - above)
        grad_u = grad_u + w * du
        grad_v = grad_v + w * dv
        sum_u = sum_u + w * lu[k]
        sum_v = sum_v + w * lv[k]
        rest_u = lu[k] + baroclinic_step * (du + cor * lv[k])
        rest_v = lv[k] + baroclinic_step * (dv - cor * lu[k])
        tail_u[k] = rest_u
        tail_v[k] = rest_v
        weight[k] = w
        for msg in (msg_a, msg_b):
            msg[W_TOP + k : W_TOP + k + 1, :] = w[ROWS - 1 :]
            msg[W_BOTTOM + k : W_BOTTOM + k + 1, :] = w[:1]
            msg[C_TOP + k : C_TOP + k + 1, :] = rest_v[ROWS - 1 :]
        own_rows[k : k + 1, :] = rest_v[:1]
    edge_w, edge_c = zero, zero
    for k in range(LAYERS):
        here = lane >> 1 == k
        edge_w = jnp.where(here, roll(weight[k], 2 * k + 1, 1), edge_w)
        edge_c = jnp.where(here, roll(tail_u[k], 2 * k + 1, 1), edge_c)
    own_pairs[...] = edge_w
    inverse = 1.0 / (depth + (1.0 - wet))
    column_u = sum_u * inverse
    column_v = sum_v * inverse
    force_u = grad_u * inverse + cor * column_v
    force_v = grad_v * inverse - cor * column_u
    fields = (depth, u, v, lev, force_u, force_v)
    flat[0] = depth
    flat[1] = force_u
    flat[2] = force_v
    flat[3] = column_u
    flat[4] = column_v
    transport_u = depth * u
    transport_v = depth * v
    is_odd = lane % 2 == 1
    west, east = zero, zero
    for f, field in enumerate(fields):
        moved = roll(field, HALO * f, 1)
        west = jnp.where(lane // HALO == f, moved, west)
        east = jnp.where(lane // HALO == (f - 1) % 8, moved, east)
    in_west = (lane >= PAIR_LANE) & (lane < PAIR_END)
    in_east = (lane >= EAST_PAIR_LANE) & (lane < EAST_PAIR_LANE + 2 * LAYERS)

    def pairs_of(w, rest, edge):
        column = jnp.sum(jnp.where(lane == edge, column_u, 0.0), axis=1, keepdims=True)
        return jnp.where(is_odd, rest - column, w)

    west = jnp.where(in_west, pairs_of(roll(edge_w, PAIR_LANE - 1, 1), roll(edge_c, PAIR_LANE, 1), 0), west)
    west = jnp.where(lane == PAIR_END, roll(transport_u, PAIR_END - HALO, 1), west)
    at = EAST_PAIR_LANE
    east = jnp.where(in_east, pairs_of(roll(edge_w, at, 1), roll(edge_c, at + 1, 1), COLS - 1), east)
    at = PAIR_END - HALO
    east = jnp.where(lane == at, roll(transport_u, at - (COLS - 1 - HALO), 1), east)
    msg_a[:ROWS] = jnp.where(even, east, west)
    msg_b[:ROWS] = jnp.where(even, west, east)
    low = lane_index((8, COLS)) < 64
    for f, field in enumerate(fields):
        lower, upper = field[ROWS - HALO : ROWS - 8], field[ROWS - 8 :]
        west = jnp.where(low, roll(lower, -16, 1), roll(upper, 48, 1))
        east = jnp.where(low, roll(lower, -48, 1), roll(upper, 16, 1))
        msg_a[TOP_ROW + 8 * f : TOP_ROW + 8 * (f + 1)] = jnp.where(even, east, west)
        msg_b[TOP_ROW + 8 * f : TOP_ROW + 8 * (f + 1)] = jnp.where(even, west, east)
    for msg in (msg_a, msg_b):
        msg[C_TOP : C_TOP + LAYERS] = msg[C_TOP : C_TOP + LAYERS] - column_v[ROWS - 1 :]
        msg[V_TOP : V_TOP + 1] = transport_v[ROWS - 1 - HALO : ROWS - HALO]
        msg[W_BOTTOM + LAYERS :] = jnp.zeros((LON_ROWS - W_BOTTOM - LAYERS, COLS), jnp.float32)
    own_rows[:LAYERS] = own_rows[:LAYERS] - column_v[:1]
    own_rows[V_BOTTOM : V_BOTTOM + 1] = transport_v[HALO : HALO + 1]
    own_rows[V_BOTTOM + 1 :] = jnp.zeros((16 - V_BOTTOM - 1, COLS), jnp.float32)


def second_kernel(g_rows, to_potential, flat, own_pairs, own_rows, own_a, got_a, got_b, ext, edges, msg_x, msg_y, msg_f):
    lon, lat = lax.axis_index("lon"), lax.axis_index("lat")
    even_lon = lax.rem(lon, 2) == 0
    even_lat = lax.rem(lat, 2) == 0
    lane = lane_index((ROWS, COLS))
    is_pair = (lane >= PAIR_LANE) & (lane < PAIR_END)
    is_odd = lane % 2 == 1
    sign = jnp.where(is_odd, -1.0, 1.0)
    east = jnp.where(even_lon, got_a[:ROWS], got_b[:ROWS])
    west = jnp.where(even_lon, got_b[:ROWS], got_a[:ROWS])

    def dots(x):
        even_sum = jnp.sum(jnp.where(is_odd, 0.0, x), axis=1, keepdims=True)
        odd_sum = jnp.sum(jnp.where(is_odd, x, 0.0), axis=1, keepdims=True)
        return 0.5 * even_sum, 0.5 * odd_sum

    apart = PAIR_LANE - EAST_PAIR_LANE
    w_halo = jnp.where(is_pair, jnp.where(is_odd, roll(west, apart + 1, 1), east), 0.0)
    c_halo = jnp.where(is_odd, roll(west, apart, 1), roll(east, -1, 1))
    w_own = roll(own_pairs[...], PAIR_LANE, 1)
    both = jnp.concatenate([w_halo, w_own], axis=0)
    both = jnp.dot(both, to_potential[...], precision=lax.Precision.HIGHEST, preferred_element_type=jnp.float32)
    p_halo, p_own = both[:ROWS], both[ROWS:]
    edges[0] = (-half * sign) * p_halo
    edges[1] = w_halo * (c_halo + (half * sign) * p_own)
    edges[2] = w_halo

    depth = flat[0]
    safe = depth + jnp.where(depth > 0.0, 0.0, 1.0)
    to_e, to_w = dots(w_own * p_halo)
    force_u = flat[1] + jnp.where(lane == COLS - 1, -to_e, jnp.where(lane == 0, to_w, 0.0)) / safe

    sides = [roll(jnp.where(lane // HALO == f, east, west), -HALO * f, 1) for f in range(6)]
    sides[1] = jnp.where(lane == HALO, roll(east, HALO - PAIR_END, 1), sides[1])
    at = COLS - HALO - 1
    sides[1] = jnp.where(lane == at, roll(west, at - (PAIR_END - HALO), 1), sides[1])
    safe = sides[0] + jnp.where(sides[0] > 0.0, 0.0, 1.0)
    to_e, to_w = dots(w_halo * p_own)
    sides[4] = sides[4] + jnp.where(lane == 0, to_e, jnp.where(lane == COLS - 1, -to_w, 0.0)) / safe
    sides[0] = jnp.where((lane == HALO) | (lane == at), 1.0, sides[0])

    for f, field in enumerate((depth, flat[6], flat[7], flat[5], force_u, flat[2])):
        ext[f, :, :COLS] = field
        ext[f, :, COLS:] = sides[f]

    lane12 = lane_index((LAYERS, COLS))
    lane16 = lane_index((HALO, COLS))

    def weight_rows(msg, w_at):
        msg[LAT_W : LAT_W + LAYERS, :] = own_a[w_at : w_at + LAYERS, :]
        beside_e = jnp.where(even_lon, got_a[w_at : w_at + LAYERS, :], got_b[w_at : w_at + LAYERS, :])
        beside_w = jnp.where(even_lon, got_b[w_at : w_at + LAYERS, :], got_a[w_at : w_at + LAYERS, :])
        beside = roll(jnp.where(lane12 < HALO, beside_e, beside_w), HALO + 64, 1)
        held = msg[LAT_SIDE + HALO : LAT_SIDE + HALO + LAYERS, :]
        msg[LAT_SIDE + HALO : LAT_SIDE + HALO + LAYERS, :] = jnp.where(lane12 // 32 == 2, beside, held)

    def lat_message(msg, north):
        start, w_at = (ROWS - HALO, W_TOP) if north else (0, W_BOTTOM)
        edge, c_at, v_at = (own_a, C_TOP, V_TOP) if north else (own_rows, 0, V_BOTTOM)
        packed = [jnp.zeros((HALO, COLS), jnp.float32)] * 2
        for f in range(6):
            msg[HALO * f : HALO * (f + 1), :] = ext[f, start : start + HALO, :COLS]
            side = roll(ext[f, start : start + HALO, COLS:], HALO + 32 * (f % 4), 1)
            packed[f // 4] = jnp.where(lane16 // 32 == f % 4, side, packed[f // 4])
        msg[LAT_SIDE : LAT_SIDE + HALO, :] = packed[0]
        msg[LAT_SIDE + HALO :, :] = packed[1]
        weight_rows(msg, w_at)
        msg[LAT_C : LAT_C + LAYERS, :] = edge[c_at : c_at + LAYERS, :]
        msg[LAT_V : LAT_V + 1, :] = edge[v_at : v_at + 1, :]
        msg[LAT_V + 1 : LAT_SIDE, :] = jnp.zeros((LAT_SIDE - LAT_V - 1, COLS), jnp.float32)

    at_top = lat == lax.axis_size("lat") - 1
    msg_y[LAT_SIDE + HALO :, :] = jnp.zeros((HALO, COLS), jnp.float32)

    @pl.when(even_lat)
    def _():
        lat_message(msg_x, True)
        lat_message(msg_f, False)
        weight_rows(msg_y, W_BOTTOM)

    @pl.when(jnp.logical_not(even_lat))
    def _():
        lat_message(msg_x, False)
        weight_rows(msg_y, W_TOP)

    @pl.when(jnp.logical_not(even_lat) & jnp.logical_not(at_top))
    def _():
        lat_message(msg_f, True)

    @pl.when(at_top)
    def _():
        lane8 = lane_index((8, COLS))
        row8 = row_index((8, COLS))
        offset = jnp.broadcast_to(g_rows[LAYERS + 1 : LAYERS + 2, :].astype(jnp.int32), (8, COLS))
        source = (offset - lane8) & (COLS - 1)
        taker = source
        block = (COLS + offset - taker) >> 7
        side_block = jnp.where(taker < HALO, offset - taker, 2 * COLS + offset - taker) >> 7

        def gather(x, index, axis):
            return jnp.take_along_axis(x, index, axis=axis, mode="promise_in_bounds")

        def window(w_tile, o_tile, e_tile):
            main = jnp.where(block == 0, w_tile, jnp.where(block == 1, o_tile, e_tile))
            side = jnp.where(side_block == 0, w_tile, jnp.where(side_block == 1, o_tile, e_tile))
            return gather(main, source, 1), gather(side, source, 1)

        def tiles(at):
            on_e = jnp.where(even_lon, got_a[at : at + 8, :], got_b[at : at + 8, :])
            on_w = jnp.where(even_lon, got_b[at : at + 8, :], got_a[at : at + 8, :])
            return on_w, own_a[at : at + 8, :], on_e

        packed = {}

        def pack(at, group, x):
            x = roll(x, HALO + 32 * group, 1)
            packed[at] = jnp.where(lane8 // 32 == group, x, packed[at]) if at in packed else x

        for f in range(6):
            sign = 1.0 if f in (0, 3) else -1.0
            for t in range(2):
                at = ROWS - 8 * (t + 1)
                mine = ext[f, at : at + 8, :COLS]
                side = ext[f, at : at + 8, COLS:]
                on_w, _, on_e = tiles(TOP_ROW + 8 * f)
                on_e = jnp.where(lane8 < HALO, side, roll(on_e, -48 if t == 0 else 16, 1))
                on_w = jnp.where(lane8 >= COLS - HALO, side, roll(on_w, -16 if t == 0 else 48, 1))
                main, beside = window(on_w, mine, on_e)
                msg_f[HALO * f + 8 * t : HALO * f + 8 * (t + 1), :] = sign * gather(main, 7 - row8, 0)
                pack(LAT_SIDE + HALO * (f // 4) + 8 * t, f % 4, sign * gather(beside, 7 - row8, 0))
        for t in range(3):
            main, beside = window(*tiles(W_TOP + 8 * t))
            sign = jnp.where(row8 + 8 * t < LAYERS, 1.0, -1.0)
            msg_f[LAT_W + 8 * t : LAT_W + 8 * (t + 1), :] = sign * main
            if t < 2:
                pack(LAT_SIDE + HALO + 8 * t, 2, beside)
        main, _ = window(*tiles(V_TOP))
        msg_f[LAT_V : LAT_V + 8, :] = -main
        for at, x in packed.items():
            msg_f[at : at + 8, :] = x


def third_kernel(
    g_rows, tail_u, tail_v, weight, th, floor, flat, cor_ref, edges, ext, own_x, own_y, own_f, got_x, got_f_hbm,
    new_u_hbm, new_v_hbm, new_th_hbm, new_lev_hbm, mean_u_hbm, mean_v_hbm,
    far, level_pad, v_pad, state, fixed, pots, seam_w, seam_rows, new_u, new_v, new_th, flux_v_pad, planes,
    sems, plane_sems, far_sem,
):
    lat = lax.axis_index("lat")
    even = lax.rem(lat, 2) == 0
    at_top = lat == lax.axis_size("lat") - 1
    at_bottom = lat == 0

    far_copies = []
    for n in range(FAR_PARTS):
        part = pl.ds(n * (LAT_ROWS // FAR_PARTS), LAT_ROWS // FAR_PARTS)
        far_copies.append(pltpu.make_async_copy(got_f_hbm.at[part], far.at[part], far_sem.at[n]))
    for copy in far_copies:
        copy.start()
    inner = slice(HALO, HALO + ROWS)

    def place(at, count, depth, u, v, level, force_u, force_v, rate):
        rows = pl.ds(at, count)
        cor = cor_ref[rows, :]
        cor = jnp.concatenate([cor, cor], axis=1)
        wet = jnp.where(depth > 0.0, 1.0, 0.0)
        fixed[0, rows, :] = depth
        fixed[1, rows, :] = wet * (1.0 - barotropic_step * bottom_drag)
        fixed[2, rows, :] = wet * (barotropic_step * cor)
        fixed[3, rows, :] = wet * (barotropic_step * force_u)
        fixed[4, rows, :] = wet * (barotropic_step * force_v)
        fixed[5, rows, :] = wet * (0.5 * barotropic_step)
        fixed[6, rows, :] = jnp.full((count, WIDE), rate, jnp.float32)
        state[0, rows, :] = u
        state[1, rows, :] = v
        level_pad[pl.ds(at + 8, count), :] = level

    place(HALO, ROWS, *(ext[f] for f in range(6)), 0.5 * barotropic_step)

    def strip(got, mine, slot, is_north, keep):
        at = pl.multiple_of(jnp.where(is_north, HALO + ROWS, 0), HALO)
        sign = jnp.where(is_north, 1.0, -1.0)
        fields = []
        for f in range(6):
            main = got[HALO * f : HALO * (f + 1), :]
            side = got[LAT_SIDE + HALO * (f // 4) : LAT_SIDE + HALO * (f // 4 + 1), :]
            side = roll(side, -HALO - 32 * (f % 4), 1)
            fields.append(jnp.concatenate([main, side], axis=1))
        if keep is not None:
            fields = [jnp.where(keep, field, 0.0) for field in fields]
        rate = 0.5 * barotropic_step
        place(at, HALO, *fields, rate if keep is None else jnp.where(keep, rate, 0.0))
        v_row = got[LAT_V : LAT_V + 1, :]
        if keep is not None:
            v_row = jnp.where(keep, v_row, 0.0)
        v_rows = pl.ds(pl.multiple_of(jnp.where(is_north, 8 + FULL, 0), 8), 8)
        v_pad[v_rows, :COLS] = jnp.broadcast_to(v_row, (8, COLS))
        v_pad[v_rows, COLS:] = jnp.zeros((8, COLS), jnp.float32)
        for n, ref in enumerate((mine, got)):
            w = ref[LAT_W : LAT_W + LAYERS, :]
            side = roll(ref[LAT_SIDE + HALO : LAT_SIDE + HALO + LAYERS, :], -HALO - 64, 1)
            if n == 1 and keep is not None:
                w, side = jnp.where(keep, w, 0.0), jnp.where(keep, side, 0.0)
            seam_w[n, :LAYERS, :COLS] = w
            seam_w[n, :LAYERS, COLS:] = side
        sum_o, sum_s, pot_o, pot_s, to_o, to_s = (jnp.zeros((1, WIDE), jnp.float32) for _ in range(6))
        for k in range(LAYERS):
            wo, ws = seam_w[0, k : k + 1, :], seam_w[1, k : k + 1, :]
            g = jnp.concatenate([g_rows[k : k + 1, :]] * 2, axis=1)
            sum_o, sum_s = sum_o + wo, sum_s + ws
            pot_o, pot_s = pot_o + g * sum_o, pot_s + g * sum_s
            to_o = to_o + wo * pot_s
            to_s = to_s + ws * pot_o
            pots[0, k : k + 1, :] = pot_o[:, :COLS]
            pots[1, k : k + 1, :] = pot_s[:, :COLS]
        safe_o = sum_o + jnp.where(sum_o > 0.0, 0.0, 1.0)
        safe_s = sum_s + jnp.where(sum_s > 0.0, 0.0, 1.0)
        scale = 0.5 * barotropic_step * sign
        row8 = row_index((8, WIDE))
        own_rows = pl.ds(pl.multiple_of(jnp.where(is_north, HALO + ROWS - 8, HALO), 8), 8)
        strip_rows = pl.ds(pl.multiple_of(jnp.where(is_north, HALO + ROWS, HALO - 8), 8), 8)
        last, first = row8 == jnp.where(is_north, 7, 0), row8 == jnp.where(is_north, 0, 7)
        fixed[4, own_rows, :] = fixed[4, own_rows, :] - jnp.where(last, scale * to_o / safe_o, 0.0)
        fixed[4, strip_rows, :] = fixed[4, strip_rows, :] + jnp.where(first, scale * to_s / safe_s, 0.0)
        side = jnp.where(is_north, 0, 3)
        w = seam_w[1, :LAYERS, :COLS]
        seam_rows[side, :LAYERS, :] = (-half * sign) * pots[1, :LAYERS, :]
        seam_rows[side + 1, :LAYERS, :] = w * (got[LAT_C : LAT_C + LAYERS, :] + (half * sign) * pots[0, :LAYERS, :])
        seam_rows[side + 2, :LAYERS, :] = w

    strip(got_x, own_x, 0, even, None)
    for copy in far_copies:
        copy.wait()

    far[...] = jnp.where(at_top & (g_rows[LAYERS + 2 : LAYERS + 3, :] > 0.0), own_f[...], far[...])
    strip(far, own_y, 1, jnp.logical_not(even), jnp.logical_not(at_bottom))

    def blocks(skip):
        edges_at = list(range(skip, FULL - skip, 8)) + [FULL - skip]
        return list(zip(edges_at[:-1], edges_at[1:]))

    for begin, end in blocks(0):
        v_pad[8 + begin : 8 + end, :] = fixed[0, begin:end, :] * state[1, begin:end, :]
    for step in range(SUBSTEPS):
        skip = (2 * step) // 8 * 8
        for begin, end in blocks(skip):
            trans_u = fixed[0, begin:end, :] * state[0, begin:end, :]
            dv = v_pad[9 + begin : 9 + end, :] - v_pad[7 + begin : 7 + end, :]
            du = pltpu.roll(trans_u, WIDE - 1, 1) - pltpu.roll(trans_u, 1, 1)
            held = level_pad[8 + begin : 8 + end, :]
            level_pad[8 + begin : 8 + end, :] = held - fixed[6, begin:end, :] * (du + dv)
        for begin, end in blocks(skip):
            u, v = state[0, begin:end, :], state[1, begin:end, :]
            level = level_pad[8 + begin : 8 + end, :]
            dy = level_pad[9 + begin : 9 + end, :] - level_pad[7 + begin : 7 + end, :]
            dx = pltpu.roll(level, WIDE - 1, 1) - pltpu.roll(level, 1, 1)
            keep, turn, slope = fixed[1, begin:end, :], fixed[2, begin:end, :], fixed[5, begin:end, :]
            next_u = keep * u + turn * v + fixed[3, begin:end, :] - slope * dx
            next_v = keep * v - turn * u + fixed[4, begin:end, :] - slope * dy
            state[0, begin:end, :] = next_u
            state[1, begin:end, :] = next_v
            state[2, begin:end, :] = next_u if step == 0 else state[2, begin:end, :] + next_u
            state[3, begin:end, :] = next_v if step == 0 else state[3, begin:end, :] + next_v
            v_pad[8 + begin : 8 + end, :] = fixed[0, begin:end, :] * next_v
    planes[0] = level_pad[8 + HALO : 8 + HALO + ROWS, :COLS]
    planes[1] = state[2, inner, :COLS] * (1.0 / SUBSTEPS)
    planes[2] = state[3, inner, :COLS] * (1.0 / SUBSTEPS)
    plane_copies = [
        pltpu.make_async_copy(planes.at[n], out, plane_sems.at[n])
        for n, out in enumerate((new_lev_hbm, mean_u_hbm, mean_v_hbm))
    ]
    for copy in plane_copies:
        copy.start()

    to_force = baroclinic_step / barotropic_step

    def rest(n, rows, lanes):
        return state[2 + n, rows, lanes] * (1.0 / SUBSTEPS) - to_force * fixed[3 + n, rows, lanes]

    main, beside = slice(0, COLS), slice(COLS, WIDE)
    lane = lane_index((ROWS, COLS))
    row = row_index((ROWS, COLS))
    is_e, is_w = lane == COLS - 1, lane == 0
    base_u = rest(0, inner, main) - flat[3]
    base_v = rest(1, inner, main) - flat[4]
    side_u = rest(0, inner, beside)
    rest_e = jnp.sum(jnp.where(is_w, side_u, 0.0), axis=1, keepdims=True)
    rest_w = jnp.sum(jnp.where(is_e, side_u, 0.0), axis=1, keepdims=True)
    pair_flux = edges[1] + edges[2] * jnp.where(lane % 2 == 0, rest_e, rest_w)
    pair_fix = edges[0]
    rest_n = rest(1, slice(HALO + ROWS, HALO + ROWS + 1), main)
    rest_s = rest(1, slice(HALO - 1, HALO), main)
    for side, line in ((0, rest_n), (3, rest_s)):
        seam_rows[side + 1, :LAYERS, :] = seam_rows[side + 1, :LAYERS, :] + seam_rows[side + 2, :LAYERS, :] * line
    levels = jnp.where(floor[0] > 0, floor[1], 0)
    copies = []
    parts = ((0, 4), (4, 8), (8, 11), (11, 12))
    lanes16 = lane_index((32, COLS))
    rows16 = row_index((32, COLS))
    is_e, is_w = lanes16 == COLS - 1, lanes16 == 0
    is_edge = is_e | is_w
    for k in range(LAYERS):
        shift = COLS - 1 - PAIR_LANE - 2 * k
        flux_v_pad[k, 7:8, :] = seam_rows[4, k : k + 1, :]
        flux_v_pad[k, 8 + ROWS : 9 + ROWS, :] = seam_rows[1, k : k + 1, :]
        for begin in range(0, ROWS, 32):
            at = slice(begin, begin + 32)
            w = weight[k, at, :]
            mask = levels[at] > k
            rest_u = tail_u[k, at, :] + base_u[at] + jnp.where(is_edge, roll(pair_fix[at], shift, 1), 0.0)
            rest_v = tail_v[k, at, :] + base_v[at]
            if begin == 0:
                rest_v = rest_v + jnp.where(rows16 == 0, seam_rows[3, k : k + 1, :], 0.0)
            if begin == ROWS - 32:
                rest_v = rest_v + jnp.where(rows16 == 32 - 1, seam_rows[0, k : k + 1, :], 0.0)
            out_u = jnp.where(mask, rest_u, 0.0)
            out_v = jnp.where(mask, rest_v, 0.0)
            new_u[k, at, :] = out_u
            new_v[k, at, :] = out_v
            flux_u = w * out_u
            flux_v_pad[k, 8 + begin : 8 + begin + 32, :] = w * out_v
            halo = roll(pair_flux[at], shift, 1)
            east = jnp.where(is_e, halo, pltpu.roll(flux_u, COLS - 1, 1))
            west = jnp.where(is_w, halo, pltpu.roll(flux_u, 1, 1))
            new_th[k, at, :] = th[k, at, :] - half * (east - west)
        north = flux_v_pad[k, 9 : 9 + ROWS, :]
        south = flux_v_pad[k, 7 : 7 + ROWS, :]
        new_th[k] = new_th[k] - half * (north - south)
        for part, (begin, end) in enumerate(parts):
            if k == end - 1:
                rows = pl.ds(begin, end - begin)
                for n, (held, out) in enumerate(((new_u, new_u_hbm), (new_v, new_v_hbm), (new_th, new_th_hbm))):
                    copy = pltpu.make_async_copy(held.at[rows], out.at[rows], sems.at[n, part])
                    copy.start()
                    copies.append(copy)
    for copy in copies + plane_copies:
        copy.wait()


def vmem(count):
    return [pl.BlockSpec(memory_space=pltpu.VMEM)] * count


def hbm(count):
    return [pl.BlockSpec(memory_space=pltpu.HBM)] * count


def in_hbm(*arrays):
    return tuple(pltpu.with_memory_space_constraint(x, pltpu.HBM) for x in arrays)


def f32(*shape):
    return jax.ShapeDtypeStruct(shape, jnp.float32)


PARAMS = pltpu.CompilerParams(vmem_limit_bytes=40 * 2**20)


def local(lu, lv, th, lev, u, v, land, bottom, fold_map, gravity):
    lons, lats = lax.axis_size("lon"), lax.axis_size("lat")
    lon_msg, lat_msg = f32(LON_ROWS, COLS), f32(LAT_ROWS, COLS)
    layers, plane = f32(LAYERS, ROWS, COLS), f32(ROWS, COLS)
    held = pltpu.VMEM((LAYERS, ROWS, COLS), jnp.float32)
    total = lons * COLS
    pivot = fold_map[0] + lax.axis_index("lon") * COLS
    shift = jnp.mod(pivot - COLS // 2, total) // COLS

    msg_a, msg_b, own_pairs, own_rows, flat, cor, g_rows, to_potential, tail_u, tail_v, weight, th, floor = pl.pallas_call(
        first_kernel,
        out_shape=(
            lon_msg, lon_msg, plane, f32(16, COLS), f32(8, ROWS, COLS), f32(FULL, COLS), f32(16, COLS), f32(COLS, COLS),
            layers, layers, layers, layers,
            jax.ShapeDtypeStruct((2, ROWS, COLS), jnp.int32),
        ),
        in_specs=hbm(10),
        out_specs=vmem(13),
        scratch_shapes=[
            held,
            held,
            pltpu.SMEM((LAYERS,), jnp.float32),
            pltpu.SMEM((COLS,), jnp.int32),
            pltpu.SemaphoreType.DMA((10,)),
        ],
        compiler_params=PARAMS,
        name="edges",
    )(*in_hbm(gravity, lu, lv, th, lev, u, v, land, bottom, fold_map))

    got_b = lax.ppermute(msg_b, "lon", [(i, (((i + 1) ^ 1) - 1) % lons) for i in range(lons)])
    got_a = lax.ppermute(msg_a, "lon", [(i, i ^ 1) for i in range(lons)])
    got_a, got_b, shift = lax.optimization_barrier((got_a, got_b, shift))

    ext, edges, msg_x, msg_y, msg_f = pl.pallas_call(
        second_kernel,
        out_shape=(f32(6, ROWS, WIDE), f32(3, ROWS, COLS), lat_msg, lat_msg, lat_msg),
        in_specs=vmem(8),
        out_specs=vmem(5),
        compiler_params=PARAMS,
        name="extend",
    )(g_rows, to_potential, flat, own_pairs, own_rows, msg_a, got_a, got_b)

    got_x = lax.ppermute(msg_x, "lat", [(i, i ^ 1) for i in range(lats)])
    top = lats - 1
    rows = [(b * lats + i, b * lats + ((i + 1) ^ 1) - 1) for b in range(lons) for i in range(1, top)]
    rows += [(b * lats, (b ^ 1) * lats) for b in range(lons)]

    def exchange(q):
        pairs = list(rows)
        for b in range(lons):
            source = (q - b) % lons
            source = (b + lons // 2) % lons if source == b else source
            pairs.append((source * lats + top, b * lats + top))
        return lambda x: lax.ppermute(x, ("lon", "lat"), pairs)

    got_f = lax.switch(shift, [exchange(q) for q in range(lons)], msg_f)

    padded = pltpu.VMEM((FULL + 16, WIDE), jnp.float32)
    rows16 = pltpu.VMEM((6, 16, COLS), jnp.float32)
    return pl.pallas_call(
        third_kernel,
        out_shape=(layers, layers, layers, plane, plane, plane),
        in_specs=vmem(14) + hbm(1),
        out_specs=hbm(6),
        scratch_shapes=[
            pltpu.VMEM((LAT_ROWS, COLS), jnp.float32),
            padded,
            padded,
            pltpu.VMEM((4, FULL, WIDE), jnp.float32),
            pltpu.VMEM((7, FULL, WIDE), jnp.float32),
            rows16,
            pltpu.VMEM((2, 16, WIDE), jnp.float32),
            rows16,
            held,
            held,
            held,
            pltpu.VMEM((LAYERS, ROWS + 16, COLS), jnp.float32),
            pltpu.VMEM((3, ROWS, COLS), jnp.float32),
            pltpu.SemaphoreType.DMA((3, 4)),
            pltpu.SemaphoreType.DMA((3,)),
            pltpu.SemaphoreType.DMA((FAR_PARTS,)),
        ],
        compiler_params=PARAMS,
        name="advance",
    )(g_rows, tail_u, tail_v, weight, th, floor, flat, cor, edges, ext, msg_x, msg_y, msg_f, got_x, *in_hbm(got_f))


def solution(mesh):
    layered, plane = P(None, "lat", "lon"), P("lat", "lon")
    return jax.shard_map(
        local,
        mesh=mesh,
        in_specs=(layered,) * 3 + (plane,) * 5 + (P("lon"), P()),
        out_specs=(layered,) * 3 + (plane,) * 3,
        check_vma=False,
    )
```

```python
import jax
import jax.numpy as jnp
from jax import lax
from jax.experimental import pallas as pl
from jax.experimental.pallas import tpu as pltpu
from jax.sharding import PartitionSpec as P

SUBSTEPS = 8
LAYERS = 12
TOTAL_ROWS = 512
ROWS, COLS = 64, 128
HALO = 16

barotropic_step = 0.45
baroclinic_step = 0.1
coriolis_scale = 0.3
bottom_drag = 0.05

PAIR_LANE, EAST_PAIR_LANE = 96, 80
PAIR_END = PAIR_LANE + 2 * LAYERS
TOP_ROW, W_TOP, C_TOP, V_TOP, W_BOTTOM, LON_ROWS = 64, 112, 124, 136, 137, 152
V_BOTTOM = LAYERS
LAT_W, LAT_C, LAT_V, LAT_SIDE, LAT_ROWS = 96, 108, 120, 128, 160
FULL = ROWS + 2 * HALO
WIDE = 2 * COLS
half = 0.5 * baroclinic_step
FAR_PARTS = 2


def lane_index(shape):
    return lax.broadcasted_iota(jnp.int32, shape, 1)


def row_index(shape):
    return lax.broadcasted_iota(jnp.int32, shape, 0)


def roll(x, shift, axis):
    shift = shift % x.shape[axis]
    return x if shift == 0 else pltpu.roll(x, shift, axis)


def first_kernel(
    gravity_hbm, lu_hbm, lv_hbm, th_hbm, lev_hbm, u_hbm, v_hbm, land_hbm, bottom_hbm, fold_hbm,
    msg_a, msg_b, own_pairs, own_rows, flat, cor_out, g_rows, to_potential, tail_u, tail_v, weight, th, floor,
    lu, lv, gravity, fold, sems,
):
    pairs = (
        (th_hbm, th), (land_hbm, floor.at[0]), (bottom_hbm, floor.at[1]), (gravity_hbm, gravity), (lu_hbm, lu),
        (lv_hbm, lv), (lev_hbm, flat.at[5]), (u_hbm, flat.at[6]), (v_hbm, flat.at[7]),
        (fold_hbm, fold),
    )
    copies = [pltpu.make_async_copy(a, b, sems.at[n]) for n, (a, b) in enumerate(pairs)]
    for copy in copies:
        copy.start()
    lon, lat = lax.axis_index("lon"), lax.axis_index("lat")
    even = lax.rem(lon, 2) == 0
    rows = (row_index((FULL, COLS)) + (lat * ROWS - HALO)).astype(jnp.float32)
    cor_all = -coriolis_scale * jnp.cos((rows + 0.5) * (jnp.pi / TOTAL_ROWS))
    cor_out[...] = cor_all
    cor = cor_all[HALO : HALO + ROWS]
    lane = lane_index((ROWS, COLS))
    row = row_index((ROWS, COLS))
    copies[3].wait()
    line = (lane_index((COLS, COLS)) - PAIR_LANE) >> 1
    at = (row_index((COLS, COLS)) - PAIR_LANE) >> 1
    upper, lower = jnp.zeros((COLS, COLS), jnp.float32), jnp.zeros((COLS, COLS), jnp.float32)
    total = 0.0
    for k in range(LAYERS):
        g_rows[k : k + 1, :] = jnp.full((1, COLS), gravity[k], jnp.float32)
        lower = jnp.where(at == k, total, lower)
        total = total + gravity[k]
        upper = jnp.where(line == k, total, upper)
    used = (at >= 0) & (at <= line) & (line < LAYERS) & (((lane_index((COLS, COLS)) - row_index((COLS, COLS))) & 1) == 0)
    to_potential[...] = jnp.where(used, upper - lower, 0.0)
    for copy in copies[:3] + copies[4:]:
        copy.wait()
    wet = floor[0].astype(jnp.float32)
    bot = floor[1]
    lev, u, v = flat[5], flat[6], flat[7]
    zero = jnp.zeros((ROWS, COLS), jnp.float32)
    g_rows[LAYERS : LAYERS + 1, :] = jnp.zeros((1, COLS), jnp.float32)
    offset = 64 + ((fold[0] + 64) & (COLS - 1))
    g_rows[LAYERS + 1 : LAYERS + 2, :] = jnp.full((1, COLS), offset, jnp.int32).astype(jnp.float32)
    lons = lax.axis_size("lon")
    apart = lax.rem((fold[0] + lons * COLS - 64) // COLS - lon + lons, lons)
    g_rows[LAYERS + 2 : LAYERS + 3, :] = jnp.full((1, COLS), jnp.where(apart == 0, 1.0, 0.0), jnp.float32)
    g_rows[LAYERS + 3 :, :] = jnp.zeros((1, COLS), jnp.float32)

    depth, potential = zero, zero
    grad_u, grad_v, sum_u, sum_v = zero, zero, zero, zero
    for k in range(LAYERS):
        w = jnp.where(bot > k, wet, 0.0) * th[k]
        depth = depth + w
        potential = potential + gravity[k] * depth
        right = jnp.where(lane == COLS - 1, 0.0, roll(potential, -1, 1))
        left = jnp.where(lane == 0, 0.0, roll(potential, 1, 1))
        above = jnp.where(row == ROWS - 1, 0.0, roll(potential, -1, 0))
        below = jnp.where(row == 0, 0.0, roll(potential, 1, 0))
        du = 0.5 * (left - right)
        dv = 0.5 * (below - above)
        grad_u = grad_u + w * du
        grad_v = grad_v + w * dv
        sum_u = sum_u + w * lu[k]
        sum_v = sum_v + w * lv[k]
        rest_u = lu[k] + baroclinic_step * (du + cor * lv[k])
        rest_v = lv[k] + baroclinic_step * (dv - cor * lu[k])
        tail_u[k] = rest_u
        tail_v[k] = rest_v
        weight[k] = w
        for msg in (msg_a, msg_b):
            msg[W_TOP + k : W_TOP + k + 1, :] = w[ROWS - 1 :]
            msg[W_BOTTOM + k : W_BOTTOM + k + 1, :] = w[:1]
            msg[C_TOP + k : C_TOP + k + 1, :] = rest_v[ROWS - 1 :]
        own_rows[k : k + 1, :] = rest_v[:1]
    edge_w, edge_c = zero, zero
    for k in range(LAYERS):
        here = lane >> 1 == k
        edge_w = jnp.where(here, roll(weight[k], 2 * k + 1, 1), edge_w)
        edge_c = jnp.where(here, roll(tail_u[k], 2 * k + 1, 1), edge_c)
    own_pairs[...] = edge_w
    inverse = 1.0 / (depth + (1.0 - wet))
    column_u = sum_u * inverse
    column_v = sum_v * inverse
    force_u = grad_u * inverse + cor * column_v
    force_v = grad_v * inverse - cor * column_u
    fields = (depth, u, v, lev, force_u, force_v)
    flat[0] = depth
    flat[1] = force_u
    flat[2] = force_v
    flat[3] = column_u
    flat[4] = column_v
    transport_u = depth * u
    transport_v = depth * v
    is_odd = lane % 2 == 1
    west, east = zero, zero
    for f, field in enumerate(fields):
        moved = roll(field, HALO * f, 1)
        west = jnp.where(lane // HALO == f, moved, west)
        east = jnp.where(lane // HALO == (f - 1) % 8, moved, east)
    in_west = (lane >= PAIR_LANE) & (lane < PAIR_END)
    in_east = (lane >= EAST_PAIR_LANE) & (lane < EAST_PAIR_LANE + 2 * LAYERS)

    def pairs_of(w, rest, edge):
        column = jnp.sum(jnp.where(lane == edge, column_u, 0.0), axis=1, keepdims=True)
        return jnp.where(is_odd, rest - column, w)

    west = jnp.where(in_west, pairs_of(roll(edge_w, PAIR_LANE - 1, 1), roll(edge_c, PAIR_LANE, 1), 0), west)
    west = jnp.where(lane == PAIR_END, roll(transport_u, PAIR_END - HALO, 1), west)
    at = EAST_PAIR_LANE
    east = jnp.where(in_east, pairs_of(roll(edge_w, at, 1), roll(edge_c, at + 1, 1), COLS - 1), east)
    at = PAIR_END - HALO
    east = jnp.where(lane == at, roll(transport_u, at - (COLS - 1 - HALO), 1), east)
    msg_a[:ROWS] = jnp.where(even, east, west)
    msg_b[:ROWS] = jnp.where(even, west, east)
    low = lane_index((8, COLS)) < 64
    for f, field in enumerate(fields):
        lower, upper = field[ROWS - HALO : ROWS - 8], field[ROWS - 8 :]
        west = jnp.where(low, roll(lower, -16, 1), roll(upper, 48, 1))
        east = jnp.where(low, roll(lower, -48, 1), roll(upper, 16, 1))
        msg_a[TOP_ROW + 8 * f : TOP_ROW + 8 * (f + 1)] = jnp.where(even, east, west)
        msg_b[TOP_ROW + 8 * f : TOP_ROW + 8 * (f + 1)] = jnp.where(even, west, east)
    for msg in (msg_a, msg_b):
        msg[C_TOP : C_TOP + LAYERS] = msg[C_TOP : C_TOP + LAYERS] - column_v[ROWS - 1 :]
        msg[V_TOP : V_TOP + 1] = transport_v[ROWS - 1 - HALO : ROWS - HALO]
        msg[W_BOTTOM + LAYERS :] = jnp.zeros((LON_ROWS - W_BOTTOM - LAYERS, COLS), jnp.float32)
    own_rows[:LAYERS] = own_rows[:LAYERS] - column_v[:1]
    own_rows[V_BOTTOM : V_BOTTOM + 1] = transport_v[HALO : HALO + 1]
    own_rows[V_BOTTOM + 1 :] = jnp.zeros((16 - V_BOTTOM - 1, COLS), jnp.float32)


def second_kernel(g_rows, to_potential, flat, own_pairs, own_rows, own_a, got_a, got_b, ext, edges, msg_x, msg_y, msg_f):
    lon, lat = lax.axis_index("lon"), lax.axis_index("lat")
    even_lon = lax.rem(lon, 2) == 0
    even_lat = lax.rem(lat, 2) == 0
    lane = lane_index((ROWS, COLS))
    is_pair = (lane >= PAIR_LANE) & (lane < PAIR_END)
    is_odd = lane % 2 == 1
    sign = jnp.where(is_odd, -1.0, 1.0)
    east = jnp.where(even_lon, got_a[:ROWS], got_b[:ROWS])
    west = jnp.where(even_lon, got_b[:ROWS], got_a[:ROWS])

    def dots(x):
        even_sum = jnp.sum(jnp.where(is_odd, 0.0, x), axis=1, keepdims=True)
        odd_sum = jnp.sum(jnp.where(is_odd, x, 0.0), axis=1, keepdims=True)
        return 0.5 * even_sum, 0.5 * odd_sum

    apart = PAIR_LANE - EAST_PAIR_LANE
    w_halo = jnp.where(is_pair, jnp.where(is_odd, roll(west, apart + 1, 1), east), 0.0)
    c_halo = jnp.where(is_odd, roll(west, apart, 1), roll(east, -1, 1))
    w_own = roll(own_pairs[...], PAIR_LANE, 1)
    both = jnp.concatenate([w_halo, w_own], axis=0)
    both = jnp.dot(both, to_potential[...], precision=lax.Precision.HIGHEST, preferred_element_type=jnp.float32)
    p_halo, p_own = both[:ROWS], both[ROWS:]
    edges[0] = (-half * sign) * p_halo
    edges[1] = w_halo * (c_halo + (half * sign) * p_own)
    edges[2] = w_halo

    depth = flat[0]
    safe = depth + jnp.where(depth > 0.0, 0.0, 1.0)
    to_e, to_w = dots(w_own * p_halo)
    force_u = flat[1] + jnp.where(lane == COLS - 1, -to_e, jnp.where(lane == 0, to_w, 0.0)) / safe

    sides = [roll(jnp.where(lane // HALO == f, east, west), -HALO * f, 1) for f in range(6)]
    sides[1] = jnp.where(lane == HALO, roll(east, HALO - PAIR_END, 1), sides[1])
    at = COLS - HALO - 1
    sides[1] = jnp.where(lane == at, roll(west, at - (PAIR_END - HALO), 1), sides[1])
    safe = sides[0] + jnp.where(sides[0] > 0.0, 0.0, 1.0)
    to_e, to_w = dots(w_halo * p_own)
    sides[4] = sides[4] + jnp.where(lane == 0, to_e, jnp.where(lane == COLS - 1, -to_w, 0.0)) / safe
    sides[0] = jnp.where((lane == HALO) | (lane == at), 1.0, sides[0])

    for f, field in enumerate((depth, flat[6], flat[7], flat[5], force_u, flat[2])):
        ext[f, :, :COLS] = field
        ext[f, :, COLS:] = sides[f]

    lane12 = lane_index((LAYERS, COLS))
    lane16 = lane_index((HALO, COLS))

    def lat_message(msg, north):
        start, w_at = (ROWS - HALO, W_TOP) if north else (0, W_BOTTOM)
        edge, c_at, v_at = (own_a, C_TOP, V_TOP) if north else (own_rows, 0, V_BOTTOM)
        packed = [jnp.zeros((HALO, COLS), jnp.float32)] * 2
        for f in range(6):
            msg[HALO * f : HALO * (f + 1), :] = ext[f, start : start + HALO, :COLS]
            side = roll(ext[f, start : start + HALO, COLS:], HALO + 32 * (f % 4), 1)
            packed[f // 4] = jnp.where(lane16 // 32 == f % 4, side, packed[f // 4])
        msg[LAT_SIDE : LAT_SIDE + HALO, :] = packed[0]
        msg[LAT_SIDE + HALO :, :] = packed[1]
        msg[LAT_W : LAT_W + LAYERS, :] = own_a[w_at : w_at + LAYERS, :]
        beside_e = jnp.where(even_lon, got_a[w_at : w_at + LAYERS, :], got_b[w_at : w_at + LAYERS, :])
        beside_w = jnp.where(even_lon, got_b[w_at : w_at + LAYERS, :], got_a[w_at : w_at + LAYERS, :])
        beside = roll(jnp.where(lane12 < HALO, beside_e, beside_w), HALO + 64, 1)
        held = msg[LAT_SIDE + HALO : LAT_SIDE + HALO + LAYERS, :]
        msg[LAT_SIDE + HALO : LAT_SIDE + HALO + LAYERS, :] = jnp.where(lane12 // 32 == 2, beside, held)
        msg[LAT_C : LAT_C + LAYERS, :] = edge[c_at : c_at + LAYERS, :]
        msg[LAT_V : LAT_V + 1, :] = edge[v_at : v_at + 1, :]
        msg[LAT_V + 1 : LAT_SIDE, :] = jnp.zeros((LAT_SIDE - LAT_V - 1, COLS), jnp.float32)

    @pl.when(even_lat)
    def _():
        lat_message(msg_x, True)
        lat_message(msg_y, False)

    @pl.when(jnp.logical_not(even_lat))
    def _():
        lat_message(msg_x, False)
        lat_message(msg_y, True)


    @pl.when(lat == lax.axis_size("lat") - 1)
    def _():
        lane8 = lane_index((8, COLS))
        row8 = row_index((8, COLS))
        offset = jnp.broadcast_to(g_rows[LAYERS + 1 : LAYERS + 2, :].astype(jnp.int32), (8, COLS))
        source = (offset - lane8) & (COLS - 1)
        taker = source
        block = (COLS + offset - taker) >> 7
        side_block = jnp.where(taker < HALO, offset - taker, 2 * COLS + offset - taker) >> 7

        def gather(x, index, axis):
            return jnp.take_along_axis(x, index, axis=axis, mode="promise_in_bounds")

        def window(w_tile, o_tile, e_tile):
            main = jnp.where(block == 0, w_tile, jnp.where(block == 1, o_tile, e_tile))
            side = jnp.where(side_block == 0, w_tile, jnp.where(side_block == 1, o_tile, e_tile))
            return gather(main, source, 1), gather(side, source, 1)

        def tiles(at):
            on_e = jnp.where(even_lon, got_a[at : at + 8, :], got_b[at : at + 8, :])
            on_w = jnp.where(even_lon, got_b[at : at + 8, :], got_a[at : at + 8, :])
            return on_w, own_a[at : at + 8, :], on_e

        packed = {}

        def pack(at, group, x):
            x = roll(x, HALO + 32 * group, 1)
            packed[at] = jnp.where(lane8 // 32 == group, x, packed[at]) if at in packed else x

        for f in range(6):
            sign = 1.0 if f in (0, 3) else -1.0
            for t in range(2):
                at = ROWS - 8 * (t + 1)
                mine = ext[f, at : at + 8, :COLS]
                side = ext[f, at : at + 8, COLS:]
                on_w, _, on_e = tiles(TOP_ROW + 8 * f)
                on_e = jnp.where(lane8 < HALO, side, roll(on_e, -48 if t == 0 else 16, 1))
                on_w = jnp.where(lane8 >= COLS - HALO, side, roll(on_w, -16 if t == 0 else 48, 1))
                main, beside = window(on_w, mine, on_e)
                msg_f[HALO * f + 8 * t : HALO * f + 8 * (t + 1), :] = sign * gather(main, 7 - row8, 0)
                pack(LAT_SIDE + HALO * (f // 4) + 8 * t, f % 4, sign * gather(beside, 7 - row8, 0))
        for t in range(3):
            main, beside = window(*tiles(W_TOP + 8 * t))
            sign = jnp.where(row8 + 8 * t < LAYERS, 1.0, -1.0)
            msg_f[LAT_W + 8 * t : LAT_W + 8 * (t + 1), :] = sign * main
            if t < 2:
                pack(LAT_SIDE + HALO + 8 * t, 2, beside)
        main, _ = window(*tiles(V_TOP))
        msg_f[LAT_V : LAT_V + 8, :] = -main
        for at, x in packed.items():
            msg_f[at : at + 8, :] = x

    @pl.when(lat != lax.axis_size("lat") - 1)
    def _():
        msg_f[...] = msg_y[...]


def third_kernel(
    g_rows, tail_u, tail_v, weight, th, floor, flat, cor_ref, edges, ext, own_x, own_y, own_f, got_x, got_f_hbm,
    new_u_hbm, new_v_hbm, new_th_hbm, new_lev_hbm, mean_u_hbm, mean_v_hbm,
    far, level_pad, v_pad, state, fixed, pots, seam_w, seam_rows, new_u, new_v, new_th, flux_v_pad, planes,
    sems, plane_sems, far_sem,
):
    lat = lax.axis_index("lat")
    even = lax.rem(lat, 2) == 0
    at_top = lat == lax.axis_size("lat") - 1
    at_bottom = lat == 0

    far_copies = []
    for n in range(FAR_PARTS):
        part = pl.ds(n * (LAT_ROWS // FAR_PARTS), LAT_ROWS // FAR_PARTS)
        far_copies.append(pltpu.make_async_copy(got_f_hbm.at[part], far.at[part], far_sem.at[n]))
    for copy in far_copies:
        copy.start()
    inner = slice(HALO, HALO + ROWS)

    def place(at, count, depth, u, v, level, force_u, force_v, rate):
        rows = pl.ds(at, count)
        cor = cor_ref[rows, :]
        cor = jnp.concatenate([cor, cor], axis=1)
        wet = jnp.where(depth > 0.0, 1.0, 0.0)
        fixed[0, rows, :] = depth
        fixed[1, rows, :] = wet * (1.0 - barotropic_step * bottom_drag)
        fixed[2, rows, :] = wet * (barotropic_step * cor)
        fixed[3, rows, :] = wet * (barotropic_step * force_u)
        fixed[4, rows, :] = wet * (barotropic_step * force_v)
        fixed[5, rows, :] = wet * (0.5 * barotropic_step)
        fixed[6, rows, :] = jnp.full((count, WIDE), rate, jnp.float32)
        state[0, rows, :] = u
        state[1, rows, :] = v
        level_pad[pl.ds(at + 8, count), :] = level

    place(HALO, ROWS, *(ext[f] for f in range(6)), 0.5 * barotropic_step)

    def strip(got, mine, slot, is_north, keep):
        at = pl.multiple_of(jnp.where(is_north, HALO + ROWS, 0), HALO)
        sign = jnp.where(is_north, 1.0, -1.0)
        fields = []
        for f in range(6):
            main = got[HALO * f : HALO * (f + 1), :]
            side = got[LAT_SIDE + HALO * (f // 4) : LAT_SIDE + HALO * (f // 4 + 1), :]
            side = roll(side, -HALO - 32 * (f % 4), 1)
            fields.append(jnp.concatenate([main, side], axis=1))
        if keep is not None:
            fields = [jnp.where(keep, field, 0.0) for field in fields]
        rate = 0.5 * barotropic_step
        place(at, HALO, *fields, rate if keep is None else jnp.where(keep, rate, 0.0))
        v_row = got[LAT_V : LAT_V + 1, :]
        if keep is not None:
            v_row = jnp.where(keep, v_row, 0.0)
        v_rows = pl.ds(pl.multiple_of(jnp.where(is_north, 8 + FULL, 0), 8), 8)
        v_pad[v_rows, :COLS] = jnp.broadcast_to(v_row, (8, COLS))
        v_pad[v_rows, COLS:] = jnp.zeros((8, COLS), jnp.float32)
        for n, ref in enumerate((mine, got)):
            w = ref[LAT_W : LAT_W + LAYERS, :]
            side = roll(ref[LAT_SIDE + HALO : LAT_SIDE + HALO + LAYERS, :], -HALO - 64, 1)
            if n == 1 and keep is not None:
                w, side = jnp.where(keep, w, 0.0), jnp.where(keep, side, 0.0)
            seam_w[n, :LAYERS, :COLS] = w
            seam_w[n, :LAYERS, COLS:] = side
        sum_o, sum_s, pot_o, pot_s, to_o, to_s = (jnp.zeros((1, WIDE), jnp.float32) for _ in range(6))
        for k in range(LAYERS):
            wo, ws = seam_w[0, k : k + 1, :], seam_w[1, k : k + 1, :]
            g = jnp.concatenate([g_rows[k : k + 1, :]] * 2, axis=1)
            sum_o, sum_s = sum_o + wo, sum_s + ws
            pot_o, pot_s = pot_o + g * sum_o, pot_s + g * sum_s
            to_o = to_o + wo * pot_s
            to_s = to_s + ws * pot_o
            pots[0, k : k + 1, :] = pot_o[:, :COLS]
            pots[1, k : k + 1, :] = pot_s[:, :COLS]
        safe_o = sum_o + jnp.where(sum_o > 0.0, 0.0, 1.0)
        safe_s = sum_s + jnp.where(sum_s > 0.0, 0.0, 1.0)
        scale = 0.5 * barotropic_step * sign
        row8 = row_index((8, WIDE))
        own_rows = pl.ds(pl.multiple_of(jnp.where(is_north, HALO + ROWS - 8, HALO), 8), 8)
        strip_rows = pl.ds(pl.multiple_of(jnp.where(is_north, HALO + ROWS, HALO - 8), 8), 8)
        last, first = row8 == jnp.where(is_north, 7, 0), row8 == jnp.where(is_north, 0, 7)
        fixed[4, own_rows, :] = fixed[4, own_rows, :] - jnp.where(last, scale * to_o / safe_o, 0.0)
        fixed[4, strip_rows, :] = fixed[4, strip_rows, :] + jnp.where(first, scale * to_s / safe_s, 0.0)
        side = jnp.where(is_north, 0, 3)
        w = seam_w[1, :LAYERS, :COLS]
        seam_rows[side, :LAYERS, :] = (-half * sign) * pots[1, :LAYERS, :]
        seam_rows[side + 1, :LAYERS, :] = w * (got[LAT_C : LAT_C + LAYERS, :] + (half * sign) * pots[0, :LAYERS, :])
        seam_rows[side + 2, :LAYERS, :] = w

    strip(got_x, own_x, 0, even, None)
    for copy in far_copies:
        copy.wait()

    far[...] = jnp.where(at_top & (g_rows[LAYERS + 2 : LAYERS + 3, :] > 0.0), own_f[...], far[...])
    strip(far, own_y, 1, jnp.logical_not(even), jnp.logical_not(at_bottom))

    def blocks(skip):
        edges_at = list(range(skip, FULL - skip, 8)) + [FULL - skip]
        return list(zip(edges_at[:-1], edges_at[1:]))

    for begin, end in blocks(0):
        v_pad[8 + begin : 8 + end, :] = fixed[0, begin:end, :] * state[1, begin:end, :]
    for step in range(SUBSTEPS):
        skip = (2 * step) // 8 * 8
        for begin, end in blocks(skip):
            trans_u = fixed[0, begin:end, :] * state[0, begin:end, :]
            dv = v_pad[9 + begin : 9 + end, :] - v_pad[7 + begin : 7 + end, :]
            du = pltpu.roll(trans_u, WIDE - 1, 1) - pltpu.roll(trans_u, 1, 1)
            held = level_pad[8 + begin : 8 + end, :]
            level_pad[8 + begin : 8 + end, :] = held - fixed[6, begin:end, :] * (du + dv)
        for begin, end in blocks(skip):
            u, v = state[0, begin:end, :], state[1, begin:end, :]
            level = level_pad[8 + begin : 8 + end, :]
            dy = level_pad[9 + begin : 9 + end, :] - level_pad[7 + begin : 7 + end, :]
            dx = pltpu.roll(level, WIDE - 1, 1) - pltpu.roll(level, 1, 1)
            keep, turn, slope = fixed[1, begin:end, :], fixed[2, begin:end, :], fixed[5, begin:end, :]
            next_u = keep * u + turn * v + fixed[3, begin:end, :] - slope * dx
            next_v = keep * v - turn * u + fixed[4, begin:end, :] - slope * dy
            state[0, begin:end, :] = next_u
            state[1, begin:end, :] = next_v
            state[2, begin:end, :] = next_u if step == 0 else state[2, begin:end, :] + next_u
            state[3, begin:end, :] = next_v if step == 0 else state[3, begin:end, :] + next_v
            v_pad[8 + begin : 8 + end, :] = fixed[0, begin:end, :] * next_v
    planes[0] = level_pad[8 + HALO : 8 + HALO + ROWS, :COLS]
    planes[1] = state[2, inner, :COLS] * (1.0 / SUBSTEPS)
    planes[2] = state[3, inner, :COLS] * (1.0 / SUBSTEPS)
    plane_copies = [
        pltpu.make_async_copy(planes.at[n], out, plane_sems.at[n])
        for n, out in enumerate((new_lev_hbm, mean_u_hbm, mean_v_hbm))
    ]
    for copy in plane_copies:
        copy.start()

    to_force = baroclinic_step / barotropic_step

    def rest(n, rows, lanes):
        return state[2 + n, rows, lanes] * (1.0 / SUBSTEPS) - to_force * fixed[3 + n, rows, lanes]

    main, beside = slice(0, COLS), slice(COLS, WIDE)
    lane = lane_index((ROWS, COLS))
    row = row_index((ROWS, COLS))
    is_e, is_w = lane == COLS - 1, lane == 0
    base_u = rest(0, inner, main) - flat[3]
    base_v = rest(1, inner, main) - flat[4]
    side_u = rest(0, inner, beside)
    rest_e = jnp.sum(jnp.where(is_w, side_u, 0.0), axis=1, keepdims=True)
    rest_w = jnp.sum(jnp.where(is_e, side_u, 0.0), axis=1, keepdims=True)
    pair_flux = edges[1] + edges[2] * jnp.where(lane % 2 == 0, rest_e, rest_w)
    pair_fix = edges[0]
    rest_n = rest(1, slice(HALO + ROWS, HALO + ROWS + 1), main)
    rest_s = rest(1, slice(HALO - 1, HALO), main)
    for side, line in ((0, rest_n), (3, rest_s)):
        seam_rows[side + 1, :LAYERS, :] = seam_rows[side + 1, :LAYERS, :] + seam_rows[side + 2, :LAYERS, :] * line
    levels = jnp.where(floor[0] > 0, floor[1], 0)
    copies = []
    parts = ((0, 4), (4, 8), (8, 11), (11, 12))
    lanes16 = lane_index((32, COLS))
    rows16 = row_index((32, COLS))
    is_e, is_w = lanes16 == COLS - 1, lanes16 == 0
    is_edge = is_e | is_w
    for k in range(LAYERS):
        shift = COLS - 1 - PAIR_LANE - 2 * k
        flux_v_pad[k, 7:8, :] = seam_rows[4, k : k + 1, :]
        flux_v_pad[k, 8 + ROWS : 9 + ROWS, :] = seam_rows[1, k : k + 1, :]
        for begin in range(0, ROWS, 32):
            at = slice(begin, begin + 32)
            w = weight[k, at, :]
            mask = levels[at] > k
            rest_u = tail_u[k, at, :] + base_u[at] + jnp.where(is_edge, roll(pair_fix[at], shift, 1), 0.0)
            rest_v = tail_v[k, at, :] + base_v[at]
            if begin == 0:
                rest_v = rest_v + jnp.where(rows16 == 0, seam_rows[3, k : k + 1, :], 0.0)
            if begin == ROWS - 32:
                rest_v = rest_v + jnp.where(rows16 == 32 - 1, seam_rows[0, k : k + 1, :], 0.0)
            out_u = jnp.where(mask, rest_u, 0.0)
            out_v = jnp.where(mask, rest_v, 0.0)
            new_u[k, at, :] = out_u
            new_v[k, at, :] = out_v
            flux_u = w * out_u
            flux_v_pad[k, 8 + begin : 8 + begin + 32, :] = w * out_v
            halo = roll(pair_flux[at], shift, 1)
            east = jnp.where(is_e, halo, pltpu.roll(flux_u, COLS - 1, 1))
            west = jnp.where(is_w, halo, pltpu.roll(flux_u, 1, 1))
            new_th[k, at, :] = th[k, at, :] - half * (east - west)
        north = flux_v_pad[k, 9 : 9 + ROWS, :]
        south = flux_v_pad[k, 7 : 7 + ROWS, :]
        new_th[k] = new_th[k] - half * (north - south)
        for part, (begin, end) in enumerate(parts):
            if k == end - 1:
                rows = pl.ds(begin, end - begin)
                for n, (held, out) in enumerate(((new_u, new_u_hbm), (new_v, new_v_hbm), (new_th, new_th_hbm))):
                    copy = pltpu.make_async_copy(held.at[rows], out.at[rows], sems.at[n, part])
                    copy.start()
                    copies.append(copy)
    for copy in copies + plane_copies:
        copy.wait()


def vmem(count):
    return [pl.BlockSpec(memory_space=pltpu.VMEM)] * count


def hbm(count):
    return [pl.BlockSpec(memory_space=pltpu.HBM)] * count


def in_hbm(*arrays):
    return tuple(pltpu.with_memory_space_constraint(x, pltpu.HBM) for x in arrays)


def f32(*shape):
    return jax.ShapeDtypeStruct(shape, jnp.float32)


PARAMS = pltpu.CompilerParams(vmem_limit_bytes=40 * 2**20)


def local(lu, lv, th, lev, u, v, land, bottom, fold_map, gravity):
    lons, lats = lax.axis_size("lon"), lax.axis_size("lat")
    lon_msg, lat_msg = f32(LON_ROWS, COLS), f32(LAT_ROWS, COLS)
    layers, plane = f32(LAYERS, ROWS, COLS), f32(ROWS, COLS)
    held = pltpu.VMEM((LAYERS, ROWS, COLS), jnp.float32)
    total = lons * COLS
    pivot = fold_map[0] + lax.axis_index("lon") * COLS
    shift = jnp.mod(pivot - COLS // 2, total) // COLS

    msg_a, msg_b, own_pairs, own_rows, flat, cor, g_rows, to_potential, tail_u, tail_v, weight, th, floor = pl.pallas_call(
        first_kernel,
        out_shape=(
            lon_msg, lon_msg, plane, f32(16, COLS), f32(8, ROWS, COLS), f32(FULL, COLS), f32(16, COLS), f32(COLS, COLS),
            layers, layers, layers, layers,
            jax.ShapeDtypeStruct((2, ROWS, COLS), jnp.int32),
        ),
        in_specs=hbm(10),
        out_specs=vmem(13),
        scratch_shapes=[
            held,
            held,
            pltpu.SMEM((LAYERS,), jnp.float32),
            pltpu.SMEM((COLS,), jnp.int32),
            pltpu.SemaphoreType.DMA((10,)),
        ],
        compiler_params=PARAMS,
        name="edges",
    )(*in_hbm(gravity, lu, lv, th, lev, u, v, land, bottom, fold_map))

    got_a = lax.ppermute(msg_a, "lon", [(i, i ^ 1) for i in range(lons)])
    got_b = lax.ppermute(msg_b, "lon", [(i, (((i + 1) ^ 1) - 1) % lons) for i in range(lons)])
    got_a, got_b, shift = lax.optimization_barrier((got_a, got_b, shift))

    ext, edges, msg_x, msg_y, msg_f = pl.pallas_call(
        second_kernel,
        out_shape=(f32(6, ROWS, WIDE), f32(3, ROWS, COLS), lat_msg, lat_msg, lat_msg),
        in_specs=vmem(8),
        out_specs=vmem(5),
        compiler_params=PARAMS,
        name="extend",
    )(g_rows, to_potential, flat, own_pairs, own_rows, msg_a, got_a, got_b)

    got_x = lax.ppermute(msg_x, "lat", [(i, i ^ 1) for i in range(lats)])
    top = lats - 1
    rows = [(b * lats + i, b * lats + ((i + 1) ^ 1) - 1) for b in range(lons) for i in range(1, top)]
    rows += [(b * lats, (b ^ 1) * lats) for b in range(lons)]

    def exchange(q):
        pairs = list(rows)
        for b in range(lons):
            source = (q - b) % lons
            source = (b + lons // 2) % lons if source == b else source
            pairs.append((source * lats + top, b * lats + top))
        return lambda x: lax.ppermute(x, ("lon", "lat"), pairs)

    got_f = lax.switch(shift, [exchange(q) for q in range(lons)], msg_f)

    padded = pltpu.VMEM((FULL + 16, WIDE), jnp.float32)
    rows16 = pltpu.VMEM((6, 16, COLS), jnp.float32)
    return pl.pallas_call(
        third_kernel,
        out_shape=(layers, layers, layers, plane, plane, plane),
        in_specs=vmem(14) + hbm(1),
        out_specs=hbm(6),
        scratch_shapes=[
            pltpu.VMEM((LAT_ROWS, COLS), jnp.float32),
            padded,
            padded,
            pltpu.VMEM((4, FULL, WIDE), jnp.float32),
            pltpu.VMEM((7, FULL, WIDE), jnp.float32),
            rows16,
            pltpu.VMEM((2, 16, WIDE), jnp.float32),
            rows16,
            held,
            held,
            held,
            pltpu.VMEM((LAYERS, ROWS + 16, COLS), jnp.float32),
            pltpu.VMEM((3, ROWS, COLS), jnp.float32),
            pltpu.SemaphoreType.DMA((3, 4)),
            pltpu.SemaphoreType.DMA((3,)),
            pltpu.SemaphoreType.DMA((FAR_PARTS,)),
        ],
        compiler_params=PARAMS,
        name="advance",
    )(g_rows, tail_u, tail_v, weight, th, floor, flat, cor, edges, ext, msg_x, msg_y, msg_f, got_x, *in_hbm(got_f))


def solution(mesh):
    layered, plane = P(None, "lat", "lon"), P("lat", "lon")
    return jax.shard_map(
        local,
        mesh=mesh,
        in_specs=(layered,) * 3 + (plane,) * 5 + (P("lon"), P()),
        out_specs=(layered,) * 3 + (plane,) * 3,
        check_vma=False,
    )
```
